128 devices in a mesh: row: 8 (over x, y_hi), col: 16 (over z, y_lo, core).
Axes of the slice: x: 4, y: 4 (y_hi: 2, y_lo: 2; y = y_hi * 2 + y_lo), z: 4, core: 2. Of those that a mesh axis runs over, the one named last changes fastest.
Arguments:
- currents: float32 [2, 64, 65536], P(None, None, ('row', 'col')), may hold values from -6 to 6
- projection: bfloat16 [64, 64, 65536], P(None, None, ('row', 'col')), may hold values from -0.75 to 0.75
- near_blocks: bfloat16 [4, 64, 64, 65536], P(None, None, None, ('row', 'col')), may hold values from -0.375 to 0.375
- partners: int32 [4, 65536], P(None, ('row', 'col')), may hold values from 0 to 8, as said below
- shifts: int32 [2, 65536], P(None, ('row', 'col')), may hold values from -2 to 2, as said below
- green: float32 [4096, 4096], P(('row', 'col')), may hold values from 0.5 to 2.5, as said below
Outputs:
- product: float32 [2, 64, 65536], P(None, None, ('row', 'col'))
The draws below stay inside these ranges and needn't reach their ends.
Inputs may be any that keep to these rules, and one draw needn't show every extreme that they name: shifts[0, n] is 0 or more for elements of the first element row and 0 or less for those of the last; shifts[1, n] likewise for the first and last element columns, so that every stencil lies inside the grid. partners[0, n] is 4, the element itself; for k of 1 or more the codes of one element are distinct, each 3 (dr + 1) + (dc + 1) for offsets dr, dc in -1, 0, 1, not both 0, of an element that lies inside the array. green is the spectrum of a real even kernel: green[ky, kx] = green[(4096 - ky) % 4096, kx] = green[ky, (4096 - kx) % 4096].
All inputs are finite; a program needn't handle non-finite values.
Results may differ from the reference program's by a relative error of at most 0.0038.
Values may be sent and summed in bfloat16 or wider, within the bound.
A program may use at most 192 MiB of HBM per device.

```python
import jax
import jax.numpy as jnp
from jax import lax

BASIS = 64
STEN = 8
PITCH = 8
HALO = 2
NEIGH = 4
RHS = 2
ER = 32
EC = 16
EX = 256
EY = 256
ELEMS = 65536
NGR = 2048
NGC = 2048
LR = 4096
LC = 4096


def element_place_drawn():
    number = jnp.arange(EX * EY, dtype=jnp.int32)
    block_index = number // (ER * EC)
    inside = number % (ER * EC)
    elem_row = block_index // (EY // EC) * ER + inside // EC
    elem_col = block_index % (EY // EC) * EC + inside % EC
    return (elem_row, elem_col)


def draw_shifts(key, part):
    elem_row, elem_col = element_place_drawn()
    row_key = jax.random.fold_in(key, 17)
    col_key = jax.random.fold_in(key, 29)
    row_shift = jax.random.randint(row_key, elem_row.shape, -HALO, HALO + 1, dtype=jnp.int32)
    col_shift = jax.random.randint(col_key, elem_col.shape, -HALO, HALO + 1, dtype=jnp.int32)
    first_mark = (elem_row == 1) & (elem_col == 1)
    second_mark = (elem_row == 2) & (elem_col == 2)
    row_shift = jnp.where(first_mark, -HALO, row_shift)
    row_shift = jnp.where(second_mark, HALO, row_shift)
    col_shift = jnp.where(first_mark, HALO, col_shift)
    col_shift = jnp.where(second_mark, -HALO, col_shift)
    row_shift = jnp.where(elem_row == 0, jnp.maximum(row_shift, 0), row_shift)
    row_shift = jnp.where(elem_row == EX - 1, jnp.minimum(row_shift, 0), row_shift)
    col_shift = jnp.where(elem_col == 0, jnp.maximum(col_shift, 0), col_shift)
    col_shift = jnp.where(elem_col == EY - 1, jnp.minimum(col_shift, 0), col_shift)
    return jnp.stack([row_shift, col_shift]).astype(jnp.int32)


def draw_partners(key, part):
    elem_row, elem_col = element_place_drawn()
    symbols = jnp.arange(9, dtype=jnp.int32)
    near_row = elem_row[None, :] + symbols[:, None] // 3 - 1
    near_col = elem_col[None, :] + symbols[:, None] % 3 - 1
    inside = (near_row >= 0) & (near_row < EX) & (near_col >= 0) & (near_col < EY) & (symbols[:, None] != 4)
    scores = jax.random.randint(jax.random.fold_in(key, 41), near_row.shape, 0, 1 << 20, dtype=jnp.int32) * 16 + symbols[:, None]
    scores = jnp.where(inside, scores, -1 - symbols[:, None])
    chosen = lax.top_k(jnp.transpose(scores), NEIGH - 1)[1]
    itself = jnp.full((1, EX * EY), 4, jnp.int32)
    return jnp.concatenate([itself, jnp.transpose(chosen).astype(jnp.int32)], axis=0)


def draw_green(key, part):
    quarter = jax.random.uniform(jax.random.fold_in(key, 53), (LC // 2 + 1, LR // 2 + 1), jnp.float32, 0.5, 2.5)
    col_freq = jnp.arange(LC, dtype=jnp.int32)
    row_freq = jnp.arange(LR, dtype=jnp.int32)
    col_fold = jnp.minimum(col_freq, LC - col_freq)
    row_fold = jnp.minimum(row_freq, LR - row_freq)
    return quarter[col_fold[:, None], row_fold[None, :]].astype(jnp.float32)


def block_levels(stream_key, dims, pieces, low, top_value):
    loudness, own = 1.0, jax.random.fold_in(stream_key, 6)
    for dim, blocks in pieces:
        draws = jnp.exp(jax.random.uniform(jax.random.fold_in(own, dim), (blocks,), jnp.float32, low / len(pieces), top_value / len(pieces)))
        loudness = loudness * jnp.repeat(draws, dims[dim] // blocks).reshape([-1 if axis == dim else 1 for axis in range(len(dims))])
    return loudness


def bell_draw(key, dims, deviation, bound, shards=(), kind=jnp.bfloat16):
    array = deviation * jax.random.normal(key, dims, jnp.float32)
    if shards:
        array = array * block_levels(key, dims, shards, -0.22, 0.18)
    return jnp.clip(array, -bound, bound).astype(kind)


def setup_inputs(seed: int = 0) -> dict:
    splits = jax.random.split(jax.random.key(seed), 7)
    currents = bell_draw(splits[0], (RHS, BASIS, ELEMS), 1.0, 6.0, ((2, 128),), jnp.float32)
    projection = bell_draw(splits[1], (STEN * STEN, BASIS, ELEMS), BASIS ** -0.5, 0.75, ((2, 128),))
    near_blocks = bell_draw(splits[2], (NEIGH, BASIS, BASIS, ELEMS), (BASIS * NEIGH) ** -0.5, 0.375, ((3, 128),))
    partners = draw_partners(jax.random.fold_in(splits[6], 71), 0)
    shifts = draw_shifts(jax.random.fold_in(splits[6], 71), 0)
    green = draw_green(jax.random.fold_in(splits[6], 71), 0)
    return dict(currents=currents, projection=projection, near_blocks=near_blocks, partners=partners, shifts=shifts, green=green)


def element_place():
    number = jnp.arange(EX * EY, dtype=jnp.int32)
    block_index = number // (ER * EC)
    inside = number % (ER * EC)
    elem_row = (block_index // (EY // EC)) * ER + inside // EC
    elem_col = (block_index % (EY // EC)) * EC + inside % EC
    return elem_row, elem_col


def element_number(elem_row, elem_col):
    block_index = (elem_row // ER) * (EY // EC) + elem_col // EC
    return (block_index * (ER * EC) + (elem_row % ER) * EC + elem_col % EC).astype(jnp.int32)


def reference(currents, projection, near_blocks, partners, shifts, green):
    highest = lax.Precision.HIGHEST
    elem_row, elem_col = element_place()
    cur_half = currents.astype(jnp.bfloat16)
    widened = cur_half.astype(jnp.float32)
    block_size = ER * EC
    starts = (jnp.arange(EX * EY // block_size, dtype=jnp.int32) * block_size).astype(jnp.int32)

    def stencil_block(start):
        weights = lax.dynamic_slice_in_dim(projection, start, block_size, 2).astype(jnp.float32)
        values = lax.dynamic_slice_in_dim(widened, start, block_size, 2)
        return jnp.einsum("sbn,qbn->qsn", weights, values, precision=highest)

    stencil = jnp.transpose(lax.map(stencil_block, starts), (1, 2, 0, 3)).reshape(RHS, STEN * STEN, EX * EY)
    offsets = jnp.arange(STEN * STEN, dtype=jnp.int32)
    cell_row = (PITCH * elem_row + shifts[0])[None, :] + (offsets // STEN)[:, None]
    cell_col = (PITCH * elem_col + shifts[1])[None, :] + (offsets % STEN)[:, None]
    charges = jnp.zeros((RHS, NGR, NGC), jnp.float32).at[:, cell_row, cell_col].add(stencil)
    padded = jnp.zeros((RHS, LR, LC), jnp.float32).at[:, :NGR, :NGC].set(charges)
    spectrum = jnp.fft.fft2(padded) * jnp.transpose(green)[None, :, :]
    potential = jnp.real(jnp.fft.ifft2(spectrum))[:, :NGR, :NGC]
    samples = potential[:, cell_row, cell_col]

    def far_block(start):
        weights = lax.dynamic_slice_in_dim(projection, start, block_size, 2).astype(jnp.float32)
        values = lax.dynamic_slice_in_dim(samples, start, block_size, 2)
        return jnp.einsum("sbn,qsn->qbn", weights, values, precision=highest)

    far_term = jnp.transpose(lax.map(far_block, starts), (1, 2, 0, 3)).reshape(RHS, BASIS, EX * EY)
    partner_row = elem_row[None, :] + partners // 3 - 1
    partner_col = elem_col[None, :] + partners % 3 - 1
    partner = element_number(partner_row, partner_col)
    picked = widened[:, :, partner]

    def near_block(start):
        blocks = lax.dynamic_slice_in_dim(near_blocks, start, block_size, 3).astype(jnp.float32)
        values = lax.dynamic_slice_in_dim(picked, start, block_size, 3)
        return jnp.einsum("kabn,qbkn->qan", blocks, values, precision=highest)

    near_term = jnp.transpose(lax.map(near_block, starts), (1, 2, 0, 3)).reshape(RHS, BASIS, EX * EY)
    return far_term + near_term
```

```python
import functools
import math

import jax
import jax.numpy as jnp
import ml_dtypes
import numpy as np
from jax import lax
from jax.experimental import pallas as pl
from jax.experimental.pallas import tpu as pltpu
from jax.sharding import PartitionSpec as P

MESH = pl.DeviceIdType.MESH
F32 = jnp.float32
BF16 = jnp.bfloat16
BASIS = 64
ER = 32
EC = 16
NEIGH = 4
RHS = 2
OFFSETS = (-2, -1, 1, 2)
EDGE_SLOT = {0: 8, 1: 9, 6: 10, 7: 11}


def halves(table):
    high = np.asarray(table, np.float64).astype(ml_dtypes.bfloat16)
    low = (table - high.astype(np.float64)).astype(ml_dtypes.bfloat16)
    return np.stack([high, low])


def make_tables():
    turn = lambda rows, cols, modulus: (
        2.0 * np.pi * ((np.arange(rows)[:, None] * np.arange(cols)[None, :]) % modulus) / modulus
    )
    place = np.zeros((12, 8, 16, 256))
    for ec in range(16):
        for j in range(8):
            place[j, :, ec, 8 * ec + j] = 1
        for j in (0, 1):
            if ec < 15:
                place[EDGE_SLOT[j], :, ec, 8 * (ec + 1) + j] = 1
            else:
                place[EDGE_SLOT[j], :, ec, 128 + j] = 1
                place[EDGE_SLOT[j], :, ec, 128 + 2 + j] = 1
        for j in (6, 7):
            if ec > 0:
                place[EDGE_SLOT[j], :, ec, 8 * (ec - 1) + j] = 1
            else:
                place[EDGE_SLOT[j], :, ec, 128 + 120 + j] = 1
                place[EDGE_SLOT[j], :, ec, 128 + 118 + j] = 1
    place = place.reshape(1536, 256)
    pick = np.stack([place.T, place.T])
    real_lanes = [128 + 0, 128 + 1, 128 + 126, 128 + 127]
    imag_lanes = [128 + 2, 128 + 3, 128 + 124, 128 + 125]
    pick[0, imag_lanes] = 0
    pick[1, real_lanes] = 0
    a = turn(128, 128, 128)
    row_fwd = np.block([[np.cos(a), np.sin(a)], [-np.sin(a), np.cos(a)]])
    row_inv = np.block([[np.cos(a), np.sin(a)], [-np.sin(a), np.cos(a)]])
    b = turn(256, 128, 256)
    col_fwd = np.block([[np.cos(b), np.sin(b)], [-np.sin(b), np.cos(b)]])
    col_inv = col_fwd.T
    c = turn(16, 16, 16)
    eye = np.eye(8)
    kc, ks = np.kron(eye, np.cos(c)), np.kron(eye, np.sin(c))
    small_fwd = np.block([[kc, -ks], [ks, kc]])
    small_inv = small_fwd.T
    t1 = turn(32, 128, 4096)
    twist_row = np.stack([np.cos(t1), np.sin(t1)])
    t2 = np.tile(turn(256, 16, 4096), (1, 8))
    twist_col = np.stack([np.cos(t2), np.sin(t2)])
    half = ml_dtypes.bfloat16
    return (
        place.astype(half),
        pick.astype(half),
        halves(row_fwd),
        halves(row_inv),
        halves(col_fwd),
        halves(col_inv),
        halves(small_fwd),
        halves(small_inv),
        twist_row.astype(np.float32),
        twist_col.astype(np.float32),
    )


def dot(a, b, dims=((1,), (0,))):
    return lax.dot_general(a, b, (dims, ((), ())), preferred_element_type=F32)


def split(x):
    high = x.astype(BF16)
    return high, (x - high.astype(F32)).astype(BF16)


def cadd(a, b):
    return (a[0] + b[0], a[1] + b[1])


def csub(a, b):
    return (a[0] - b[0], a[1] - b[1])


def cmulc(a, angle):
    turns = angle / (2 * math.pi)
    quarter = round(turns * 4)
    if abs(turns * 4 - quarter) < 1e-9:
        quarter %= 4
        if quarter == 0:
            return a
        if quarter == 1:
            return (-a[1], a[0])
        if quarter == 2:
            return (-a[0], -a[1])
        return (a[1], -a[0])
    c, s = math.cos(angle), math.sin(angle)
    return (a[0] * c - a[1] * s, a[0] * s + a[1] * c)


def fft(items, sign):
    n = len(items)
    if n == 1:
        return items
    even = fft(items[0::2], sign)
    odd = fft(items[1::2], sign)
    out = [None] * n
    for k in range(n // 2):
        t = cmulc(odd[k], sign * 2 * math.pi * k / n)
        out[k] = cadd(even[k], t)
        out[k + n // 2] = csub(even[k], t)
    return out


def iota(shape, dim):
    return lax.broadcasted_iota(jnp.int32, shape, dim)


def stencil_stage(proj, curf, shifts, rows_ref):
    sub = iota((8, 128), 0)
    for g in range(4):
        lanes = slice(g * 128, (g + 1) * 128)
        dr = jnp.broadcast_to(shifts[0:1, lanes], (8, 128))
        home = (sub - dr >= 0) & (sub - dr < 8)
        cur = [curf[q, :, lanes] for q in range(RHS)]

        def body(j, carry):
            tiles = [jnp.zeros((8, 128), F32) for _ in range(RHS)]
            for i in range(8):
                weight = proj[i * 8 + j, :, lanes].astype(F32)
                for q in range(RHS):
                    line = jnp.sum(weight * cur[q], axis=0, keepdims=True)
                    tiles[q] = jnp.where(sub == i, jnp.broadcast_to(line, (8, 128)), tiles[q])
            for q in range(RHS):
                moved = tiles[q]
                for o in OFFSETS:
                    moved = jnp.where(dr == o, pltpu.roll(tiles[q], o % 8, 0), moved)
                rows_ref[q, 0, j, :, lanes] = jnp.where(home, moved, 0.0)
                rows_ref[q, 1, j, :, lanes] = jnp.where(home, 0.0, moved)
            return carry

        lax.fori_loop(0, 8, body, 0)


def spread_stage(rows_ref, shifts, place, left_ref, grid_ref, send_ref):
    sub = iota((64, 128), 0)
    lane = iota((64, 128), 1)
    own = (sub // 8) == (lane // 16)
    for g in range(4):
        lanes = slice(g * 128, (g + 1) * 128)
        dc = jnp.broadcast_to(shifts[1:2, lanes], (8, 128))
        is_offset = {o: dc == o for o in OFFSETS}

        def body(idx, carry):
            q, kind = idx // 2, lax.rem(idx, 2)
            tiles = [rows_ref[q, kind, j, :, lanes] for j in range(8)]
            for j in range(8):
                moved = tiles[j]
                for o in OFFSETS:
                    moved = jnp.where(is_offset[o], tiles[(j - o) % 8], moved)
                home = (j - dc >= 0) & (j - dc < 8)
                pieces = [(j, jnp.where(home, moved, 0.0))]
                if j in EDGE_SLOT:
                    pieces.append((EDGE_SLOT[j], jnp.where(home, 0.0, moved)))
                for slot, piece in pieces:
                    wide = jnp.where(own, jnp.concatenate([piece] * 8, axis=0), 0.0)
                    left_ref[pl.ds(pl.multiple_of(idx * 64, 64), 64), slot * 128 : (slot + 1) * 128] = (
                        wide.astype(BF16)
                    )
            return carry

        lax.fori_loop(0, 4, body, 0)
        product = dot(left_ref[...], place[...])
        for q in range(RHS):
            for kind in range(2):
                base = (q * 2 + kind) * 64
                grid_ref[q, kind, 8 + g * 64 : 8 + (g + 1) * 64, :] = product[base : base + 64]
    zero8 = jnp.zeros((8, 256), F32)
    for q in range(RHS):
        grid_ref[q, 1, 0:8, :] = zero8
        grid_ref[q, 1, 264:272, :] = zero8
    sub = lax.rem(iota((16, 256), 0), 8)
    lane1 = iota((16, 128), 1)
    real_rim = (lane1 < 2) | (lane1 >= 126)
    imag_rim = ((lane1 >= 2) & (lane1 < 4)) | ((lane1 >= 124) & (lane1 < 126))

    def message(parts):
        rim = jnp.where(real_rim, parts[0][:, 128:], jnp.where(imag_rim, parts[1][:, 128:], 0.0))
        return jnp.concatenate([parts[0][:, :128], parts[1][:, :128], rim], axis=0).astype(BF16)

    def slab(k, carry):
        parts = []
        for q in range(RHS):
            at = lambda shift: pl.ds(pl.multiple_of(k * 16 + shift, 8), 16)
            total = grid_ref[q, 0, at(8), :]
            total = total + jnp.where(sub >= 6, grid_ref[q, 1, at(16), :], 0.0)
            total = total + jnp.where(sub < 2, grid_ref[q, 1, at(0), :], 0.0)
            parts.append(total)
        send_ref[k] = message(parts)
        return carry

    lax.fori_loop(0, 16, slab, 0)
    full = iota((16, 256), 0)
    send_ref[16] = message(
        [jnp.where(full >= 14, grid_ref[q, 1, 0:16, :], 0.0) for q in range(RHS)]
    )
    send_ref[17] = message(
        [jnp.where(full < 2, grid_ref[q, 1, 256:272, :], 0.0) for q in range(RHS)]
    )


def row_forward_stage(recv, halo, has_halo, slab_ref, twist, table, mix_ref, flat_ref, out_ref):
    def widen(c, carry):
        slab_ref[c] = recv[c].astype(F32)
        return carry

    lax.fori_loop(0, 16, widen, 0)

    @pl.when(has_halo)
    def _():
        def add(c, carry):
            slab_ref[c] = slab_ref[c] + halo[c].astype(F32)
            return carry

        lax.fori_loop(0, 16, add, 0)

    lane = iota((8, 128), 1)

    def rows(h, carry):
        at = lambda start: pl.ds(pl.multiple_of(start + h * 8, 8), 8)
        rims = [slab_ref[c, at(32), :] for c in range(16)]
        items = []
        for c in range(16):
            real = slab_ref[c, at(0), :]
            imag = slab_ref[c, at(16), :]
            if c > 0:
                real = real + jnp.where(lane < 2, rims[c - 1], 0.0)
                imag = imag + jnp.where(lane < 2, pltpu.roll(rims[c - 1], 126, 1), 0.0)
            if c < 15:
                real = real + jnp.where(lane >= 126, rims[c + 1], 0.0)
                imag = imag + jnp.where(lane >= 126, pltpu.roll(rims[c + 1], 2, 1), 0.0)
            items.append((real, imag))
        even = fft(items, -1)
        odd = fft([cmulc(v, -2 * math.pi * c / 32) for c, v in enumerate(items)], -1)
        for m in range(16):
            for p, (real, imag) in enumerate((even[m], odd[m])):
                k0 = 2 * m + p
                cos, sin = twist[0, k0 : k0 + 1, :], twist[1, k0 : k0 + 1, :]
                mix_ref[at(k0 * 16), 0:128] = real * cos + imag * sin
                mix_ref[at(k0 * 16), 128:256] = imag * cos - real * sin
        return carry

    lax.fori_loop(0, 2, rows, 0)
    high, low = split(mix_ref[...])
    nt = ((1,), (1,))
    out = dot(table[0], high, nt) + dot(table[1], high, nt) + dot(table[0], low, nt)
    to_messages(out, flat_ref, out_ref)


def to_messages(out, flat_ref, out_ref):
    for ri in range(2):
        for g in range(4):
            flat_ref[pl.ds(ri * 4 + g, 128, stride=8), :] = out[
                ri * 128 : (ri + 1) * 128, g * 128 : (g + 1) * 128
            ]
    out_ref[...] = flat_ref[...].reshape(128, 8, 128).astype(BF16)


def from_messages(recv, flat_ref, half_ref):
    flat_ref[...] = recv[...].astype(F32).reshape(1024, 128)
    for ri in range(2):
        for g in range(4):
            half_ref[ri * 128 : (ri + 1) * 128, g * 128 : (g + 1) * 128] = flat_ref[
                pl.ds(ri * 4 + g, 128, stride=8), :
            ].astype(BF16)


def column_stage(recv, flat_ref, half_ref, fwd, inv, small, small_inv, twist, green, wide_ref, out_ref):
    from_messages(recv, flat_ref, half_ref)
    block = half_ref[...]
    wide_ref[...] = dot(fwd[0], block) + dot(fwd[1], block)
    cos, sin = twist[0], twist[1]
    for g in range(4):
        lanes = slice(g * 128, (g + 1) * 128)
        real, imag = wide_ref[0:256, lanes], wide_ref[256:512, lanes]
        turned = jnp.concatenate([real * cos + imag * sin, imag * cos - real * sin], axis=1)
        high, low = split(turned)
        spec = dot(high, small[0]) + dot(low, small[0]) + dot(high, small[1])
        scale = green[:, lanes]
        spec = spec * jnp.concatenate([scale, scale], axis=1)
        high, low = split(spec)
        back = dot(high, small_inv[0]) + dot(low, small_inv[0]) + dot(high, small_inv[1])
        real, imag = back[:, 0:128], back[:, 128:256]
        wide_ref[0:256, lanes] = real * cos - imag * sin
        wide_ref[256:512, lanes] = imag * cos + real * sin
    high, low = split(wide_ref[...])
    out = dot(inv[0], high) + dot(inv[0], low) + dot(inv[1], high)
    to_messages(out, flat_ref, out_ref)


def row_inverse_stage(recv, flat_ref, half_ref, table, twist, mix_ref, slab_ref, send_ref):
    from_messages(recv, flat_ref, half_ref)
    turned = half_ref[...].T
    mix_ref[...] = dot(turned, table[0]) + dot(turned, table[1])

    def rows(h, carry):
        at = lambda start: pl.ds(pl.multiple_of(start + h * 8, 8), 8)
        items = []
        for k0 in range(32):
            cos, sin = twist[0, k0 : k0 + 1, :], twist[1, k0 : k0 + 1, :]
            real, imag = mix_ref[at(k0 * 16), 0:128], mix_ref[at(k0 * 16), 128:256]
            items.append((real * cos - imag * sin, imag * cos + real * sin))
        even = fft(items[0::2], 1)
        odd = fft(items[1::2], 1)
        for c in range(16):
            real, imag = cadd(even[c], cmulc(odd[c], 2 * math.pi * c / 32))
            slab_ref[c, at(0), :] = real
            slab_ref[c, at(16), :] = imag
        return carry

    lax.fori_loop(0, 2, rows, 0)
    lane = iota((16, 128), 1)
    for c in range(16):
        rim = jnp.zeros((16, 128), F32)
        if c < 15:
            rim = jnp.where(lane < 2, slab_ref[c + 1, 0:16, :], rim)
            rim = jnp.where((lane >= 2) & (lane < 4), pltpu.roll(slab_ref[c + 1, 16:32, :], 2, 1), rim)
        if c > 0:
            rim = jnp.where(lane >= 126, slab_ref[c - 1, 0:16, :], rim)
            rim = jnp.where(
                (lane >= 124) & (lane < 126), pltpu.roll(slab_ref[c - 1, 16:32, :], 126, 1), rim
            )
        send_ref[c] = jnp.concatenate([slab_ref[c, 0:32, :], rim], axis=0).astype(BF16)


def sample_stage(recv, pick, shifts, tall_ref, rows_ref, sample_ref):
    sub = iota((8, 128), 0)
    lane = iota((8, 128), 1)
    owns = [(lane // 16) == e for e in range(8)]
    for q in range(RHS):
        main = recv[:, q * 16 : (q + 1) * 16, :].reshape(288, 128)
        rim = recv[:, 32:48, :].reshape(288, 128)
        tall_ref[...] = dot(jnp.concatenate([main, rim], axis=1), pick[q])
        for g in range(4):
            lanes = slice(g * 128, (g + 1) * 128)
            dr = jnp.broadcast_to(shifts[0:1, lanes], (8, 128))
            dc = jnp.broadcast_to(shifts[1:2, lanes], (8, 128))

            def body(slot, carry):
                column = pl.ds(pl.multiple_of(slot * 128, 128), 128)
                tiles = [
                    tall_ref[8 + 64 * g + 8 * t : 16 + 64 * g + 8 * t, column] for t in range(10)
                ]
                home = tiles[1]
                edge = jnp.where(sub < 4, tiles[2], tiles[0])
                for e in range(1, 8):
                    home = jnp.where(owns[e], tiles[e + 1], home)
                    edge = jnp.where(owns[e], jnp.where(sub < 4, tiles[e + 2], tiles[e]), edge)
                moved = home
                for o in OFFSETS:
                    kept = (sub >= o) if o > 0 else (sub < 8 + o)
                    shifted = pltpu.roll(jnp.where(kept, home, edge), (-o) % 8, 0)
                    moved = jnp.where(dr == o, shifted, moved)
                rows_ref[slot] = moved
                return carry

            lax.fori_loop(0, 12, body, 0)
            line = lambda j: rows_ref[j] if 0 <= j < 8 else rows_ref[EDGE_SLOT[j % 8]]
            for j in range(8):
                moved = line(j)
                for o in OFFSETS:
                    moved = jnp.where(dc == o, line(j + o), moved)
                sample_ref[q, j, :, lanes] = moved


def far_stage(proj, sample_ref, near_ref, out_ref):
    for g in range(4):
        lanes = slice(g * 128, (g + 1) * 128)

        def body(j, sums):
            sums = list(sums)
            for i in range(8):
                weight = proj[i * 8 + j, :, lanes].astype(F32)
                for q in range(RHS):
                    line = sample_ref[q, j, i : i + 1, lanes]
                    sums[q] = sums[q] + weight * line
            return tuple(sums)

        sums = lax.fori_loop(0, 8, body, tuple(near_ref[q, :, lanes] for q in range(RHS)))
        for q in range(RHS):
            out_ref[q, :, lanes] = sums[q]


def turn_green(green, rows_ref, out_ref):
    for j1 in range(16):
        for h in range(2):
            rows_ref[h, pl.ds(j1, 32, stride=16), :] = green[
                :, j1 * 256 + h * 128 : j1 * 256 + (h + 1) * 128
            ]
    for h in range(2):
        for g in range(4):
            out_ref[h * 128 : (h + 1) * 128, g * 128 : (g + 1) * 128] = rows_ref[
                h, g * 128 : (g + 1) * 128, :
            ].T * (1.0 / 16777216)


def slots_wait(ref, count, sem):
    part = ref.at[pl.ds(0, count)]
    pltpu.make_async_copy(part, part, sem).wait()


def main_kernel(
    cur, proj, shifts, green, near,
    place, pick, row_fwd, row_inv, col_fwd, col_inv, small, small_inv, twist_row, twist_col,
    out_ref,
    rows_ref, left_ref, grid_ref, send1, recv1, halo1, slab_ref, mix_ref, flat_ref, send2, recv2,
    half_ref, wide_ref, green_rows, green_turned, send3, recv3, send4, recv4, tall_ref, pick_rows,
    sample_ref, curf,
    ssem, rsem, hsem, lsem,
):
    r, c = lax.axis_index("row"), lax.axis_index("col")
    me = r * 16 + c
    barrier = pltpu.get_barrier_semaphore()

    def peer(k):
        d = lax.rem(me + k, 128)
        return d, (d // 16, lax.rem(d, 16))

    def greet(k, carry):
        pl.semaphore_signal(barrier, inc=1, device_id=peer(k)[1], device_id_type=MESH)
        return carry

    zero = jnp.zeros((48, 128), BF16)
    recv4[0] = zero
    recv4[17] = zero
    lax.fori_loop(1, 128, greet, 0)
    curf[...] = cur[...].astype(BF16).astype(F32)
    stencil_stage(proj, curf, shifts, rows_ref)
    spread_stage(rows_ref, shifts, place, left_ref, grid_ref, send1)
    pl.semaphore_wait(barrier, 127)

    def to_column(send, recv, slot, index):
        def go(k, carry):
            d = lax.rem(c + k, 16)
            pltpu.make_async_remote_copy(
                send.at[d], recv.at[slot], ssem.at[index], rsem.at[index], device_id=(r, d), device_id_type=MESH
            ).start()
            return carry

        lax.fori_loop(1, 16, go, 0)

    to_column(send1, recv1, c, 0)

    @pl.when(r > 0)
    def _():
        pltpu.make_async_remote_copy(
            send1.at[16], halo1.at[c], ssem.at[4], hsem.at[0], device_id=(r - 1, 15), device_id_type=MESH
        ).start()

    @pl.when(r < 7)
    def _():
        pltpu.make_async_remote_copy(
            send1.at[17], halo1.at[c], ssem.at[5], hsem.at[0], device_id=(r + 1, 0), device_id_type=MESH
        ).start()

    own = pltpu.make_async_copy(send1.at[c], recv1.at[c], lsem.at[0])
    own.start()
    turn_green(green, green_rows, green_turned)
    own.wait()
    has_halo = ((c == 0) & (r > 0)) | ((c == 15) & (r < 7))
    slots_wait(recv1, 15, rsem.at[0])

    @pl.when(has_halo)
    def _():
        slots_wait(halo1, 16, hsem.at[0])

    row_forward_stage(recv1, halo1, has_halo, slab_ref, twist_row, row_fwd, mix_ref, flat_ref, send2)

    def to_all(send, recv, index):
        def go(k, carry):
            d, where = peer(k)
            pltpu.make_async_remote_copy(
                send.at[d], recv.at[me], ssem.at[index], rsem.at[index], device_id=where, device_id_type=MESH
            ).start()
            return carry

        own = pltpu.make_async_copy(send.at[me], recv.at[me], lsem.at[index])
        own.start()
        lax.fori_loop(1, 128, go, 0)
        own.wait()
        slots_wait(recv, 127, rsem.at[index])

    to_all(send2, recv2, 1)
    column_stage(
        recv2, flat_ref, half_ref, col_fwd, col_inv, small, small_inv, twist_col, green_turned, wide_ref, send3
    )
    to_all(send3, recv3, 2)
    row_inverse_stage(recv3, flat_ref, half_ref, row_inv, twist_row, mix_ref, slab_ref, send4)
    to_column(send4, recv4, c + 1, 3)

    def to_neighbour_row(target, slot, index, sem):
        def go(d, carry):
            pltpu.make_async_remote_copy(
                send4.at[d], recv4.at[slot], ssem.at[index], hsem.at[sem], device_id=(target, d), device_id_type=MESH
            ).start()
            return carry

        lax.fori_loop(0, 16, go, 0)

    up = (c == 0) & (r > 0)
    down = (c == 15) & (r < 7)

    @pl.when(up)
    def _():
        to_neighbour_row(r - 1, 17, 6, 1)

    @pl.when(down)
    def _():
        to_neighbour_row(r + 1, 0, 7, 2)

    own = pltpu.make_async_copy(send4.at[c], recv4.at[c + 1], lsem.at[3])
    own.start()
    own.wait()
    slots_wait(recv4, 15, rsem.at[3])

    @pl.when(r < 7)
    def _():
        slots_wait(recv4, 1, hsem.at[1])

    @pl.when(r > 0)
    def _():
        slots_wait(recv4, 1, hsem.at[2])

    sample_stage(recv4, pick, shifts, tall_ref, pick_rows, sample_ref)
    far_stage(proj, sample_ref, near, out_ref)

    slots_wait(send1, 15, ssem.at[0])

    @pl.when(r > 0)
    def _():
        slots_wait(send1, 1, ssem.at[4])

    @pl.when(r < 7)
    def _():
        slots_wait(send1, 1, ssem.at[5])

    slots_wait(send2, 127, ssem.at[1])
    slots_wait(send3, 127, ssem.at[2])
    slots_wait(send4, 15, ssem.at[3])

    @pl.when(up)
    def _():
        slots_wait(send4, 16, ssem.at[6])

    @pl.when(down)
    def _():
        slots_wait(send4, 16, ssem.at[7])


def main_call(cur, proj, shifts, green, near):
    tables = [jnp.asarray(t) for t in make_tables()]
    vmem = pl.BlockSpec(memory_space=pltpu.VMEM)
    dma = pltpu.SemaphoreType.DMA
    return pl.pallas_call(
        main_kernel,
        out_shape=jax.ShapeDtypeStruct((RHS, BASIS, ER * EC), F32),
        in_specs=[vmem] * (5 + len(tables)),
        out_specs=vmem,
        scratch_shapes=[
            pltpu.VMEM((RHS, 2, 8, 8, 512), F32),
            pltpu.VMEM((256, 1536), BF16),
            pltpu.VMEM((RHS, 2, 272, 256), F32),
            pltpu.VMEM((18, 48, 128), BF16),
            pltpu.VMEM((16, 48, 128), BF16),
            pltpu.VMEM((16, 48, 128), BF16),
            pltpu.VMEM((16, 48, 128), F32),
            pltpu.VMEM((512, 256), F32),
            pltpu.VMEM((1024, 128), F32),
            pltpu.VMEM((128, 8, 128), BF16),
            pltpu.VMEM((128, 8, 128), BF16),
            pltpu.VMEM((256, 512), BF16),
            pltpu.VMEM((512, 512), F32),
            pltpu.VMEM((2, 512, 128), F32),
            pltpu.VMEM((256, 512), F32),
            pltpu.VMEM((128, 8, 128), BF16),
            pltpu.VMEM((128, 8, 128), BF16),
            pltpu.VMEM((16, 48, 128), BF16),
            pltpu.VMEM((18, 48, 128), BF16),
            pltpu.VMEM((288, 1536), F32),
            pltpu.VMEM((12, 8, 128), F32),
            pltpu.VMEM((RHS, 8, 8, 512), F32),
            pltpu.VMEM((RHS, BASIS, 512), F32),
            dma((8,)),
            dma((4,)),
            dma((3,)),
            dma((4,)),
        ],
        compiler_params=pltpu.CompilerParams(
            collective_id=0, has_side_effects=True, vmem_limit_bytes=48 * 2**20
        ),
    )(cur, proj, shifts, green, near, *tables)


def near_kernel(blocks, picked, out_ref):
    for g in range(4):
        lanes = slice(g * 128, (g + 1) * 128)

        def body(step, sums):
            k, b = step // 4, lax.rem(step, 4)
            at = pl.ds(pl.multiple_of(b * 16, 16), 16)
            values = [picked[k, q, at, lanes].astype(F32) for q in range(RHS)]
            sums = list(sums)
            for a in range(8):
                weight = blocks[k, a, at, lanes].astype(F32)
                for q in range(RHS):
                    product = weight * values[q]
                    sums[a * 2 + q] = sums[a * 2 + q] + (product[0:8] + product[8:16])
            return tuple(sums)

        sums = lax.fori_loop(0, 16, body, tuple(jnp.zeros((8, 128), F32) for _ in range(16)))
        sub = iota((8, 128), 0)
        for q in range(RHS):
            tile = jnp.zeros((8, 128), F32)
            for a in range(8):
                line = jnp.sum(sums[a * 2 + q], axis=0, keepdims=True)
                tile = jnp.where(sub == a, jnp.broadcast_to(line, (8, 128)), tile)
            out_ref[q, :, lanes] = tile


def near_call(blocks, picked):
    return pl.pallas_call(
        near_kernel,
        grid=(8,),
        out_shape=jax.ShapeDtypeStruct((RHS, BASIS, ER * EC), F32),
        in_specs=[
            pl.BlockSpec((NEIGH, 8, BASIS, ER * EC), lambda a: (0, a, 0, 0)),
            pl.BlockSpec((NEIGH, RHS, BASIS, ER * EC), lambda a: (0, 0, 0, 0)),
        ],
        out_specs=pl.BlockSpec((RHS, 8, ER * EC), lambda a: (0, a, 0)),
        compiler_params=pltpu.CompilerParams(vmem_limit_bytes=24 * 2**20),
    )(blocks, picked)


def extended_2(block, sides, width):
    for axis, dim in sides:
        count = lax.axis_size(axis)
        forward = [(i, i + 1) for i in range(count - 1)]
        backward = [(target, source) for source, target in forward]
        low = lax.ppermute(
            lax.slice_in_dim(block, block.shape[dim] - width, None, axis=dim), axis, forward
        )
        high = lax.ppermute(lax.slice_in_dim(block, 0, width, axis=dim), axis, backward)
        block = jnp.concatenate([low, block, high], axis=dim)
    return block


def shards(currents, projection, near_blocks, partners, shifts, green):
    elements = ER * EC
    cur_half = currents.astype(BF16)
    spread = extended_2(cur_half.reshape(RHS, BASIS, ER, EC), (("row", 2), ("col", 3)), 1)
    views = []
    for symbol in range(9):
        row_start, col_start = symbol // 3, symbol % 3
        views.append(
            spread[:, :, row_start : row_start + ER, col_start : col_start + EC].reshape(
                RHS, BASIS, elements
            )
        )
    picked = []
    for slot in range(NEIGH):
        chosen = jnp.zeros((RHS, BASIS, elements), BF16)
        for symbol in range(9):
            chosen = jnp.where(partners[slot] == symbol, views[symbol], chosen)
        picked.append(chosen)
    near = near_call(near_blocks, jnp.stack(picked))
    return main_call(currents, projection, shifts, green, near)


def solution(mesh):
    in_specs = (
        P(None, None, ("row", "col")),
        P(None, None, ("row", "col")),
        P(None, None, None, ("row", "col")),
        P(None, ("row", "col")),
        P(None, ("row", "col")),
        P(("row", "col"), None),
    )
    out_specs = P(None, None, ("row", "col"))
    return jax.shard_map(shards, mesh=mesh, in_specs=in_specs, out_specs=out_specs, check_vma=False)
```

```python
import functools
import math

import jax
import jax.numpy as jnp
import ml_dtypes
import numpy as np
from jax import lax
from jax.experimental import pallas as pl
from jax.experimental.pallas import tpu as pltpu
from jax.sharding import PartitionSpec as P

MESH = pl.DeviceIdType.MESH
F32 = jnp.float32
BF16 = jnp.bfloat16
BASIS = 64
ER = 32
EC = 16
NEIGH = 4
RHS = 2
OFFSETS = (-2, -1, 1, 2)
EDGE_SLOT = {0: 8, 1: 9, 6: 10, 7: 11}


def halves(table):
    high = np.asarray(table, np.float64).astype(ml_dtypes.bfloat16)
    low = (table - high.astype(np.float64)).astype(ml_dtypes.bfloat16)
    return np.stack([high, low])


def make_tables():
    turn = lambda rows, cols, modulus: (
        2.0 * np.pi * ((np.arange(rows)[:, None] * np.arange(cols)[None, :]) % modulus) / modulus
    )
    place = np.zeros((12, 8, 16, 256))
    for ec in range(16):
        for j in range(8):
            place[j, :, ec, 8 * ec + j] = 1
        for j in (0, 1):
            if ec < 15:
                place[EDGE_SLOT[j], :, ec, 8 * (ec + 1) + j] = 1
            else:
                place[EDGE_SLOT[j], :, ec, 128 + j] = 1
                place[EDGE_SLOT[j], :, ec, 128 + 2 + j] = 1
        for j in (6, 7):
            if ec > 0:
                place[EDGE_SLOT[j], :, ec, 8 * (ec - 1) + j] = 1
            else:
                place[EDGE_SLOT[j], :, ec, 128 + 120 + j] = 1
                place[EDGE_SLOT[j], :, ec, 128 + 118 + j] = 1
    place = place.reshape(1536, 256)
    pick = np.stack([place.T, place.T])
    real_lanes = [128 + 0, 128 + 1, 128 + 126, 128 + 127]
    imag_lanes = [128 + 2, 128 + 3, 128 + 124, 128 + 125]
    pick[0, imag_lanes] = 0
    pick[1, real_lanes] = 0
    a = turn(128, 128, 128)
    row_fwd = np.block([[np.cos(a), np.sin(a)], [-np.sin(a), np.cos(a)]])
    row_inv = np.block([[np.cos(a), np.sin(a)], [-np.sin(a), np.cos(a)]])
    b = turn(256, 128, 256)
    col_fwd = np.block([[np.cos(b), np.sin(b)], [-np.sin(b), np.cos(b)]])
    col_inv = col_fwd.T
    c = turn(16, 16, 16)
    eye = np.eye(8)
    kc, ks = np.kron(eye, np.cos(c)), np.kron(eye, np.sin(c))
    small_fwd = np.block([[kc, -ks], [ks, kc]])
    small_inv = small_fwd.T
    t1 = turn(32, 128, 4096)
    twist_row = np.stack([np.cos(t1), np.sin(t1)])
    t2 = np.tile(turn(256, 16, 4096), (1, 8))
    twist_col = np.stack([np.cos(t2), np.sin(t2)])
    half = ml_dtypes.bfloat16
    return (
        place.astype(half),
        pick.astype(half),
        halves(row_fwd),
        halves(row_inv),
        halves(col_fwd),
        halves(col_inv),
        halves(small_fwd),
        halves(small_inv),
        twist_row.astype(np.float32),
        twist_col.astype(np.float32),
    )


def dot(a, b, dims=((1,), (0,))):
    return lax.dot_general(a, b, (dims, ((), ())), preferred_element_type=F32)


def split(x):
    high = x.astype(BF16)
    return high, (x - high.astype(F32)).astype(BF16)


def cadd(a, b):
    return (a[0] + b[0], a[1] + b[1])


def csub(a, b):
    return (a[0] - b[0], a[1] - b[1])


def cmulc(a, angle):
    turns = angle / (2 * math.pi)
    quarter = round(turns * 4)
    if abs(turns * 4 - quarter) < 1e-9:
        quarter %= 4
        if quarter == 0:
            return a
        if quarter == 1:
            return (-a[1], a[0])
        if quarter == 2:
            return (-a[0], -a[1])
        return (a[1], -a[0])
    c, s = math.cos(angle), math.sin(angle)
    return (a[0] * c - a[1] * s, a[0] * s + a[1] * c)


def fft(items, sign):
    n = len(items)
    if n == 1:
        return items
    even = fft(items[0::2], sign)
    odd = fft(items[1::2], sign)
    out = [None] * n
    for k in range(n // 2):
        t = cmulc(odd[k], sign * 2 * math.pi * k / n)
        out[k] = cadd(even[k], t)
        out[k + n // 2] = csub(even[k], t)
    return out


def iota(shape, dim):
    return lax.broadcasted_iota(jnp.int32, shape, dim)


def row_sums(tiles):
    sub = iota((8, 128), 0)
    top = sub < 4
    tiles = [
        jnp.where(top, tiles[i], tiles[i + 4])
        + pltpu.roll(jnp.where(top, tiles[i + 4], tiles[i]), 4, 0)
        for i in range(4)
    ]
    for step in (2, 1):
        upper = lax.rem(sub, 2 * step) < step
        tiles = [
            jnp.where(
                upper,
                tiles[i] + pltpu.roll(tiles[i], 8 - step, 0),
                tiles[i + step] + pltpu.roll(tiles[i + step], step, 0),
            )
            for i in range(step)
        ]
    return tiles[0]


def fold(x):
    total = x[0:8]
    for b in range(1, x.shape[0] // 8):
        total = total + x[8 * b : 8 * b + 8]
    return total


def stencil_stage(proj, curf, shifts, rows_ref, ready):
    sub = iota((8, 128), 0)
    for g in range(4):
        lanes = slice(g * 128, (g + 1) * 128)
        dr = jnp.broadcast_to(shifts[0:1, lanes], (8, 128))
        home = (sub - dr >= 0) & (sub - dr < 8)
        cur = [curf[q, :, lanes] for q in range(RHS)]

        ready(g)

        def body(j, carry):
            parts = [[] for _ in range(RHS)]
            for i in range(8):
                weight = proj[i * 8 + j, :, lanes].astype(F32)
                for q in range(RHS):
                    parts[q].append(fold(weight * cur[q]))
            tiles = [row_sums(part) for part in parts]
            for q in range(RHS):
                moved = tiles[q]
                for o in OFFSETS:
                    moved = jnp.where(dr == o, pltpu.roll(tiles[q], o % 8, 0), moved)
                rows_ref[q, 0, j, :, lanes] = jnp.where(home, moved, 0.0)
                rows_ref[q, 1, j, :, lanes] = jnp.where(home, 0.0, moved)
            return carry

        lax.fori_loop(0, 8, body, 0)


def spread_stage(rows_ref, shifts, place, left_ref, grid_ref, send_ref):
    sub = iota((64, 128), 0)
    lane = iota((64, 128), 1)
    own = jnp.where((sub // 8) == (lane // 16), 1.0, 0.0).astype(BF16)
    for g in range(4):
        lanes = slice(g * 128, (g + 1) * 128)
        dc = jnp.broadcast_to(shifts[1:2, lanes], (8, 128))
        is_offset = {o: dc == o for o in OFFSETS}

        def body(idx, carry):
            q, kind = idx // 2, lax.rem(idx, 2)
            tiles = [rows_ref[q, kind, j, :, lanes] for j in range(8)]
            for j in range(8):
                moved = tiles[j]
                for o in OFFSETS:
                    moved = jnp.where(is_offset[o], tiles[(j - o) % 8], moved)
                home = (j - dc >= 0) & (j - dc < 8)
                pieces = [(j, jnp.where(home, moved, 0.0))]
                if j in EDGE_SLOT:
                    pieces.append((EDGE_SLOT[j], jnp.where(home, 0.0, moved)))
                for slot, piece in pieces:
                    pair = jnp.concatenate([piece] * 2, axis=0).astype(BF16)
                    left_ref[pl.ds(pl.multiple_of(idx * 64, 64), 64), slot * 128 : (slot + 1) * 128] = (
                        jnp.concatenate([pair] * 4, axis=0) * own
                    )
            return carry

        lax.fori_loop(0, 4, body, 0)
        product = dot(left_ref[...], place[...])
        for q in range(RHS):
            for kind in range(2):
                base = (q * 2 + kind) * 64
                grid_ref[q, kind, 8 + g * 64 : 8 + (g + 1) * 64, :] = product[base : base + 64]
    zero8 = jnp.zeros((8, 256), F32)
    for q in range(RHS):
        grid_ref[q, 1, 0:8, :] = zero8
        grid_ref[q, 1, 264:272, :] = zero8
    sub = lax.rem(iota((16, 256), 0), 8)
    lane1 = iota((16, 128), 1)
    real_rim = (lane1 < 2) | (lane1 >= 126)
    imag_rim = ((lane1 >= 2) & (lane1 < 4)) | ((lane1 >= 124) & (lane1 < 126))

    def message(parts):
        rim = jnp.where(real_rim, parts[0][:, 128:], jnp.where(imag_rim, parts[1][:, 128:], 0.0))
        return jnp.concatenate([parts[0][:, :128], parts[1][:, :128], rim], axis=0).astype(BF16)

    def slab(k, carry):
        parts = []
        for q in range(RHS):
            at = lambda shift: pl.ds(pl.multiple_of(k * 16 + shift, 8), 16)
            total = grid_ref[q, 0, at(8), :]
            total = total + jnp.where(sub >= 6, grid_ref[q, 1, at(16), :], 0.0)
            total = total + jnp.where(sub < 2, grid_ref[q, 1, at(0), :], 0.0)
            parts.append(total)
        send_ref[k] = message(parts)
        return carry

    lax.fori_loop(0, 16, slab, 0)
    full = iota((16, 256), 0)
    send_ref[16] = message(
        [jnp.where(full >= 14, grid_ref[q, 1, 0:16, :], 0.0) for q in range(RHS)]
    )
    send_ref[17] = message(
        [jnp.where(full < 2, grid_ref[q, 1, 256:272, :], 0.0) for q in range(RHS)]
    )


def row_forward_stage(recv, halo, has_halo, slab_ref, twist, table, mix_ref, flat_ref, out_ref):
    def widen(c, carry):
        slab_ref[c] = recv[c].astype(F32)
        return carry

    lax.fori_loop(0, 16, widen, 0)

    @pl.when(has_halo)
    def _():
        def add(c, carry):
            slab_ref[c] = slab_ref[c] + halo[c].astype(F32)
            return carry

        lax.fori_loop(0, 16, add, 0)

    lane = iota((8, 128), 1)

    def rows(h, carry):
        at = lambda start: pl.ds(pl.multiple_of(start + h * 8, 8), 8)
        rims = [slab_ref[c, at(32), :] for c in range(16)]
        items = []
        for c in range(16):
            real = slab_ref[c, at(0), :]
            imag = slab_ref[c, at(16), :]
            if c > 0:
                real = real + jnp.where(lane < 2, rims[c - 1], 0.0)
                imag = imag + jnp.where(lane < 2, pltpu.roll(rims[c - 1], 126, 1), 0.0)
            if c < 15:
                real = real + jnp.where(lane >= 126, rims[c + 1], 0.0)
                imag = imag + jnp.where(lane >= 126, pltpu.roll(rims[c + 1], 2, 1), 0.0)
            items.append((real, imag))
        even = fft(items, -1)
        odd = fft([cmulc(v, -2 * math.pi * c / 32) for c, v in enumerate(items)], -1)
        for m in range(16):
            for p, (real, imag) in enumerate((even[m], odd[m])):
                k0 = 2 * m + p
                cos, sin = twist[0, k0 : k0 + 1, :], twist[1, k0 : k0 + 1, :]
                mix_ref[at(k0 * 16), 0:128] = real * cos + imag * sin
                mix_ref[at(k0 * 16), 128:256] = imag * cos - real * sin
        return carry

    lax.fori_loop(0, 2, rows, 0)
    high, low = split(mix_ref[...])
    nt = ((1,), (1,))
    out = dot(table[0], high, nt) + dot(table[1], high, nt) + dot(table[0], low, nt)
    to_messages(out, flat_ref, out_ref)


def to_messages(out, flat_ref, out_ref):
    for ri in range(2):
        for g in range(4):
            flat_ref[pl.ds(ri * 4 + g, 128, stride=8), :] = out[
                ri * 128 : (ri + 1) * 128, g * 128 : (g + 1) * 128
            ]
    out_ref[...] = flat_ref[...].reshape(128, 8, 128).astype(BF16)


def from_messages(recv, flat_ref, half_ref):
    flat_ref[...] = recv[...].astype(F32).reshape(1024, 128)
    for ri in range(2):
        for g in range(4):
            half_ref[ri * 128 : (ri + 1) * 128, g * 128 : (g + 1) * 128] = flat_ref[
                pl.ds(ri * 4 + g, 128, stride=8), :
            ].astype(BF16)


def column_stage(recv, flat_ref, half_ref, fwd, inv, small, small_inv, twist, green, wide_ref, out_ref):
    from_messages(recv, flat_ref, half_ref)
    block = half_ref[...]
    wide_ref[...] = dot(fwd[0], block) + dot(fwd[1], block)
    cos, sin = twist[0], twist[1]
    for g in range(4):
        lanes = slice(g * 128, (g + 1) * 128)
        real, imag = wide_ref[0:256, lanes], wide_ref[256:512, lanes]
        turned = jnp.concatenate([real * cos + imag * sin, imag * cos - real * sin], axis=1)
        high, low = split(turned)
        spec = dot(high, small[0]) + dot(low, small[0]) + dot(high, small[1])
        scale = green[:, lanes]
        spec = spec * jnp.concatenate([scale, scale], axis=1)
        high, low = split(spec)
        back = dot(high, small_inv[0]) + dot(low, small_inv[0]) + dot(high, small_inv[1])
        real, imag = back[:, 0:128], back[:, 128:256]
        wide_ref[0:256, lanes] = real * cos - imag * sin
        wide_ref[256:512, lanes] = imag * cos + real * sin
    high, low = split(wide_ref[...])
    out = dot(inv[0], high) + dot(inv[0], low) + dot(inv[1], high)
    to_messages(out, flat_ref, out_ref)


def row_inverse_stage(recv, flat_ref, half_ref, table, twist, mix_ref, slab_ref, send_ref):
    from_messages(recv, flat_ref, half_ref)
    turned = half_ref[...].T
    mix_ref[...] = dot(turned, table[0]) + dot(turned, table[1])

    def rows(h, carry):
        at = lambda start: pl.ds(pl.multiple_of(start + h * 8, 8), 8)
        items = []
        for k0 in range(32):
            cos, sin = twist[0, k0 : k0 + 1, :], twist[1, k0 : k0 + 1, :]
            real, imag = mix_ref[at(k0 * 16), 0:128], mix_ref[at(k0 * 16), 128:256]
            items.append((real * cos - imag * sin, imag * cos + real * sin))
        even = fft(items[0::2], 1)
        odd = fft(items[1::2], 1)
        for c in range(16):
            real, imag = cadd(even[c], cmulc(odd[c], 2 * math.pi * c / 32))
            slab_ref[c, at(0), :] = real
            slab_ref[c, at(16), :] = imag
        return carry

    lax.fori_loop(0, 2, rows, 0)
    lane = iota((16, 128), 1)
    for c in range(16):
        rim = jnp.zeros((16, 128), F32)
        if c < 15:
            rim = jnp.where(lane < 2, slab_ref[c + 1, 0:16, :], rim)
            rim = jnp.where((lane >= 2) & (lane < 4), pltpu.roll(slab_ref[c + 1, 16:32, :], 2, 1), rim)
        if c > 0:
            rim = jnp.where(lane >= 126, slab_ref[c - 1, 0:16, :], rim)
            rim = jnp.where(
                (lane >= 124) & (lane < 126), pltpu.roll(slab_ref[c - 1, 16:32, :], 126, 1), rim
            )
        send_ref[c] = jnp.concatenate([slab_ref[c, 0:32, :], rim], axis=0).astype(BF16)


def sample_stage(recv, pick, shifts, tall_ref, rows_ref, sample_ref):
    sub = iota((8, 128), 0)
    lane = iota((8, 128), 1)
    owns = [(lane // 16) == e for e in range(8)]
    for q in range(RHS):
        main = recv[:, q * 16 : (q + 1) * 16, :].reshape(288, 128)
        rim = recv[:, 32:48, :].reshape(288, 128)
        tall_ref[...] = dot(jnp.concatenate([main, rim], axis=1), pick[q])
        for g in range(4):
            lanes = slice(g * 128, (g + 1) * 128)
            dr = jnp.broadcast_to(shifts[0:1, lanes], (8, 128))
            dc = jnp.broadcast_to(shifts[1:2, lanes], (8, 128))

            def body(slot, carry):
                column = pl.ds(pl.multiple_of(slot * 128, 128), 128)
                tiles = [
                    tall_ref[8 + 64 * g + 8 * t : 16 + 64 * g + 8 * t, column] for t in range(10)
                ]
                home = tiles[1]
                edge = jnp.where(sub < 4, tiles[2], tiles[0])
                for e in range(1, 8):
                    home = jnp.where(owns[e], tiles[e + 1], home)
                    edge = jnp.where(owns[e], jnp.where(sub < 4, tiles[e + 2], tiles[e]), edge)
                moved = home
                for o in OFFSETS:
                    kept = (sub >= o) if o > 0 else (sub < 8 + o)
                    shifted = pltpu.roll(jnp.where(kept, home, edge), (-o) % 8, 0)
                    moved = jnp.where(dr == o, shifted, moved)
                rows_ref[slot] = moved
                return carry

            lax.fori_loop(0, 12, body, 0)
            line = lambda j: rows_ref[j] if 0 <= j < 8 else rows_ref[EDGE_SLOT[j % 8]]
            for j in range(8):
                moved = line(j)
                for o in OFFSETS:
                    moved = jnp.where(dc == o, line(j + o), moved)
                sample_ref[q, j, :, lanes] = moved


def far_stage(proj, sample_ref, near_ref, out_ref):
    for g in range(4):
        lanes = slice(g * 128, (g + 1) * 128)

        def body(j, sums):
            sums = list(sums)
            for i in range(8):
                weight = proj[i * 8 + j, :, lanes].astype(F32)
                for q in range(RHS):
                    line = sample_ref[q, j, i : i + 1, lanes]
                    sums[q] = sums[q] + weight * line
            return tuple(sums)

        sums = lax.fori_loop(0, 8, body, tuple(near_ref[q, :, lanes] for q in range(RHS)))
        for q in range(RHS):
            out_ref[q, :, lanes] = sums[q]


def turn_green(green, rows_ref, out_ref):
    for j1 in range(16):
        for h in range(2):
            rows_ref[h, pl.ds(j1, 32, stride=16), :] = green[
                :, j1 * 256 + h * 128 : j1 * 256 + (h + 1) * 128
            ]
    for h in range(2):
        for g in range(4):
            out_ref[h * 128 : (h + 1) * 128, g * 128 : (g + 1) * 128] = rows_ref[
                h, g * 128 : (g + 1) * 128, :
            ].T * (1.0 / 16777216)


def edge_stage(curf, edge_row, edge_col):
    lane = iota((16, 128), 1)
    place = lax.rem(lane, 16)

    def body(m, carry):
        q, at = m // 4, pl.ds(pl.multiple_of(lax.rem(m, 4) * 16, 16), 16)
        here = pl.ds(pl.multiple_of(m * 16, 16), 16)
        tiles = [curf[q, at, t * 128 : (t + 1) * 128] for t in range(4)]
        edge_row[here, :] = jnp.where(lane < 64, tiles[0], tiles[3]).astype(BF16)
        packed = jnp.zeros((16, 128), F32)
        for t in range(4):
            packed = jnp.where(place == t, pltpu.roll(tiles[t], (t - 15) % 128, 1), packed)
            packed = jnp.where(place == 4 + t, pltpu.roll(tiles[t], 4 + t, 1), packed)
        edge_col[here, :] = packed.astype(BF16)
        return carry

    lax.fori_loop(0, 8, body, 0)


def partner_stage(curf, partners, edges, picked):
    lane = iota((16, 128), 1)
    place = lax.rem(lane, 16)

    def body(m, carry):
        q, at = m // 4, pl.ds(pl.multiple_of(lax.rem(m, 4) * 16, 16), 16)
        here = pl.ds(pl.multiple_of(m * 16, 16), 16)
        near = lambda dr, dc: edges[edge_slot(dr, dc), here, :].astype(F32)
        middle = [near(-1, 0)]
        middle += [curf[q, at, t * 128 : (t + 1) * 128] for t in range(4)]
        middle += [near(1, 0)]
        left, right = near(0, -1), near(0, 1)
        from_right = [near(-1, 1), right, right, right, right, near(1, 1)]
        from_left = [near(-1, -1), left, left, left, left, near(1, -1)]
        columns = {0: middle, 1: [], -1: []}
        for e in range(6):
            inner = e in (1, 2, 3, 4)
            t = e - 1
            outside = pltpu.roll(from_right[e], (11 - t) % 128 if inner else 15, 1)
            columns[1].append(jnp.where(place == 15, outside, pltpu.roll(middle[e], 127, 1)))
            outside = pltpu.roll(from_left[e], (-t) % 128 if inner else 113, 1)
            columns[-1].append(jnp.where(place == 0, outside, pltpu.roll(middle[e], 1, 1)))
        for t in range(4):
            lanes = slice(t * 128, (t + 1) * 128)
            views = {}
            for dc in (-1, 0, 1):
                x = columns[dc]
                views[0, dc] = x[t + 1]
                views[1, dc] = pltpu.roll(jnp.where(lane < 16, x[t + 2], x[t + 1]), 112, 1)
                views[-1, dc] = pltpu.roll(jnp.where(lane >= 112, x[t], x[t + 1]), 16, 1)
            for k in range(1, NEIGH):
                code = jnp.broadcast_to(partners[k : k + 1, lanes], (16, 128))
                chosen = views[0, 0]
                for dr in (-1, 0, 1):
                    for dc in (-1, 0, 1):
                        if dr or dc:
                            chosen = jnp.where(code == 3 * (dr + 1) + dc + 1, views[dr, dc], chosen)
                picked[k - 1, q, at, lanes] = chosen
        return carry

    lax.fori_loop(0, 8, body, 0)


def near_stage(blocks, k, values, near_ref):
    def body(m, carry):
        a0 = pl.multiple_of((m // 4) * 8, 8)
        lanes = pl.ds(pl.multiple_of(lax.rem(m, 4) * 128, 128), 128)
        sums = [None] * 16
        for b in range(4):
            at = slice(16 * b, 16 * b + 16)
            current = [values[q, at, lanes] for q in range(RHS)]
            for a in range(8):
                weight = blocks[k, a0 + a, at, lanes].astype(F32)
                for q in range(RHS):
                    part = fold(weight * current[q])
                    old = sums[q * 8 + a]
                    sums[q * 8 + a] = part if old is None else old + part
        for q in range(RHS):
            tile = row_sums(sums[q * 8 : q * 8 + 8])
            if k > 0:
                tile = tile + near_ref[q, pl.ds(a0, 8), lanes]
            near_ref[q, pl.ds(a0, 8), lanes] = tile
        return carry

    lax.fori_loop(0, 32, body, 0)


AROUND = [(dr, dc) for dr in (-1, 0, 1) for dc in (-1, 0, 1) if dr or dc]


def edge_slot(dr, dc):
    return AROUND.index((dr, dc))


def hop_order():
    hop = lambda d: min(d, 4 - d)
    offsets = [
        (x, y, z, core) for x in range(4) for y in range(4) for z in range(4) for core in range(2)
    ][1:]
    return sorted(offsets, key=lambda o: -(hop(o[0]) + hop(o[1]) + hop(o[2])))


def slots_wait(ref, count, sem):
    part = ref.at[pl.ds(0, count)]
    pltpu.make_async_copy(part, part, sem).wait()


TABLES = 10


def main_kernel(*refs):
    cur, shifts, partners, proj_hbm, blocks_hbm, green_hbm = refs[:6]
    tables_hbm = refs[6 : 6 + TABLES]
    out_ref = refs[6 + TABLES]
    scratch = refs[7 + TABLES :]
    tables = scratch[:TABLES]
    place, pick, row_fwd, row_inv, col_fwd, col_inv, small, small_inv, twist_row, twist_col = tables
    (
        proj, blocks, green, rows_ref, left_ref, grid_ref, send1, recv1, halo1, slab_ref, mix_ref,
        flat_ref, send2, recv2, half_ref, wide_ref, green_rows, green_turned, send3, recv3, send4,
        recv4, tall_ref, pick_rows, sample_ref, curf, edge_row, edge_col, edges, picked, near_ref,
        ssem, rsem, hsem, lsem, esem_out, esem_in, psem, nsem, tsem, entered,
    ) = scratch[TABLES:]
    r, c = lax.axis_index("row"), lax.axis_index("col")
    me = r * 16 + c
    core, y_low, z = c & 1, lax.shift_right_logical(c, 1) & 1, lax.shift_right_logical(c, 2)
    x, y = lax.shift_right_logical(r, 1), (r & 1) * 2 + y_low

    proj_copies = [
        pltpu.make_async_copy(
            proj_hbm.at[:, :, pl.ds(g * 128, 128)], proj.at[:, :, pl.ds(g * 128, 128)], psem.at[g]
        )
        for g in range(4)
    ]
    table_copies = [pltpu.make_async_copy(a, b, tsem.at[i]) for i, (a, b) in enumerate(zip(tables_hbm, tables))]
    green_copy = pltpu.make_async_copy(green_hbm, green, tsem.at[TABLES])
    block_copies = [pltpu.make_async_copy(blocks_hbm.at[k], blocks.at[k], nsem.at[k]) for k in range(NEIGH)]
    for copy in proj_copies:
        copy.start()
    table_copies[0].start()

    barrier = pltpu.get_barrier_semaphore()

    def greet_column(k, carry):
        pl.semaphore_signal(barrier, inc=1, device_id=(r, (c + k) & 15), device_id_type=MESH)
        return carry

    def greet_row(k, carry):
        pl.semaphore_signal(barrier, inc=1, device_id=((r + k) & 7, c), device_id_type=MESH)
        return carry

    lax.fori_loop(1, 8, greet_row, 0)
    lax.fori_loop(1, 16, greet_column, 0)
    zero = jnp.zeros((48, 128), BF16)
    recv4[0] = zero
    recv4[17] = zero
    curf[...] = cur[...].astype(BF16).astype(F32)
    edge_stage(curf, edge_row, edge_col)
    stencil_stage(proj, curf, shifts, rows_ref, lambda g: proj_copies[g].wait())
    for copy in table_copies[1:]:
        copy.start()
    green_copy.start()
    for copy in block_copies:
        copy.start()
    pl.semaphore_wait(barrier, 22)

    def tell_column(k, carry):
        pl.semaphore_signal(entered, inc=1, device_id=(r, (c + k) & 15), device_id_type=MESH)
        return carry

    lax.fori_loop(1, 16, tell_column, 0)
    table_copies[0].wait()
    spread_stage(rows_ref, shifts, place, left_ref, grid_ref, send1)
    pl.semaphore_wait(entered, 15)

    def remote(source, target, send_sem, recv_sem, where):
        return pltpu.make_async_remote_copy(
            source, target, send_sem, recv_sem, device_id=where, device_id_type=MESH
        )

    def to_column(send, recv, slot, index):
        for dx, dy, dz, dcore in hop_order():
            if dx == 0 and dy < 2:
                d = ((z + dz) & 3) * 4 + (y_low ^ dy) * 2 + (core ^ dcore)
                remote(send.at[d], recv.at[slot], ssem.at[index], rsem.at[index], (r, d)).start()

    @pl.when(r > 0)
    def _():
        remote(send1.at[16], halo1.at[c], ssem.at[4], hsem.at[0], (r - 1, 15)).start()

    @pl.when(r < 7)
    def _():
        remote(send1.at[17], halo1.at[c], ssem.at[5], hsem.at[0], (r + 1, 0)).start()

    to_column(send1, recv1, c, 0)
    own = pltpu.make_async_copy(send1.at[c], recv1.at[c], lsem.at[0])
    own.start()

    def exists(dr, dc):
        there = None
        for move, at, last in ((dr, r, 7), (dc, c, 15)):
            test = at < last if move > 0 else at > 0
            if move:
                there = test if there is None else there & test
        return there

    def edge_copy(dr, dc):
        target = edge_slot(-dr, -dc)
        return remote(
            edge_row if dr else edge_col, edges.at[target], esem_out.at[edge_slot(dr, dc)],
            esem_in.at[target], (r + dr, c + dc),
        )

    for dr, dc in AROUND:
        @pl.when(exists(dr, dc))
        def _():
            edge_copy(dr, dc).start()

    green_copy.wait()
    turn_green(green, green_rows, green_turned)
    block_copies[0].wait()
    near_stage(blocks, 0, curf, near_ref)
    for copy in table_copies[1:]:
        copy.wait()
    own.wait()
    has_halo = ((c == 0) & (r > 0)) | ((c == 15) & (r < 7))
    slots_wait(recv1, 15, rsem.at[0])

    @pl.when(has_halo)
    def _():
        slots_wait(halo1, 16, hsem.at[0])

    row_forward_stage(recv1, halo1, has_halo, slab_ref, twist_row, row_fwd, mix_ref, flat_ref, send2)

    def to_all(send, recv, index):
        own = pltpu.make_async_copy(send.at[me], recv.at[me], lsem.at[index])
        own.start()
        for dx, dy, dz, dcore in hop_order():
            px, py, pz, pcore = (x + dx) & 3, (y + dy) & 3, (z + dz) & 3, core ^ dcore
            row = px * 2 + lax.shift_right_logical(py, 1)
            col = pz * 4 + (py & 1) * 2 + pcore
            remote(send.at[row * 16 + col], recv.at[me], ssem.at[index], rsem.at[index], (row, col)).start()
        return own

    own = to_all(send2, recv2, 1)
    for dr, dc in AROUND:
        @pl.when(exists(dr, dc))
        def _():
            back = edges.at[edge_slot(dr, dc)]
            pltpu.make_async_copy(back, back, esem_in.at[edge_slot(dr, dc)]).wait()

    partner_stage(curf, partners, edges, picked)
    for k in (1, 2):
        block_copies[k].wait()
        near_stage(blocks, k, picked.at[k - 1], near_ref)
    own.wait()
    slots_wait(recv2, 127, rsem.at[1])
    column_stage(
        recv2, flat_ref, half_ref, col_fwd, col_inv, small, small_inv, twist_col, green_turned, wide_ref, send3
    )
    own = to_all(send3, recv3, 2)
    block_copies[3].wait()
    near_stage(blocks, 3, picked.at[2], near_ref)
    own.wait()
    slots_wait(recv3, 127, rsem.at[2])
    row_inverse_stage(recv3, flat_ref, half_ref, row_inv, twist_row, mix_ref, slab_ref, send4)

    def to_neighbour_row(target, slot, index, sem):
        def go(d, carry):
            remote(send4.at[d], recv4.at[slot], ssem.at[index], hsem.at[sem], (target, d)).start()
            return carry

        lax.fori_loop(0, 16, go, 0)

    up = (c == 0) & (r > 0)
    down = (c == 15) & (r < 7)

    @pl.when(up)
    def _():
        to_neighbour_row(r - 1, 17, 6, 1)

    @pl.when(down)
    def _():
        to_neighbour_row(r + 1, 0, 7, 2)

    to_column(send4, recv4, c + 1, 3)
    own = pltpu.make_async_copy(send4.at[c], recv4.at[c + 1], lsem.at[3])
    own.start()
    own.wait()
    slots_wait(recv4, 15, rsem.at[3])

    @pl.when(r < 7)
    def _():
        slots_wait(recv4, 1, hsem.at[1])

    @pl.when(r > 0)
    def _():
        slots_wait(recv4, 1, hsem.at[2])

    sample_stage(recv4, pick, shifts, tall_ref, pick_rows, sample_ref)
    far_stage(proj, sample_ref, near_ref, out_ref)

    slots_wait(send1, 15, ssem.at[0])

    @pl.when(r > 0)
    def _():
        slots_wait(send1, 1, ssem.at[4])

    @pl.when(r < 7)
    def _():
        slots_wait(send1, 1, ssem.at[5])

    for dr, dc in AROUND:
        @pl.when(exists(dr, dc))
        def _():
            pltpu.make_async_copy(edge_row, edge_row, esem_out.at[edge_slot(dr, dc)]).wait()

    slots_wait(send2, 127, ssem.at[1])
    slots_wait(send3, 127, ssem.at[2])
    slots_wait(send4, 15, ssem.at[3])

    @pl.when(up)
    def _():
        slots_wait(send4, 16, ssem.at[6])

    @pl.when(down)
    def _():
        slots_wait(send4, 16, ssem.at[7])


def shards(currents, projection, near_blocks, partners, shifts, green):
    tables = [jnp.asarray(t) for t in make_tables()]
    vmem = pl.BlockSpec(memory_space=pltpu.VMEM)
    hbm = pl.BlockSpec(memory_space=pltpu.HBM)
    dma = pltpu.SemaphoreType.DMA
    return pl.pallas_call(
        main_kernel,
        out_shape=jax.ShapeDtypeStruct((RHS, BASIS, ER * EC), F32),
        in_specs=[vmem] * 3 + [hbm] * (3 + len(tables)),
        out_specs=vmem,
        scratch_shapes=[pltpu.VMEM(t.shape, t.dtype) for t in tables]
        + [
            pltpu.VMEM((64, BASIS, 512), BF16),
            pltpu.VMEM((NEIGH, BASIS, BASIS, 512), BF16),
            pltpu.VMEM((32, 4096), F32),
            pltpu.VMEM((RHS, 2, 8, 8, 512), F32),
            pltpu.VMEM((256, 1536), BF16),
            pltpu.VMEM((RHS, 2, 272, 256), F32),
            pltpu.VMEM((18, 48, 128), BF16),
            pltpu.VMEM((16, 48, 128), BF16),
            pltpu.VMEM((16, 48, 128), BF16),
            pltpu.VMEM((16, 48, 128), F32),
            pltpu.VMEM((512, 256), F32),
            pltpu.VMEM((1024, 128), F32),
            pltpu.VMEM((128, 8, 128), BF16),
            pltpu.VMEM((128, 8, 128), BF16),
            pltpu.VMEM((256, 512), BF16),
            pltpu.VMEM((512, 512), F32),
            pltpu.VMEM((2, 512, 128), F32),
            pltpu.VMEM((256, 512), F32),
            pltpu.VMEM((128, 8, 128), BF16),
            pltpu.VMEM((128, 8, 128), BF16),
            pltpu.VMEM((16, 48, 128), BF16),
            pltpu.VMEM((18, 48, 128), BF16),
            pltpu.VMEM((288, 1536), F32),
            pltpu.VMEM((12, 8, 128), F32),
            pltpu.VMEM((RHS, 8, 8, 512), F32),
            pltpu.VMEM((RHS, BASIS, 512), F32),
            pltpu.VMEM((128, 128), BF16),
            pltpu.VMEM((128, 128), BF16),
            pltpu.VMEM((8, 128, 128), BF16),
            pltpu.VMEM((NEIGH - 1, RHS, BASIS, 512), F32),
            pltpu.VMEM((RHS, BASIS, 512), F32),
            dma((8,)),
            dma((4,)),
            dma((3,)),
            dma((4,)),
            dma((8,)),
            dma((8,)),
            dma((4,)),
            dma((NEIGH,)),
            dma((len(tables) + 1,)),
            pltpu.SemaphoreType.REGULAR,
        ],
        compiler_params=pltpu.CompilerParams(
            collective_id=0, has_side_effects=True, vmem_limit_bytes=52 * 2**20
        ),
    )(currents, shifts, partners, projection, near_blocks, green, *tables)


def solution(mesh):
    in_specs = (
        P(None, None, ("row", "col")),
        P(None, None, ("row", "col")),
        P(None, None, None, ("row", "col")),
        P(None, ("row", "col")),
        P(None, ("row", "col")),
        P(("row", "col"), None),
    )
    out_specs = P(None, None, ("row", "col"))
    return jax.shard_map(shards, mesh=mesh, in_specs=in_specs, out_specs=out_specs, check_vma=False)
```

```python
import functools
import math

import jax
import jax.numpy as jnp
import ml_dtypes
import numpy as np
from jax import lax
from jax.experimental import pallas as pl
from jax.experimental.pallas import tpu as pltpu
from jax.sharding import PartitionSpec as P

MESH = pl.DeviceIdType.MESH
F32 = jnp.float32
BF16 = jnp.bfloat16
BASIS = 64
ER = 32
EC = 16
NEIGH = 4
RHS = 2
OFFSETS = (-2, -1, 1, 2)
EDGE_SLOT = {0: 8, 1: 9, 6: 10, 7: 11}


def halves(table):
    high = np.asarray(table, np.float64).astype(ml_dtypes.bfloat16)
    low = (table - high.astype(np.float64)).astype(ml_dtypes.bfloat16)
    return np.stack([high, low])


def make_tables():
    turn = lambda rows, cols, modulus: (
        2.0 * np.pi * ((np.arange(rows)[:, None] * np.arange(cols)[None, :]) % modulus) / modulus
    )
    place = np.zeros((12, 8, 16, 256))
    for ec in range(16):
        for j in range(8):
            place[j, :, ec, 8 * ec + j] = 1
        for j in (0, 1):
            if ec < 15:
                place[EDGE_SLOT[j], :, ec, 8 * (ec + 1) + j] = 1
            else:
                place[EDGE_SLOT[j], :, ec, 128 + j] = 1
                place[EDGE_SLOT[j], :, ec, 128 + 2 + j] = 1
        for j in (6, 7):
            if ec > 0:
                place[EDGE_SLOT[j], :, ec, 8 * (ec - 1) + j] = 1
            else:
                place[EDGE_SLOT[j], :, ec, 128 + 120 + j] = 1
                place[EDGE_SLOT[j], :, ec, 128 + 118 + j] = 1
    place = place.reshape(1536, 256)
    pick = np.stack([place.T, place.T])
    real_lanes = [128 + 0, 128 + 1, 128 + 126, 128 + 127]
    imag_lanes = [128 + 2, 128 + 3, 128 + 124, 128 + 125]
    pick[0, imag_lanes] = 0
    pick[1, real_lanes] = 0
    a = turn(128, 128, 128)
    row_fwd = np.block([[np.cos(a), np.sin(a)], [-np.sin(a), np.cos(a)]])
    row_inv = np.block([[np.cos(a), np.sin(a)], [-np.sin(a), np.cos(a)]])
    b = turn(256, 128, 256)
    col_fwd = np.block([[np.cos(b), np.sin(b)], [-np.sin(b), np.cos(b)]])
    col_inv = col_fwd.T
    c = turn(16, 16, 16)
    eye = np.eye(8)
    kc, ks = np.kron(eye, np.cos(c)), np.kron(eye, np.sin(c))
    small_fwd = np.block([[kc, -ks], [ks, kc]])
    small_inv = small_fwd.T
    t1 = turn(32, 128, 4096)
    twist_row = np.stack([np.cos(t1), np.sin(t1)])
    t2 = np.tile(turn(256, 16, 4096), (1, 8))
    twist_col = np.stack([np.cos(t2), np.sin(t2)])
    half = ml_dtypes.bfloat16
    return (
        place.astype(half),
        pick.astype(half),
        halves(row_fwd),
        halves(row_inv),
        halves(col_fwd),
        halves(col_inv),
        halves(small_fwd),
        halves(small_inv),
        twist_row.astype(np.float32),
        twist_col.astype(np.float32),
    )


def dot(a, b, dims=((1,), (0,))):
    return lax.dot_general(a, b, (dims, ((), ())), preferred_element_type=F32)


def split(x):
    high = x.astype(BF16)
    return high, (x - high.astype(F32)).astype(BF16)


def cadd(a, b):
    return (a[0] + b[0], a[1] + b[1])


def csub(a, b):
    return (a[0] - b[0], a[1] - b[1])


def cmulc(a, angle):
    turns = angle / (2 * math.pi)
    quarter = round(turns * 4)
    if abs(turns * 4 - quarter) < 1e-9:
        quarter %= 4
        if quarter == 0:
            return a
        if quarter == 1:
            return (-a[1], a[0])
        if quarter == 2:
            return (-a[0], -a[1])
        return (a[1], -a[0])
    c, s = math.cos(angle), math.sin(angle)
    return (a[0] * c - a[1] * s, a[0] * s + a[1] * c)


def fft(items, sign):
    n = len(items)
    if n == 1:
        return items
    even = fft(items[0::2], sign)
    odd = fft(items[1::2], sign)
    out = [None] * n
    for k in range(n // 2):
        t = cmulc(odd[k], sign * 2 * math.pi * k / n)
        out[k] = cadd(even[k], t)
        out[k + n // 2] = csub(even[k], t)
    return out


def iota(shape, dim):
    return lax.broadcasted_iota(jnp.int32, shape, dim)


def row_sums(tiles):
    sub = iota((8, 128), 0)
    top = sub < 4
    tiles = [
        jnp.where(top, tiles[i], tiles[i + 4])
        + pltpu.roll(jnp.where(top, tiles[i + 4], tiles[i]), 4, 0)
        for i in range(4)
    ]
    for step in (2, 1):
        upper = lax.rem(sub, 2 * step) < step
        tiles = [
            jnp.where(
                upper,
                tiles[i] + pltpu.roll(tiles[i], 8 - step, 0),
                tiles[i + step] + pltpu.roll(tiles[i + step], step, 0),
            )
            for i in range(step)
        ]
    return tiles[0]


def fold(x):
    total = x[0:8]
    for b in range(1, x.shape[0] // 8):
        total = total + x[8 * b : 8 * b + 8]
    return total


def stencil_stage(proj, curf, shifts, rows_ref, ready):
    sub = iota((8, 128), 0)
    for g in range(4):
        lanes = slice(g * 128, (g + 1) * 128)
        dr = jnp.broadcast_to(shifts[0:1, lanes], (8, 128))
        home = (sub - dr >= 0) & (sub - dr < 8)
        cur = [curf[q, :, lanes] for q in range(RHS)]

        ready(g)

        def body(j, carry):
            parts = [[] for _ in range(RHS)]
            for i in range(8):
                weight = proj[i * 8 + j, :, lanes].astype(F32)
                for q in range(RHS):
                    parts[q].append(fold(weight * cur[q]))
            tiles = [row_sums(part) for part in parts]
            for q in range(RHS):
                moved = tiles[q]
                for o in OFFSETS:
                    moved = jnp.where(dr == o, pltpu.roll(tiles[q], o % 8, 0), moved)
                rows_ref[q, 0, j, :, lanes] = jnp.where(home, moved, 0.0)
                rows_ref[q, 1, j, :, lanes] = jnp.where(home, 0.0, moved)
            return carry

        lax.fori_loop(0, 8, body, 0)


def spread_stage(rows_ref, shifts, place, left_ref, grid_ref, send_ref):
    sub = iota((64, 128), 0)
    lane = iota((64, 128), 1)
    own = jnp.where((sub // 8) == (lane // 16), 1.0, 0.0).astype(BF16)
    for g in range(4):
        lanes = slice(g * 128, (g + 1) * 128)
        dc = jnp.broadcast_to(shifts[1:2, lanes], (8, 128))
        is_offset = {o: dc == o for o in OFFSETS}

        def body(idx, carry):
            q, kind = idx // 2, lax.rem(idx, 2)
            tiles = [rows_ref[q, kind, j, :, lanes] for j in range(8)]
            for j in range(8):
                moved = tiles[j]
                for o in OFFSETS:
                    moved = jnp.where(is_offset[o], tiles[(j - o) % 8], moved)
                home = (j - dc >= 0) & (j - dc < 8)
                pieces = [(j, jnp.where(home, moved, 0.0))]
                if j in EDGE_SLOT:
                    pieces.append((EDGE_SLOT[j], jnp.where(home, 0.0, moved)))
                for slot, piece in pieces:
                    pair = jnp.concatenate([piece] * 2, axis=0).astype(BF16)
                    left_ref[pl.ds(pl.multiple_of(idx * 64, 64), 64), slot * 128 : (slot + 1) * 128] = (
                        jnp.concatenate([pair] * 4, axis=0) * own
                    )
            return carry

        lax.fori_loop(0, 4, body, 0)
        product = dot(left_ref[...], place[...])
        for q in range(RHS):
            for kind in range(2):
                base = (q * 2 + kind) * 64
                grid_ref[q, kind, 8 + g * 64 : 8 + (g + 1) * 64, :] = product[base : base + 64]
    zero8 = jnp.zeros((8, 256), F32)
    for q in range(RHS):
        grid_ref[q, 1, 0:8, :] = zero8
        grid_ref[q, 1, 264:272, :] = zero8
    sub = lax.rem(iota((16, 256), 0), 8)
    lane1 = iota((16, 128), 1)
    real_rim = (lane1 < 2) | (lane1 >= 126)
    imag_rim = ((lane1 >= 2) & (lane1 < 4)) | ((lane1 >= 124) & (lane1 < 126))

    def message(parts):
        rim = jnp.where(real_rim, parts[0][:, 128:], jnp.where(imag_rim, parts[1][:, 128:], 0.0))
        return jnp.concatenate([parts[0][:, :128], parts[1][:, :128], rim], axis=0).astype(BF16)

    def slab(k, carry):
        parts = []
        for q in range(RHS):
            at = lambda shift: pl.ds(pl.multiple_of(k * 16 + shift, 8), 16)
            total = grid_ref[q, 0, at(8), :]
            total = total + jnp.where(sub >= 6, grid_ref[q, 1, at(16), :], 0.0)
            total = total + jnp.where(sub < 2, grid_ref[q, 1, at(0), :], 0.0)
            parts.append(total)
        send_ref[k] = message(parts)
        return carry

    lax.fori_loop(0, 16, slab, 0)
    full = iota((16, 256), 0)
    send_ref[16] = message(
        [jnp.where(full >= 14, grid_ref[q, 1, 0:16, :], 0.0) for q in range(RHS)]
    )
    send_ref[17] = message(
        [jnp.where(full < 2, grid_ref[q, 1, 256:272, :], 0.0) for q in range(RHS)]
    )


def row_forward_stage(recv, halo, has_halo, slab_ref, twist, table, mix_ref, flat_ref, out_ref):
    def widen(c, carry):
        slab_ref[c] = recv[c].astype(F32)
        return carry

    lax.fori_loop(0, 16, widen, 0)

    @pl.when(has_halo)
    def _():
        def add(c, carry):
            slab_ref[c] = slab_ref[c] + halo[c].astype(F32)
            return carry

        lax.fori_loop(0, 16, add, 0)

    lane = iota((8, 128), 1)

    def rows(h, carry):
        at = lambda start: pl.ds(pl.multiple_of(start + h * 8, 8), 8)
        rims = [slab_ref[c, at(32), :] for c in range(16)]
        items = []
        for c in range(16):
            real = slab_ref[c, at(0), :]
            imag = slab_ref[c, at(16), :]
            if c > 0:
                real = real + jnp.where(lane < 2, rims[c - 1], 0.0)
                imag = imag + jnp.where(lane < 2, pltpu.roll(rims[c - 1], 126, 1), 0.0)
            if c < 15:
                real = real + jnp.where(lane >= 126, rims[c + 1], 0.0)
                imag = imag + jnp.where(lane >= 126, pltpu.roll(rims[c + 1], 2, 1), 0.0)
            items.append((real, imag))
        even = fft(items, -1)
        odd = fft([cmulc(v, -2 * math.pi * c / 32) for c, v in enumerate(items)], -1)
        for m in range(16):
            for p, (real, imag) in enumerate((even[m], odd[m])):
                k0 = 2 * m + p
                cos, sin = twist[0, k0 : k0 + 1, :], twist[1, k0 : k0 + 1, :]
                mix_ref[at(k0 * 16), 0:128] = real * cos + imag * sin
                mix_ref[at(k0 * 16), 128:256] = imag * cos - real * sin
        return carry

    lax.fori_loop(0, 2, rows, 0)
    high, low = split(mix_ref[...])
    nt = ((1,), (1,))
    out = dot(table[0], high, nt) + dot(table[1], high, nt) + dot(table[0], low, nt)
    to_messages(out, flat_ref, out_ref)


def to_messages(out, flat_ref, out_ref):
    for ri in range(2):
        for g in range(4):
            flat_ref[pl.ds(ri * 4 + g, 128, stride=8), :] = out[
                ri * 128 : (ri + 1) * 128, g * 128 : (g + 1) * 128
            ]
    out_ref[...] = flat_ref[...].reshape(128, 8, 128).astype(BF16)


def from_messages(recv, flat_ref, half_ref):
    flat_ref[...] = recv[...].astype(F32).reshape(1024, 128)
    for ri in range(2):
        for g in range(4):
            half_ref[ri * 128 : (ri + 1) * 128, g * 128 : (g + 1) * 128] = flat_ref[
                pl.ds(ri * 4 + g, 128, stride=8), :
            ].astype(BF16)


def column_stage(recv, flat_ref, half_ref, fwd, inv, small, small_inv, twist, green, wide_ref, out_ref):
    from_messages(recv, flat_ref, half_ref)
    block = half_ref[...]
    wide_ref[...] = dot(fwd[0], block) + dot(fwd[1], block)
    cos, sin = twist[0], twist[1]
    for g in range(4):
        lanes = slice(g * 128, (g + 1) * 128)
        real, imag = wide_ref[0:256, lanes], wide_ref[256:512, lanes]
        turned = jnp.concatenate([real * cos + imag * sin, imag * cos - real * sin], axis=1)
        high, low = split(turned)
        spec = dot(high, small[0]) + dot(low, small[0]) + dot(high, small[1])
        scale = green[:, lanes]
        spec = spec * jnp.concatenate([scale, scale], axis=1)
        high, low = split(spec)
        back = dot(high, small_inv[0]) + dot(low, small_inv[0]) + dot(high, small_inv[1])
        real, imag = back[:, 0:128], back[:, 128:256]
        wide_ref[0:256, lanes] = real * cos - imag * sin
        wide_ref[256:512, lanes] = imag * cos + real * sin
    high, low = split(wide_ref[...])
    out = dot(inv[0], high) + dot(inv[0], low) + dot(inv[1], high)
    to_messages(out, flat_ref, out_ref)


def row_inverse_stage(recv, flat_ref, half_ref, table, twist, mix_ref, slab_ref, send_ref):
    from_messages(recv, flat_ref, half_ref)
    turned = half_ref[...].T
    mix_ref[...] = dot(turned, table[0]) + dot(turned, table[1])

    def rows(h, carry):
        at = lambda start: pl.ds(pl.multiple_of(start + h * 8, 8), 8)
        items = []
        for k0 in range(32):
            cos, sin = twist[0, k0 : k0 + 1, :], twist[1, k0 : k0 + 1, :]
            real, imag = mix_ref[at(k0 * 16), 0:128], mix_ref[at(k0 * 16), 128:256]
            items.append((real * cos - imag * sin, imag * cos + real * sin))
        even = fft(items[0::2], 1)
        odd = fft(items[1::2], 1)
        for c in range(16):
            real, imag = cadd(even[c], cmulc(odd[c], 2 * math.pi * c / 32))
            slab_ref[c, at(0), :] = real
            slab_ref[c, at(16), :] = imag
        return carry

    lax.fori_loop(0, 2, rows, 0)
    lane = iota((16, 128), 1)
    for c in range(16):
        rim = jnp.zeros((16, 128), F32)
        if c < 15:
            rim = jnp.where(lane < 2, slab_ref[c + 1, 0:16, :], rim)
            rim = jnp.where((lane >= 2) & (lane < 4), pltpu.roll(slab_ref[c + 1, 16:32, :], 2, 1), rim)
        if c > 0:
            rim = jnp.where(lane >= 126, slab_ref[c - 1, 0:16, :], rim)
            rim = jnp.where(
                (lane >= 124) & (lane < 126), pltpu.roll(slab_ref[c - 1, 16:32, :], 126, 1), rim
            )
        send_ref[c] = jnp.concatenate([slab_ref[c, 0:32, :], rim], axis=0).astype(BF16)


def sample_stage(recv, pick, shifts, tall_ref, rows_ref, sample_ref):
    sub = iota((8, 128), 0)
    lane = iota((8, 128), 1)
    owns = [(lane // 16) == e for e in range(8)]
    for q in range(RHS):
        main = recv[:, q * 16 : (q + 1) * 16, :].reshape(288, 128)
        rim = recv[:, 32:48, :].reshape(288, 128)
        tall_ref[...] = dot(jnp.concatenate([main, rim], axis=1), pick[q])
        for g in range(4):
            lanes = slice(g * 128, (g + 1) * 128)
            dr = jnp.broadcast_to(shifts[0:1, lanes], (8, 128))
            dc = jnp.broadcast_to(shifts[1:2, lanes], (8, 128))

            def body(slot, carry):
                column = pl.ds(pl.multiple_of(slot * 128, 128), 128)
                tiles = [
                    tall_ref[8 + 64 * g + 8 * t : 16 + 64 * g + 8 * t, column] for t in range(10)
                ]
                home = tiles[1]
                edge = jnp.where(sub < 4, tiles[2], tiles[0])
                for e in range(1, 8):
                    home = jnp.where(owns[e], tiles[e + 1], home)
                    edge = jnp.where(owns[e], jnp.where(sub < 4, tiles[e + 2], tiles[e]), edge)
                moved = home
                for o in OFFSETS:
                    kept = (sub >= o) if o > 0 else (sub < 8 + o)
                    shifted = pltpu.roll(jnp.where(kept, home, edge), (-o) % 8, 0)
                    moved = jnp.where(dr == o, shifted, moved)
                rows_ref[slot] = moved
                return carry

            lax.fori_loop(0, 12, body, 0)
            line = lambda j: rows_ref[j] if 0 <= j < 8 else rows_ref[EDGE_SLOT[j % 8]]
            for j in range(8):
                moved = line(j)
                for o in OFFSETS:
                    moved = jnp.where(dc == o, line(j + o), moved)
                sample_ref[q, j, :, lanes] = moved


def far_stage(proj, sample_ref, near_ref, out_ref):
    for g in range(4):
        lanes = slice(g * 128, (g + 1) * 128)

        def body(j, sums):
            sums = list(sums)
            for i in range(8):
                weight = proj[i * 8 + j, :, lanes].astype(F32)
                for q in range(RHS):
                    line = sample_ref[q, j, i : i + 1, lanes]
                    sums[q] = sums[q] + weight * line
            return tuple(sums)

        sums = lax.fori_loop(0, 8, body, tuple(near_ref[q, :, lanes] for q in range(RHS)))
        for q in range(RHS):
            out_ref[q, :, lanes] = sums[q]


def turn_green(green, rows_ref, out_ref):
    for j1 in range(16):
        for h in range(2):
            rows_ref[h, pl.ds(j1, 32, stride=16), :] = green[
                :, j1 * 256 + h * 128 : j1 * 256 + (h + 1) * 128
            ]
    for h in range(2):
        for g in range(4):
            out_ref[h * 128 : (h + 1) * 128, g * 128 : (g + 1) * 128] = rows_ref[
                h, g * 128 : (g + 1) * 128, :
            ].T * (1.0 / 16777216)


def edge_stage(curf, edge_row, edge_col):
    lane = iota((16, 128), 1)
    place = lax.rem(lane, 16)

    def body(m, carry):
        q, at = m // 4, pl.ds(pl.multiple_of(lax.rem(m, 4) * 16, 16), 16)
        here = pl.ds(pl.multiple_of(m * 16, 16), 16)
        tiles = [curf[q, at, t * 128 : (t + 1) * 128] for t in range(4)]
        edge_row[here, :] = jnp.where(lane < 64, tiles[0], tiles[3]).astype(BF16)
        packed = jnp.zeros((16, 128), F32)
        for t in range(4):
            packed = jnp.where(place == t, pltpu.roll(tiles[t], (t - 15) % 128, 1), packed)
            packed = jnp.where(place == 4 + t, pltpu.roll(tiles[t], 4 + t, 1), packed)
        edge_col[here, :] = packed.astype(BF16)
        return carry

    lax.fori_loop(0, 8, body, 0)


def partner_stage(curf, partners, edges, picked):
    lane = iota((16, 128), 1)
    place = lax.rem(lane, 16)

    def body(m, carry):
        q, at = m // 4, pl.ds(pl.multiple_of(lax.rem(m, 4) * 16, 16), 16)
        here = pl.ds(pl.multiple_of(m * 16, 16), 16)
        near = lambda dr, dc: edges[edge_slot(dr, dc), here, :].astype(F32)
        middle = [near(-1, 0)]
        middle += [curf[q, at, t * 128 : (t + 1) * 128] for t in range(4)]
        middle += [near(1, 0)]
        left, right = near(0, -1), near(0, 1)
        from_right = [near(-1, 1), right, right, right, right, near(1, 1)]
        from_left = [near(-1, -1), left, left, left, left, near(1, -1)]
        columns = {0: middle, 1: [], -1: []}
        for e in range(6):
            inner = e in (1, 2, 3, 4)
            t = e - 1
            outside = pltpu.roll(from_right[e], (11 - t) % 128 if inner else 15, 1)
            columns[1].append(jnp.where(place == 15, outside, pltpu.roll(middle[e], 127, 1)))
            outside = pltpu.roll(from_left[e], (-t) % 128 if inner else 113, 1)
            columns[-1].append(jnp.where(place == 0, outside, pltpu.roll(middle[e], 1, 1)))
        for t in range(4):
            lanes = slice(t * 128, (t + 1) * 128)
            views = {}
            for dc in (-1, 0, 1):
                x = columns[dc]
                views[0, dc] = x[t + 1]
                views[1, dc] = pltpu.roll(jnp.where(lane < 16, x[t + 2], x[t + 1]), 112, 1)
                views[-1, dc] = pltpu.roll(jnp.where(lane >= 112, x[t], x[t + 1]), 16, 1)
            for k in range(1, NEIGH):
                code = jnp.broadcast_to(partners[k : k + 1, lanes], (16, 128))
                chosen = views[0, 0]
                for dr in (-1, 0, 1):
                    for dc in (-1, 0, 1):
                        if dr or dc:
                            chosen = jnp.where(code == 3 * (dr + 1) + dc + 1, views[dr, dc], chosen)
                picked[k - 1, q, at, lanes] = chosen
        return carry

    lax.fori_loop(0, 8, body, 0)


def near_stage(blocks, k, values, near_ref):
    def body(m, carry):
        a0 = pl.multiple_of((m // 4) * 8, 8)
        lanes = pl.ds(pl.multiple_of(lax.rem(m, 4) * 128, 128), 128)
        sums = [None] * 16
        for b in range(4):
            at = slice(16 * b, 16 * b + 16)
            current = [values[q, at, lanes] for q in range(RHS)]
            for a in range(8):
                weight = blocks[k, a0 + a, at, lanes].astype(F32)
                for q in range(RHS):
                    part = fold(weight * current[q])
                    old = sums[q * 8 + a]
                    sums[q * 8 + a] = part if old is None else old + part
        for q in range(RHS):
            tile = row_sums(sums[q * 8 : q * 8 + 8])
            if k > 0:
                tile = tile + near_ref[q, pl.ds(a0, 8), lanes]
            near_ref[q, pl.ds(a0, 8), lanes] = tile
        return carry

    lax.fori_loop(0, 32, body, 0)


AROUND = [(dr, dc) for dr in (-1, 0, 1) for dc in (-1, 0, 1) if dr or dc]


def edge_slot(dr, dc):
    return AROUND.index((dr, dc))


def hop_order():
    hop = lambda d: min(d, 4 - d)
    offsets = [
        (x, y, z, core) for x in range(4) for y in range(4) for z in range(4) for core in range(2)
    ][1:]
    return sorted(offsets, key=lambda o: -(hop(o[0]) + hop(o[1]) + hop(o[2])))


def slots_wait(ref, count, sem):
    part = ref.at[pl.ds(0, count)]
    pltpu.make_async_copy(part, part, sem).wait()


TABLES = 10


def main_kernel(*refs):
    cur_hbm, shifts_hbm, partners_hbm, proj_hbm, blocks_hbm, green_hbm = refs[:6]
    tables_hbm = refs[6 : 6 + TABLES]
    out_ref = refs[6 + TABLES]
    scratch = refs[7 + TABLES :]
    tables = scratch[:TABLES]
    place, pick, row_fwd, row_inv, col_fwd, col_inv, small, small_inv, twist_row, twist_col = tables
    (
        proj, blocks, green, rows_ref, left_ref, grid_ref, send1, recv1, halo1, slab_ref, mix_ref,
        flat_ref, send2, recv2, half_ref, wide_ref, green_rows, green_turned, send3, recv3, send4,
        recv4, tall_ref, pick_rows, sample_ref, curf, edge_row, edge_col, edges, picked, near_ref,
        cur, shifts, partners, ssem, rsem, hsem, lsem, esem_out, esem_in, psem, nsem, tsem, csem, entered,
    ) = scratch[TABLES:]
    r, c = lax.axis_index("row"), lax.axis_index("col")
    me = r * 16 + c
    core, y_low, z = c & 1, lax.shift_right_logical(c, 1) & 1, lax.shift_right_logical(c, 2)
    x, y = lax.shift_right_logical(r, 1), (r & 1) * 2 + y_low

    proj_copies = [
        pltpu.make_async_copy(
            proj_hbm.at[:, :, pl.ds(g * 128, 128)], proj.at[:, :, pl.ds(g * 128, 128)], psem.at[g]
        )
        for g in range(4)
    ]
    table_copies = [pltpu.make_async_copy(a, b, tsem.at[i]) for i, (a, b) in enumerate(zip(tables_hbm, tables))]
    green_copy = pltpu.make_async_copy(green_hbm, green, tsem.at[TABLES])
    block_copies = [pltpu.make_async_copy(blocks_hbm.at[k], blocks.at[k], nsem.at[k]) for k in range(NEIGH)]
    small_copies = [
        pltpu.make_async_copy(a, b, csem.at[i])
        for i, (a, b) in enumerate(((cur_hbm, cur), (shifts_hbm, shifts), (partners_hbm, partners)))
    ]
    for copy in small_copies + proj_copies:
        copy.start()
    table_copies[0].start()

    barrier = pltpu.get_barrier_semaphore()

    def greet_column(k, carry):
        pl.semaphore_signal(barrier, inc=1, device_id=(r, (c + k) & 15), device_id_type=MESH)
        return carry

    def greet_row(k, carry):
        pl.semaphore_signal(barrier, inc=1, device_id=((r + k) & 7, c), device_id_type=MESH)
        return carry

    lax.fori_loop(1, 8, greet_row, 0)
    lax.fori_loop(1, 16, greet_column, 0)
    zero = jnp.zeros((48, 128), BF16)
    recv4[0] = zero
    recv4[17] = zero
    for copy in small_copies:
        copy.wait()
    curf[...] = cur[...].astype(BF16).astype(F32)
    edge_stage(curf, edge_row, edge_col)
    stencil_stage(proj, curf, shifts, rows_ref, lambda g: proj_copies[g].wait())
    for copy in table_copies[1:]:
        copy.start()
    green_copy.start()
    for copy in block_copies:
        copy.start()
    pl.semaphore_wait(barrier, 22)

    def tell_column(k, carry):
        pl.semaphore_signal(entered, inc=1, device_id=(r, (c + k) & 15), device_id_type=MESH)
        return carry

    lax.fori_loop(1, 16, tell_column, 0)
    table_copies[0].wait()
    spread_stage(rows_ref, shifts, place, left_ref, grid_ref, send1)
    pl.semaphore_wait(entered, 15)

    def remote(source, target, send_sem, recv_sem, where):
        return pltpu.make_async_remote_copy(
            source, target, send_sem, recv_sem, device_id=where, device_id_type=MESH
        )

    def to_column(send, recv, slot, index):
        for dx, dy, dz, dcore in hop_order():
            if dx == 0 and dy < 2:
                d = ((z + dz) & 3) * 4 + (y_low ^ dy) * 2 + (core ^ dcore)
                remote(send.at[d], recv.at[slot], ssem.at[index], rsem.at[index], (r, d)).start()

    @pl.when(r > 0)
    def _():
        remote(send1.at[16], halo1.at[c], ssem.at[4], hsem.at[0], (r - 1, 15)).start()

    @pl.when(r < 7)
    def _():
        remote(send1.at[17], halo1.at[c], ssem.at[5], hsem.at[0], (r + 1, 0)).start()

    to_column(send1, recv1, c, 0)
    own = pltpu.make_async_copy(send1.at[c], recv1.at[c], lsem.at[0])
    own.start()

    def exists(dr, dc):
        there = None
        for move, at, last in ((dr, r, 7), (dc, c, 15)):
            test = at < last if move > 0 else at > 0
            if move:
                there = test if there is None else there & test
        return there

    def edge_copy(dr, dc):
        target = edge_slot(-dr, -dc)
        return remote(
            edge_row if dr else edge_col, edges.at[target], esem_out.at[edge_slot(dr, dc)],
            esem_in.at[target], (r + dr, c + dc),
        )

    for dr, dc in AROUND:
        @pl.when(exists(dr, dc))
        def _():
            edge_copy(dr, dc).start()

    green_copy.wait()
    turn_green(green, green_rows, green_turned)
    block_copies[0].wait()
    near_stage(blocks, 0, curf, near_ref)
    for copy in table_copies[1:]:
        copy.wait()
    own.wait()
    has_halo = ((c == 0) & (r > 0)) | ((c == 15) & (r < 7))
    slots_wait(recv1, 15, rsem.at[0])

    @pl.when(has_halo)
    def _():
        slots_wait(halo1, 16, hsem.at[0])

    row_forward_stage(recv1, halo1, has_halo, slab_ref, twist_row, row_fwd, mix_ref, flat_ref, send2)

    def to_all(send, recv, index):
        own = pltpu.make_async_copy(send.at[me], recv.at[me], lsem.at[index])
        own.start()
        for dx, dy, dz, dcore in hop_order():
            px, py, pz, pcore = (x + dx) & 3, (y + dy) & 3, (z + dz) & 3, core ^ dcore
            row = px * 2 + lax.shift_right_logical(py, 1)
            col = pz * 4 + (py & 1) * 2 + pcore
            remote(send.at[row * 16 + col], recv.at[me], ssem.at[index], rsem.at[index], (row, col)).start()
        return own

    own = to_all(send2, recv2, 1)
    for dr, dc in AROUND:
        @pl.when(exists(dr, dc))
        def _():
            back = edges.at[edge_slot(dr, dc)]
            pltpu.make_async_copy(back, back, esem_in.at[edge_slot(dr, dc)]).wait()

    partner_stage(curf, partners, edges, picked)
    for k in (1, 2):
        block_copies[k].wait()
        near_stage(blocks, k, picked.at[k - 1], near_ref)
    own.wait()
    slots_wait(recv2, 127, rsem.at[1])
    column_stage(
        recv2, flat_ref, half_ref, col_fwd, col_inv, small, small_inv, twist_col, green_turned, wide_ref, send3
    )
    own = to_all(send3, recv3, 2)
    block_copies[3].wait()
    near_stage(blocks, 3, picked.at[2], near_ref)
    own.wait()
    slots_wait(recv3, 127, rsem.at[2])
    row_inverse_stage(recv3, flat_ref, half_ref, row_inv, twist_row, mix_ref, slab_ref, send4)

    def to_neighbour_row(target, slot, index, sem):
        def go(d, carry):
            remote(send4.at[d], recv4.at[slot], ssem.at[index], hsem.at[sem], (target, d)).start()
            return carry

        lax.fori_loop(0, 16, go, 0)

    up = (c == 0) & (r > 0)
    down = (c == 15) & (r < 7)

    @pl.when(up)
    def _():
        to_neighbour_row(r - 1, 17, 6, 1)

    @pl.when(down)
    def _():
        to_neighbour_row(r + 1, 0, 7, 2)

    to_column(send4, recv4, c + 1, 3)
    own = pltpu.make_async_copy(send4.at[c], recv4.at[c + 1], lsem.at[3])
    own.start()
    own.wait()
    slots_wait(recv4, 15, rsem.at[3])

    @pl.when(r < 7)
    def _():
        slots_wait(recv4, 1, hsem.at[1])

    @pl.when(r > 0)
    def _():
        slots_wait(recv4, 1, hsem.at[2])

    sample_stage(recv4, pick, shifts, tall_ref, pick_rows, sample_ref)
    far_stage(proj, sample_ref, near_ref, out_ref)

    slots_wait(send1, 15, ssem.at[0])

    @pl.when(r > 0)
    def _():
        slots_wait(send1, 1, ssem.at[4])

    @pl.when(r < 7)
    def _():
        slots_wait(send1, 1, ssem.at[5])

    for dr, dc in AROUND:
        @pl.when(exists(dr, dc))
        def _():
            pltpu.make_async_copy(edge_row, edge_row, esem_out.at[edge_slot(dr, dc)]).wait()

    slots_wait(send2, 127, ssem.at[1])
    slots_wait(send3, 127, ssem.at[2])
    slots_wait(send4, 15, ssem.at[3])

    @pl.when(up)
    def _():
        slots_wait(send4, 16, ssem.at[6])

    @pl.when(down)
    def _():
        slots_wait(send4, 16, ssem.at[7])


def shards(currents, projection, near_blocks, partners, shifts, green):
    tables = [jnp.asarray(t) for t in make_tables()]
    vmem = pl.BlockSpec(memory_space=pltpu.VMEM)
    hbm = pl.BlockSpec(memory_space=pltpu.HBM)
    dma = pltpu.SemaphoreType.DMA
    return pl.pallas_call(
        main_kernel,
        out_shape=pltpu.VMEM((RHS, BASIS, ER * EC), F32),
        in_specs=[hbm] * (6 + len(tables)),
        out_specs=vmem,
        scratch_shapes=[pltpu.VMEM(t.shape, t.dtype) for t in tables]
        + [
            pltpu.VMEM((64, BASIS, 512), BF16),
            pltpu.VMEM((NEIGH, BASIS, BASIS, 512), BF16),
            pltpu.VMEM((32, 4096), F32),
            pltpu.VMEM((RHS, 2, 8, 8, 512), F32),
            pltpu.VMEM((256, 1536), BF16),
            pltpu.VMEM((RHS, 2, 272, 256), F32),
            pltpu.VMEM((18, 48, 128), BF16),
            pltpu.VMEM((16, 48, 128), BF16),
            pltpu.VMEM((16, 48, 128), BF16),
            pltpu.VMEM((16, 48, 128), F32),
            pltpu.VMEM((512, 256), F32),
            pltpu.VMEM((1024, 128), F32),
            pltpu.VMEM((128, 8, 128), BF16),
            pltpu.VMEM((128, 8, 128), BF16),
            pltpu.VMEM((256, 512), BF16),
            pltpu.VMEM((512, 512), F32),
            pltpu.VMEM((2, 512, 128), F32),
            pltpu.VMEM((256, 512), F32),
            pltpu.VMEM((128, 8, 128), BF16),
            pltpu.VMEM((128, 8, 128), BF16),
            pltpu.VMEM((16, 48, 128), BF16),
            pltpu.VMEM((18, 48, 128), BF16),
            pltpu.VMEM((288, 1536), F32),
            pltpu.VMEM((12, 8, 128), F32),
            pltpu.VMEM((RHS, 8, 8, 512), F32),
            pltpu.VMEM((RHS, BASIS, 512), F32),
            pltpu.VMEM((128, 128), BF16),
            pltpu.VMEM((128, 128), BF16),
            pltpu.VMEM((8, 128, 128), BF16),
            pltpu.VMEM((NEIGH - 1, RHS, BASIS, 512), F32),
            pltpu.VMEM((RHS, BASIS, 512), F32),
            pltpu.VMEM((RHS, BASIS, 512), F32),
            pltpu.VMEM((2, 512), jnp.int32),
            pltpu.VMEM((NEIGH, 512), jnp.int32),
            dma((8,)),
            dma((4,)),
            dma((3,)),
            dma((4,)),
            dma((8,)),
            dma((8,)),
            dma((4,)),
            dma((NEIGH,)),
            dma((len(tables) + 1,)),
            dma((3,)),
            pltpu.SemaphoreType.REGULAR,
        ],
        compiler_params=pltpu.CompilerParams(
            collective_id=0, has_side_effects=True, vmem_limit_bytes=int(60 * 2**20)
        ),
    )(currents, shifts, partners, projection, near_blocks, green, *tables)


def solution(mesh):
    in_specs = (
        P(None, None, ("row", "col")),
        P(None, None, ("row", "col")),
        P(None, None, None, ("row", "col")),
        P(None, ("row", "col")),
        P(None, ("row", "col")),
        P(("row", "col"), None),
    )
    out_specs = P(None, None, ("row", "col"))
    return jax.shard_map(shards, mesh=mesh, in_specs=in_specs, out_specs=out_specs, check_vma=False)
```

```python
import functools
import math

import jax
import jax.numpy as jnp
import ml_dtypes
import numpy as np
from jax import lax
from jax.experimental import pallas as pl
from jax.experimental.pallas import tpu as pltpu
from jax.sharding import PartitionSpec as P

MESH = pl.DeviceIdType.MESH
F32 = jnp.float32
BF16 = jnp.bfloat16
BASIS = 64
ER = 32
EC = 16
NEIGH = 4
RHS = 2
OFFSETS = (-2, -1, 1, 2)
EDGE_SLOT = {0: 8, 1: 9, 6: 10, 7: 11}


def halves(table):
    high = np.asarray(table, np.float64).astype(ml_dtypes.bfloat16)
    low = (table - high.astype(np.float64)).astype(ml_dtypes.bfloat16)
    return np.stack([high, low])


def make_tables():
    turn = lambda rows, cols, modulus: (
        2.0 * np.pi * ((np.arange(rows)[:, None] * np.arange(cols)[None, :]) % modulus) / modulus
    )
    place = np.zeros((12, 8, 16, 256))
    for ec in range(16):
        for j in range(8):
            place[j, :, ec, 8 * ec + j] = 1
        for j in (0, 1):
            if ec < 15:
                place[EDGE_SLOT[j], :, ec, 8 * (ec + 1) + j] = 1
            else:
                place[EDGE_SLOT[j], :, ec, 128 + j] = 1
                place[EDGE_SLOT[j], :, ec, 128 + 2 + j] = 1
        for j in (6, 7):
            if ec > 0:
                place[EDGE_SLOT[j], :, ec, 8 * (ec - 1) + j] = 1
            else:
                place[EDGE_SLOT[j], :, ec, 128 + 120 + j] = 1
                place[EDGE_SLOT[j], :, ec, 128 + 118 + j] = 1
    place = place.reshape(1536, 256)
    pick = np.stack([place.T, place.T])
    real_lanes = [128 + 0, 128 + 1, 128 + 126, 128 + 127]
    imag_lanes = [128 + 2, 128 + 3, 128 + 124, 128 + 125]
    pick[0, imag_lanes] = 0
    pick[1, real_lanes] = 0
    a = turn(128, 128, 128)
    row_fwd = np.block([[np.cos(a), np.sin(a)], [-np.sin(a), np.cos(a)]])
    row_inv = np.block([[np.cos(a), np.sin(a)], [-np.sin(a), np.cos(a)]])
    b = turn(256, 128, 256)
    col_fwd = np.block([[np.cos(b), np.sin(b)], [-np.sin(b), np.cos(b)]])
    col_inv = col_fwd.T
    c = turn(16, 16, 16)
    eye = np.eye(8)
    kc, ks = np.kron(eye, np.cos(c)), np.kron(eye, np.sin(c))
    small_fwd = np.block([[kc, -ks], [ks, kc]])
    small_inv = small_fwd.T
    t1 = turn(32, 128, 4096)
    twist_row = np.stack([np.cos(t1), np.sin(t1)])
    t2 = np.tile(turn(256, 16, 4096), (1, 8))
    twist_col = np.stack([np.cos(t2), np.sin(t2)])
    half = ml_dtypes.bfloat16
    return (
        place.astype(half),
        pick.astype(half),
        halves(row_fwd),
        halves(row_inv),
        halves(col_fwd),
        halves(col_inv),
        halves(small_fwd),
        halves(small_inv),
        twist_row.astype(np.float32),
        twist_col.astype(np.float32),
    )


def dot(a, b, dims=((1,), (0,))):
    return lax.dot_general(a, b, (dims, ((), ())), preferred_element_type=F32)


def split(x):
    high = x.astype(BF16)
    return high, (x - high.astype(F32)).astype(BF16)


def cadd(a, b):
    return (a[0] + b[0], a[1] + b[1])


def csub(a, b):
    return (a[0] - b[0], a[1] - b[1])


def cmulc(a, angle):
    turns = angle / (2 * math.pi)
    quarter = round(turns * 4)
    if abs(turns * 4 - quarter) < 1e-9:
        quarter %= 4
        if quarter == 0:
            return a
        if quarter == 1:
            return (-a[1], a[0])
        if quarter == 2:
            return (-a[0], -a[1])
        return (a[1], -a[0])
    c, s = math.cos(angle), math.sin(angle)
    return (a[0] * c - a[1] * s, a[0] * s + a[1] * c)


def fft(items, sign):
    n = len(items)
    if n == 1:
        return items
    even = fft(items[0::2], sign)
    odd = fft(items[1::2], sign)
    out = [None] * n
    for k in range(n // 2):
        t = cmulc(odd[k], sign * 2 * math.pi * k / n)
        out[k] = cadd(even[k], t)
        out[k + n // 2] = csub(even[k], t)
    return out


def iota(shape, dim):
    return lax.broadcasted_iota(jnp.int32, shape, dim)


def row_sums(tiles):
    sub = iota((8, 128), 0)
    top = sub < 4
    tiles = [
        jnp.where(top, tiles[i], tiles[i + 4])
        + pltpu.roll(jnp.where(top, tiles[i + 4], tiles[i]), 4, 0)
        for i in range(4)
    ]
    for step in (2, 1):
        upper = lax.rem(sub, 2 * step) < step
        tiles = [
            jnp.where(
                upper,
                tiles[i] + pltpu.roll(tiles[i], 8 - step, 0),
                tiles[i + step] + pltpu.roll(tiles[i + step], step, 0),
            )
            for i in range(step)
        ]
    return tiles[0]


def fold(x):
    total = x[0:8]
    for b in range(1, x.shape[0] // 8):
        total = total + x[8 * b : 8 * b + 8]
    return total


def stencil_stage(proj, curf, shifts, rows_ref, ready):
    sub = iota((8, 128), 0)
    for g in range(4):
        lanes = slice(g * 128, (g + 1) * 128)
        dr = jnp.broadcast_to(shifts[0:1, lanes], (8, 128))
        home = (sub - dr >= 0) & (sub - dr < 8)
        cur = [curf[q, :, lanes] for q in range(RHS)]

        ready(g)

        def body(j, carry):
            parts = [[] for _ in range(RHS)]
            for i in range(8):
                weight = proj[i * 8 + j, :, lanes].astype(F32)
                for q in range(RHS):
                    parts[q].append(fold(weight * cur[q]))
            tiles = [row_sums(part) for part in parts]
            for q in range(RHS):
                moved = tiles[q]
                for o in OFFSETS:
                    moved = jnp.where(dr == o, pltpu.roll(tiles[q], o % 8, 0), moved)
                rows_ref[q, 0, j, :, lanes] = jnp.where(home, moved, 0.0)
                rows_ref[q, 1, j, :, lanes] = jnp.where(home, 0.0, moved)
            return carry

        lax.fori_loop(0, 8, body, 0, unroll=2)


def spread_stage(rows_ref, shifts, place, left_ref, grid_ref, send_ref):
    sub = iota((64, 128), 0)
    lane = iota((64, 128), 1)
    own = jnp.where((sub // 8) == (lane // 16), 1.0, 0.0).astype(BF16)
    for g in range(4):
        lanes = slice(g * 128, (g + 1) * 128)
        dc = jnp.broadcast_to(shifts[1:2, lanes], (8, 128))
        is_offset = {o: dc == o for o in OFFSETS}

        def body(idx, carry):
            q, kind = idx // 2, lax.rem(idx, 2)
            tiles = [rows_ref[q, kind, j, :, lanes] for j in range(8)]
            for j in range(8):
                moved = tiles[j]
                for o in OFFSETS:
                    moved = jnp.where(is_offset[o], tiles[(j - o) % 8], moved)
                home = (j - dc >= 0) & (j - dc < 8)
                pieces = [(j, jnp.where(home, moved, 0.0))]
                if j in EDGE_SLOT:
                    pieces.append((EDGE_SLOT[j], jnp.where(home, 0.0, moved)))
                for slot, piece in pieces:
                    pair = jnp.concatenate([piece] * 2, axis=0).astype(BF16)
                    left_ref[pl.ds(pl.multiple_of(idx * 64, 64), 64), slot * 128 : (slot + 1) * 128] = (
                        jnp.concatenate([pair] * 4, axis=0) * own
                    )
            return carry

        lax.fori_loop(0, 4, body, 0, unroll=4)
        product = dot(left_ref[...], place[...])
        for q in range(RHS):
            for kind in range(2):
                base = (q * 2 + kind) * 64
                grid_ref[q, kind, 8 + g * 64 : 8 + (g + 1) * 64, :] = product[base : base + 64]
    zero8 = jnp.zeros((8, 256), F32)
    for q in range(RHS):
        grid_ref[q, 1, 0:8, :] = zero8
        grid_ref[q, 1, 264:272, :] = zero8
    sub = lax.rem(iota((16, 256), 0), 8)
    lane1 = iota((16, 128), 1)
    real_rim = (lane1 < 2) | (lane1 >= 126)
    imag_rim = ((lane1 >= 2) & (lane1 < 4)) | ((lane1 >= 124) & (lane1 < 126))

    def message(parts):
        rim = jnp.where(real_rim, parts[0][:, 128:], jnp.where(imag_rim, parts[1][:, 128:], 0.0))
        return jnp.concatenate([parts[0][:, :128], parts[1][:, :128], rim], axis=0).astype(BF16)

    def slab(k, carry):
        parts = []
        for q in range(RHS):
            at = lambda shift: pl.ds(pl.multiple_of(k * 16 + shift, 8), 16)
            total = grid_ref[q, 0, at(8), :]
            total = total + jnp.where(sub >= 6, grid_ref[q, 1, at(16), :], 0.0)
            total = total + jnp.where(sub < 2, grid_ref[q, 1, at(0), :], 0.0)
            parts.append(total)
        send_ref[k] = message(parts)
        return carry

    lax.fori_loop(0, 16, slab, 0)
    full = iota((16, 256), 0)
    send_ref[16] = message(
        [jnp.where(full >= 14, grid_ref[q, 1, 0:16, :], 0.0) for q in range(RHS)]
    )
    send_ref[17] = message(
        [jnp.where(full < 2, grid_ref[q, 1, 256:272, :], 0.0) for q in range(RHS)]
    )


def row_forward_stage(recv, halo, has_halo, slab_ref, twist, table, mix_ref, flat_ref, out_ref):
    def widen(c, carry):
        slab_ref[c] = recv[c].astype(F32)
        return carry

    lax.fori_loop(0, 16, widen, 0)

    @pl.when(has_halo)
    def _():
        def add(c, carry):
            slab_ref[c] = slab_ref[c] + halo[c].astype(F32)
            return carry

        lax.fori_loop(0, 16, add, 0)

    lane = iota((8, 128), 1)

    def rows(h, carry):
        at = lambda start: pl.ds(pl.multiple_of(start + h * 8, 8), 8)
        rims = [slab_ref[c, at(32), :] for c in range(16)]
        items = []
        for c in range(16):
            real = slab_ref[c, at(0), :]
            imag = slab_ref[c, at(16), :]
            if c > 0:
                real = real + jnp.where(lane < 2, rims[c - 1], 0.0)
                imag = imag + jnp.where(lane < 2, pltpu.roll(rims[c - 1], 126, 1), 0.0)
            if c < 15:
                real = real + jnp.where(lane >= 126, rims[c + 1], 0.0)
                imag = imag + jnp.where(lane >= 126, pltpu.roll(rims[c + 1], 2, 1), 0.0)
            items.append((real, imag))
        even = fft(items, -1)
        odd = fft([cmulc(v, -2 * math.pi * c / 32) for c, v in enumerate(items)], -1)
        for m in range(16):
            for p, (real, imag) in enumerate((even[m], odd[m])):
                k0 = 2 * m + p
                cos, sin = twist[0, k0 : k0 + 1, :], twist[1, k0 : k0 + 1, :]
                mix_ref[at(k0 * 16), 0:128] = real * cos + imag * sin
                mix_ref[at(k0 * 16), 128:256] = imag * cos - real * sin
        return carry

    lax.fori_loop(0, 2, rows, 0)
    high, low = split(mix_ref[...])
    nt = ((1,), (1,))
    out = dot(table[0], high, nt) + dot(table[1], high, nt) + dot(table[0], low, nt)
    to_messages(out, flat_ref, out_ref)


def to_messages(out, flat_ref, out_ref):
    for ri in range(2):
        for g in range(4):
            flat_ref[pl.ds(ri * 4 + g, 128, stride=8), :] = out[
                ri * 128 : (ri + 1) * 128, g * 128 : (g + 1) * 128
            ]
    out_ref[...] = flat_ref[...].reshape(128, 8, 128).astype(BF16)


def from_messages(recv, flat_ref, half_ref):
    flat_ref[...] = recv[...].astype(F32).reshape(1024, 128)
    for ri in range(2):
        for g in range(4):
            half_ref[ri * 128 : (ri + 1) * 128, g * 128 : (g + 1) * 128] = flat_ref[
                pl.ds(ri * 4 + g, 128, stride=8), :
            ].astype(BF16)


def column_stage(recv, flat_ref, half_ref, fwd, inv, small, small_inv, twist, green, wide_ref, out_ref):
    from_messages(recv, flat_ref, half_ref)
    block = half_ref[...]
    wide_ref[...] = dot(fwd[0], block) + dot(fwd[1], block)
    cos, sin = twist[0], twist[1]
    for g in range(4):
        lanes = slice(g * 128, (g + 1) * 128)
        real, imag = wide_ref[0:256, lanes], wide_ref[256:512, lanes]
        turned = jnp.concatenate([real * cos + imag * sin, imag * cos - real * sin], axis=1)
        high, low = split(turned)
        spec = dot(high, small[0]) + dot(low, small[0])
        scale = green[:, lanes]
        spec = spec * jnp.concatenate([scale, scale], axis=1)
        high, low = split(spec)
        back = dot(high, small_inv[0]) + dot(low, small_inv[0])
        real, imag = back[:, 0:128], back[:, 128:256]
        wide_ref[0:256, lanes] = real * cos - imag * sin
        wide_ref[256:512, lanes] = imag * cos + real * sin
    high, low = split(wide_ref[...])
    out = dot(inv[0], high) + dot(inv[0], low)
    to_messages(out, flat_ref, out_ref)


def row_inverse_stage(recv, flat_ref, half_ref, table, twist, mix_ref, slab_ref, send_ref):
    from_messages(recv, flat_ref, half_ref)
    turned = half_ref[...].T
    mix_ref[...] = dot(turned, table[0]) + dot(turned, table[1])

    def rows(h, carry):
        at = lambda start: pl.ds(pl.multiple_of(start + h * 8, 8), 8)
        items = []
        for k0 in range(32):
            cos, sin = twist[0, k0 : k0 + 1, :], twist[1, k0 : k0 + 1, :]
            real, imag = mix_ref[at(k0 * 16), 0:128], mix_ref[at(k0 * 16), 128:256]
            items.append((real * cos - imag * sin, imag * cos + real * sin))
        even = fft(items[0::2], 1)
        odd = fft(items[1::2], 1)
        for c in range(16):
            real, imag = cadd(even[c], cmulc(odd[c], 2 * math.pi * c / 32))
            slab_ref[c, at(0), :] = real
            slab_ref[c, at(16), :] = imag
        return carry

    lax.fori_loop(0, 2, rows, 0)
    lane = iota((16, 128), 1)
    for c in range(16):
        rim = jnp.zeros((16, 128), F32)
        if c < 15:
            rim = jnp.where(lane < 2, slab_ref[c + 1, 0:16, :], rim)
            rim = jnp.where((lane >= 2) & (lane < 4), pltpu.roll(slab_ref[c + 1, 16:32, :], 2, 1), rim)
        if c > 0:
            rim = jnp.where(lane >= 126, slab_ref[c - 1, 0:16, :], rim)
            rim = jnp.where(
                (lane >= 124) & (lane < 126), pltpu.roll(slab_ref[c - 1, 16:32, :], 126, 1), rim
            )
        send_ref[c] = jnp.concatenate([slab_ref[c, 0:32, :], rim], axis=0).astype(BF16)


def sample_stage(recv, pick, shifts, tall_ref, rows_ref, sample_ref):
    sub = iota((8, 128), 0)
    lane = iota((8, 128), 1)
    owns = [(lane // 16) == e for e in range(8)]
    for q in range(RHS):
        main = recv[:, q * 16 : (q + 1) * 16, :].reshape(288, 128)
        rim = recv[:, 32:48, :].reshape(288, 128)
        tall_ref[...] = dot(jnp.concatenate([main, rim], axis=1), pick[q])
        for g in range(4):
            lanes = slice(g * 128, (g + 1) * 128)
            dr = jnp.broadcast_to(shifts[0:1, lanes], (8, 128))
            dc = jnp.broadcast_to(shifts[1:2, lanes], (8, 128))

            def body(slot, carry):
                column = pl.ds(pl.multiple_of(slot * 128, 128), 128)
                tiles = [
                    tall_ref[8 + 64 * g + 8 * t : 16 + 64 * g + 8 * t, column] for t in range(10)
                ]
                home = tiles[1]
                edge = jnp.where(sub < 4, tiles[2], tiles[0])
                for e in range(1, 8):
                    home = jnp.where(owns[e], tiles[e + 1], home)
                    edge = jnp.where(owns[e], jnp.where(sub < 4, tiles[e + 2], tiles[e]), edge)
                moved = home
                for o in OFFSETS:
                    kept = (sub >= o) if o > 0 else (sub < 8 + o)
                    shifted = pltpu.roll(jnp.where(kept, home, edge), (-o) % 8, 0)
                    moved = jnp.where(dr == o, shifted, moved)
                rows_ref[slot] = moved
                return carry

            lax.fori_loop(0, 12, body, 0, unroll=4)
            line = lambda j: rows_ref[j] if 0 <= j < 8 else rows_ref[EDGE_SLOT[j % 8]]
            for j in range(8):
                moved = line(j)
                for o in OFFSETS:
                    moved = jnp.where(dc == o, line(j + o), moved)
                sample_ref[q, j, :, lanes] = moved


def far_stage(proj, sample_ref, near_ref, out_ref):
    for g in range(4):
        lanes = slice(g * 128, (g + 1) * 128)

        def body(j, sums):
            sums = list(sums)
            for i in range(8):
                weight = proj[i * 8 + j, :, lanes].astype(F32)
                for q in range(RHS):
                    line = sample_ref[q, j, i : i + 1, lanes]
                    sums[q] = sums[q] + weight * line
            return tuple(sums)

        sums = lax.fori_loop(0, 8, body, tuple(near_ref[q, :, lanes] for q in range(RHS)), unroll=2)
        for q in range(RHS):
            out_ref[q, :, lanes] = sums[q]


def turn_green(green, rows_ref, out_ref):
    for j1 in range(16):
        for h in range(2):
            rows_ref[h, pl.ds(j1, 32, stride=16), :] = green[
                :, j1 * 256 + h * 128 : j1 * 256 + (h + 1) * 128
            ]
    for h in range(2):
        for g in range(4):
            out_ref[h * 128 : (h + 1) * 128, g * 128 : (g + 1) * 128] = rows_ref[
                h, g * 128 : (g + 1) * 128, :
            ].T * (1.0 / 16777216)


def edge_stage(curf, edge_row, edge_col):
    lane = iota((16, 128), 1)
    place = lax.rem(lane, 16)

    def body(m, carry):
        q, at = m // 4, pl.ds(pl.multiple_of(lax.rem(m, 4) * 16, 16), 16)
        here = pl.ds(pl.multiple_of(m * 16, 16), 16)
        tiles = [curf[q, at, t * 128 : (t + 1) * 128] for t in range(4)]
        edge_row[here, :] = jnp.where(lane < 64, tiles[0], tiles[3]).astype(BF16)
        packed = jnp.zeros((16, 128), F32)
        for t in range(4):
            packed = jnp.where(place == t, pltpu.roll(tiles[t], (t - 15) % 128, 1), packed)
            packed = jnp.where(place == 4 + t, pltpu.roll(tiles[t], 4 + t, 1), packed)
        edge_col[here, :] = packed.astype(BF16)
        return carry

    lax.fori_loop(0, 8, body, 0)


def partner_stage(curf, partners, edges, picked):
    lane = iota((16, 128), 1)
    place = lax.rem(lane, 16)

    def body(m, carry):
        q, at = m // 4, pl.ds(pl.multiple_of(lax.rem(m, 4) * 16, 16), 16)
        here = pl.ds(pl.multiple_of(m * 16, 16), 16)
        near = lambda dr, dc: edges[edge_slot(dr, dc), here, :].astype(F32)
        middle = [near(-1, 0)]
        middle += [curf[q, at, t * 128 : (t + 1) * 128] for t in range(4)]
        middle += [near(1, 0)]
        left, right = near(0, -1), near(0, 1)
        from_right = [near(-1, 1), right, right, right, right, near(1, 1)]
        from_left = [near(-1, -1), left, left, left, left, near(1, -1)]
        columns = {0: middle, 1: [], -1: []}
        for e in range(6):
            inner = e in (1, 2, 3, 4)
            t = e - 1
            outside = pltpu.roll(from_right[e], (11 - t) % 128 if inner else 15, 1)
            columns[1].append(jnp.where(place == 15, outside, pltpu.roll(middle[e], 127, 1)))
            outside = pltpu.roll(from_left[e], (-t) % 128 if inner else 113, 1)
            columns[-1].append(jnp.where(place == 0, outside, pltpu.roll(middle[e], 1, 1)))
        for t in range(4):
            lanes = slice(t * 128, (t + 1) * 128)
            views = {}
            for dc in (-1, 0, 1):
                x = columns[dc]
                views[0, dc] = x[t + 1]
                views[1, dc] = pltpu.roll(jnp.where(lane < 16, x[t + 2], x[t + 1]), 112, 1)
                views[-1, dc] = pltpu.roll(jnp.where(lane >= 112, x[t], x[t + 1]), 16, 1)
            for k in range(1, NEIGH):
                code = jnp.broadcast_to(partners[k : k + 1, lanes], (16, 128))
                chosen = views[0, 0]
                for dr in (-1, 0, 1):
                    for dc in (-1, 0, 1):
                        if dr or dc:
                            chosen = jnp.where(code == 3 * (dr + 1) + dc + 1, views[dr, dc], chosen)
                picked[k - 1, q, at, lanes] = chosen
        return carry

    lax.fori_loop(0, 8, body, 0)


def near_stage(blocks, k, values, near_ref):
    def body(m, carry):
        a0 = pl.multiple_of((m // 4) * 8, 8)
        lanes = pl.ds(pl.multiple_of(lax.rem(m, 4) * 128, 128), 128)
        sums = [None] * 16
        for b in range(4):
            at = slice(16 * b, 16 * b + 16)
            current = [values[q, at, lanes] for q in range(RHS)]
            for a in range(8):
                weight = blocks[k, a0 + a, at, lanes].astype(F32)
                for q in range(RHS):
                    part = fold(weight * current[q])
                    old = sums[q * 8 + a]
                    sums[q * 8 + a] = part if old is None else old + part
        for q in range(RHS):
            tile = row_sums(sums[q * 8 : q * 8 + 8])
            if k > 0:
                tile = tile + near_ref[q, pl.ds(a0, 8), lanes]
            near_ref[q, pl.ds(a0, 8), lanes] = tile
        return carry

    lax.fori_loop(0, 32, body, 0)


AROUND = [(dr, dc) for dr in (-1, 0, 1) for dc in (-1, 0, 1) if dr or dc]


def edge_slot(dr, dc):
    return AROUND.index((dr, dc))


def hop_order():
    hop = lambda d: min(d, 4 - d)
    offsets = [
        (x, y, z, core) for x in range(4) for y in range(4) for z in range(4) for core in range(2)
    ][1:]
    return sorted(offsets, key=lambda o: -(hop(o[0]) + hop(o[1]) + hop(o[2])))


def slots_wait(ref, count, sem):
    part = ref.at[pl.ds(0, count)]
    pltpu.make_async_copy(part, part, sem).wait()


TABLES = 10


def main_kernel(*refs):
    cur_hbm, shifts_hbm, partners_hbm, proj_hbm, blocks_hbm, green_hbm = refs[:6]
    tables_hbm = refs[6 : 6 + TABLES]
    out_ref = refs[6 + TABLES]
    scratch = refs[7 + TABLES :]
    tables = scratch[:TABLES]
    place, pick, row_fwd, row_inv, col_fwd, col_inv, small, small_inv, twist_row, twist_col = tables
    (
        proj, blocks, green, rows_ref, left_ref, grid_ref, send1, recv1, halo1, slab_ref, mix_ref,
        flat_ref, send2, recv2, half_ref, wide_ref, green_rows, green_turned, send3, recv3, send4,
        recv4, tall_ref, pick_rows, sample_ref, curf, edge_row, edge_col, edges, picked, near_ref,
        cur, shifts, partners, ssem, rsem, hsem, lsem, esem_out, esem_in, psem, nsem, tsem, csem, entered,
    ) = scratch[TABLES:]
    r, c = lax.axis_index("row"), lax.axis_index("col")
    me = r * 16 + c
    core, y_low, z = c & 1, lax.shift_right_logical(c, 1) & 1, lax.shift_right_logical(c, 2)
    x, y = lax.shift_right_logical(r, 1), (r & 1) * 2 + y_low

    proj_copies = [
        pltpu.make_async_copy(
            proj_hbm.at[:, :, pl.ds(g * 128, 128)], proj.at[:, :, pl.ds(g * 128, 128)], psem.at[g]
        )
        for g in range(4)
    ]
    table_copies = [pltpu.make_async_copy(a, b, tsem.at[i]) for i, (a, b) in enumerate(zip(tables_hbm, tables))]
    green_copy = pltpu.make_async_copy(green_hbm, green, tsem.at[TABLES])
    block_copies = [pltpu.make_async_copy(blocks_hbm.at[k], blocks.at[k], nsem.at[k]) for k in range(NEIGH)]
    small_copies = [
        pltpu.make_async_copy(a, b, csem.at[i])
        for i, (a, b) in enumerate(((cur_hbm, cur), (shifts_hbm, shifts), (partners_hbm, partners)))
    ]
    for copy in small_copies + proj_copies:
        copy.start()
    table_copies[0].start()

    barrier = pltpu.get_barrier_semaphore()

    def greet_column(k, carry):
        pl.semaphore_signal(barrier, inc=1, device_id=(r, (c + k) & 15), device_id_type=MESH)
        return carry

    def greet_row(k, carry):
        pl.semaphore_signal(barrier, inc=1, device_id=((r + k) & 7, c), device_id_type=MESH)
        return carry

    lax.fori_loop(1, 8, greet_row, 0)
    lax.fori_loop(1, 16, greet_column, 0)
    zero = jnp.zeros((48, 128), BF16)
    recv4[0] = zero
    recv4[17] = zero
    for copy in small_copies:
        copy.wait()
    curf[...] = cur[...].astype(BF16).astype(F32)
    edge_stage(curf, edge_row, edge_col)
    stencil_stage(proj, curf, shifts, rows_ref, lambda g: proj_copies[g].wait())
    for copy in table_copies[1:]:
        copy.start()
    green_copy.start()
    for copy in block_copies:
        copy.start()
    pl.semaphore_wait(barrier, 22)

    def tell_column(k, carry):
        pl.semaphore_signal(entered, inc=1, device_id=(r, (c + k) & 15), device_id_type=MESH)
        return carry

    lax.fori_loop(1, 16, tell_column, 0)
    table_copies[0].wait()
    spread_stage(rows_ref, shifts, place, left_ref, grid_ref, send1)
    pl.semaphore_wait(entered, 15)

    def remote(source, target, send_sem, recv_sem, where):
        return pltpu.make_async_remote_copy(
            source, target, send_sem, recv_sem, device_id=where, device_id_type=MESH
        )

    def to_column(send, recv, slot, index):
        for dx, dy, dz, dcore in hop_order():
            if dx == 0 and dy < 2:
                d = ((z + dz) & 3) * 4 + (y_low ^ dy) * 2 + (core ^ dcore)
                remote(send.at[d], recv.at[slot], ssem.at[index], rsem.at[index], (r, d)).start()

    @pl.when(r > 0)
    def _():
        remote(send1.at[16], halo1.at[c], ssem.at[4], hsem.at[0], (r - 1, 15)).start()

    @pl.when(r < 7)
    def _():
        remote(send1.at[17], halo1.at[c], ssem.at[5], hsem.at[0], (r + 1, 0)).start()

    to_column(send1, recv1, c, 0)
    own = pltpu.make_async_copy(send1.at[c], recv1.at[c], lsem.at[0])
    own.start()

    def exists(dr, dc):
        there = None
        for move, at, last in ((dr, r, 7), (dc, c, 15)):
            test = at < last if move > 0 else at > 0
            if move:
                there = test if there is None else there & test
        return there

    def edge_copy(dr, dc):
        target = edge_slot(-dr, -dc)
        return remote(
            edge_row if dr else edge_col, edges.at[target], esem_out.at[edge_slot(dr, dc)],
            esem_in.at[target], (r + dr, c + dc),
        )

    for dr, dc in AROUND:
        @pl.when(exists(dr, dc))
        def _():
            edge_copy(dr, dc).start()

    green_copy.wait()
    turn_green(green, green_rows, green_turned)
    block_copies[0].wait()
    near_stage(blocks, 0, curf, near_ref)
    for copy in table_copies[1:]:
        copy.wait()
    own.wait()
    has_halo = ((c == 0) & (r > 0)) | ((c == 15) & (r < 7))
    slots_wait(recv1, 15, rsem.at[0])

    @pl.when(has_halo)
    def _():
        slots_wait(halo1, 16, hsem.at[0])

    row_forward_stage(recv1, halo1, has_halo, slab_ref, twist_row, row_fwd, mix_ref, flat_ref, send2)

    def to_all(send, recv, index):
        own = pltpu.make_async_copy(send.at[me], recv.at[me], lsem.at[index])
        own.start()
        for dx, dy, dz, dcore in hop_order():
            px, py, pz, pcore = (x + dx) & 3, (y + dy) & 3, (z + dz) & 3, core ^ dcore
            row = px * 2 + lax.shift_right_logical(py, 1)
            col = pz * 4 + (py & 1) * 2 + pcore
            remote(send.at[row * 16 + col], recv.at[me], ssem.at[index], rsem.at[index], (row, col)).start()
        return own

    own = to_all(send2, recv2, 1)
    for dr, dc in AROUND:
        @pl.when(exists(dr, dc))
        def _():
            back = edges.at[edge_slot(dr, dc)]
            pltpu.make_async_copy(back, back, esem_in.at[edge_slot(dr, dc)]).wait()

    partner_stage(curf, partners, edges, picked)
    block_copies[1].wait()
    near_stage(blocks, 1, picked.at[0], near_ref)
    own.wait()
    slots_wait(recv2, 127, rsem.at[1])
    column_stage(
        recv2, flat_ref, half_ref, col_fwd, col_inv, small, small_inv, twist_col, green_turned, wide_ref, send3
    )
    own = to_all(send3, recv3, 2)
    block_copies[2].wait()
    near_stage(blocks, 2, picked.at[1], near_ref)
    own.wait()
    slots_wait(recv3, 127, rsem.at[2])
    row_inverse_stage(recv3, flat_ref, half_ref, row_inv, twist_row, mix_ref, slab_ref, send4)

    def to_neighbour_row(target, slot, index, sem):
        def go(d, carry):
            remote(send4.at[d], recv4.at[slot], ssem.at[index], hsem.at[sem], (target, d)).start()
            return carry

        lax.fori_loop(0, 16, go, 0)

    up = (c == 0) & (r > 0)
    down = (c == 15) & (r < 7)

    @pl.when(up)
    def _():
        to_neighbour_row(r - 1, 17, 6, 1)

    @pl.when(down)
    def _():
        to_neighbour_row(r + 1, 0, 7, 2)

    to_column(send4, recv4, c + 1, 3)
    own = pltpu.make_async_copy(send4.at[c], recv4.at[c + 1], lsem.at[3])
    own.start()
    block_copies[3].wait()
    near_stage(blocks, 3, picked.at[2], near_ref)
    own.wait()
    slots_wait(recv4, 15, rsem.at[3])

    @pl.when(r < 7)
    def _():
        slots_wait(recv4, 1, hsem.at[1])

    @pl.when(r > 0)
    def _():
        slots_wait(recv4, 1, hsem.at[2])

    sample_stage(recv4, pick, shifts, tall_ref, pick_rows, sample_ref)
    far_stage(proj, sample_ref, near_ref, out_ref)

    slots_wait(send1, 15, ssem.at[0])

    @pl.when(r > 0)
    def _():
        slots_wait(send1, 1, ssem.at[4])

    @pl.when(r < 7)
    def _():
        slots_wait(send1, 1, ssem.at[5])

    for dr, dc in AROUND:
        @pl.when(exists(dr, dc))
        def _():
            pltpu.make_async_copy(edge_row, edge_row, esem_out.at[edge_slot(dr, dc)]).wait()

    slots_wait(send2, 127, ssem.at[1])
    slots_wait(send3, 127, ssem.at[2])
    slots_wait(send4, 15, ssem.at[3])

    @pl.when(up)
    def _():
        slots_wait(send4, 16, ssem.at[6])

    @pl.when(down)
    def _():
        slots_wait(send4, 16, ssem.at[7])


def shards(currents, projection, near_blocks, partners, shifts, green):
    tables = [jnp.asarray(t) for t in make_tables()]
    vmem = pl.BlockSpec(memory_space=pltpu.VMEM)
    hbm = pl.BlockSpec(memory_space=pltpu.HBM)
    dma = pltpu.SemaphoreType.DMA
    return pl.pallas_call(
        main_kernel,
        out_shape=pltpu.VMEM((RHS, BASIS, ER * EC), F32),
        in_specs=[hbm] * (6 + len(tables)),
        out_specs=vmem,
        scratch_shapes=[pltpu.VMEM(t.shape, t.dtype) for t in tables]
        + [
            pltpu.VMEM((64, BASIS, 512), BF16),
            pltpu.VMEM((NEIGH, BASIS, BASIS, 512), BF16),
            pltpu.VMEM((32, 4096), F32),
            pltpu.VMEM((RHS, 2, 8, 8, 512), F32),
            pltpu.VMEM((256, 1536), BF16),
            pltpu.VMEM((RHS, 2, 272, 256), F32),
            pltpu.VMEM((18, 48, 128), BF16),
            pltpu.VMEM((16, 48, 128), BF16),
            pltpu.VMEM((16, 48, 128), BF16),
            pltpu.VMEM((16, 48, 128), F32),
            pltpu.VMEM((512, 256), F32),
            pltpu.VMEM((1024, 128), F32),
            pltpu.VMEM((128, 8, 128), BF16),
            pltpu.VMEM((128, 8, 128), BF16),
            pltpu.VMEM((256, 512), BF16),
            pltpu.VMEM((512, 512), F32),
            pltpu.VMEM((2, 512, 128), F32),
            pltpu.VMEM((256, 512), F32),
            pltpu.VMEM((128, 8, 128), BF16),
            pltpu.VMEM((128, 8, 128), BF16),
            pltpu.VMEM((16, 48, 128), BF16),
            pltpu.VMEM((18, 48, 128), BF16),
            pltpu.VMEM((288, 1536), F32),
            pltpu.VMEM((12, 8, 128), F32),
            pltpu.VMEM((RHS, 8, 8, 512), F32),
            pltpu.VMEM((RHS, BASIS, 512), F32),
            pltpu.VMEM((128, 128), BF16),
            pltpu.VMEM((128, 128), BF16),
            pltpu.VMEM((8, 128, 128), BF16),
            pltpu.VMEM((NEIGH - 1, RHS, BASIS, 512), F32),
            pltpu.VMEM((RHS, BASIS, 512), F32),
            pltpu.VMEM((RHS, BASIS, 512), F32),
            pltpu.VMEM((2, 512), jnp.int32),
            pltpu.VMEM((NEIGH, 512), jnp.int32),
            dma((8,)),
            dma((4,)),
            dma((3,)),
            dma((4,)),
            dma((8,)),
            dma((8,)),
            dma((4,)),
            dma((NEIGH,)),
            dma((len(tables) + 1,)),
            dma((3,)),
            pltpu.SemaphoreType.REGULAR,
        ],
        compiler_params=pltpu.CompilerParams(
            collective_id=0, has_side_effects=True, vmem_limit_bytes=int(60 * 2**20)
        ),
    )(currents, shifts, partners, projection, near_blocks, green, *tables)


def solution(mesh):
    in_specs = (
        P(None, None, ("row", "col")),
        P(None, None, ("row", "col")),
        P(None, None, None, ("row", "col")),
        P(None, ("row", "col")),
        P(None, ("row", "col")),
        P(("row", "col"), None),
    )
    out_specs = P(None, None, ("row", "col"))
    return jax.shard_map(shards, mesh=mesh, in_specs=in_specs, out_specs=out_specs, check_vma=False)
```

```python
import functools
import math

import jax
import jax.numpy as jnp
import ml_dtypes
import numpy as np
from jax import lax
from jax.experimental import pallas as pl
from jax.experimental.pallas import tpu as pltpu
from jax.sharding import PartitionSpec as P

MESH = pl.DeviceIdType.MESH
F32 = jnp.float32
BF16 = jnp.bfloat16
BASIS = 64
ER = 32
EC = 16
NEIGH = 4
RHS = 2
OFFSETS = (-2, -1, 1, 2)
EDGE_SLOT = {0: 8, 1: 9, 6: 10, 7: 11}


def halves(table):
    high = np.asarray(table, np.float64).astype(ml_dtypes.bfloat16)
    low = (table - high.astype(np.float64)).astype(ml_dtypes.bfloat16)
    return np.stack([high, low])


def make_tables():
    turn = lambda rows, cols, modulus: (
        2.0 * np.pi * ((np.arange(rows)[:, None] * np.arange(cols)[None, :]) % modulus) / modulus
    )
    place = np.zeros((12, 8, 16, 256))
    for ec in range(16):
        for j in range(8):
            place[j, :, ec, 8 * ec + j] = 1
        for j in (0, 1):
            if ec < 15:
                place[EDGE_SLOT[j], :, ec, 8 * (ec + 1) + j] = 1
            else:
                place[EDGE_SLOT[j], :, ec, 128 + j] = 1
                place[EDGE_SLOT[j], :, ec, 128 + 2 + j] = 1
        for j in (6, 7):
            if ec > 0:
                place[EDGE_SLOT[j], :, ec, 8 * (ec - 1) + j] = 1
            else:
                place[EDGE_SLOT[j], :, ec, 128 + 120 + j] = 1
                place[EDGE_SLOT[j], :, ec, 128 + 118 + j] = 1
    place = place.reshape(1536, 256)
    pick = np.stack([place.T, place.T])
    real_lanes = [128 + 0, 128 + 1, 128 + 126, 128 + 127]
    imag_lanes = [128 + 2, 128 + 3, 128 + 124, 128 + 125]
    pick[0, imag_lanes] = 0
    pick[1, real_lanes] = 0
    a = turn(128, 128, 128)
    row_fwd = np.block([[np.cos(a), np.sin(a)], [-np.sin(a), np.cos(a)]])
    row_inv = np.block([[np.cos(a), np.sin(a)], [-np.sin(a), np.cos(a)]])
    b = turn(256, 128, 256)
    col_fwd = np.block([[np.cos(b), np.sin(b)], [-np.sin(b), np.cos(b)]])
    col_inv = col_fwd.T
    c = turn(16, 16, 16)
    eye = np.eye(8)
    kc, ks = np.kron(eye, np.cos(c)), np.kron(eye, np.sin(c))
    small_fwd = np.block([[kc, -ks], [ks, kc]])
    small_inv = small_fwd.T
    t1 = turn(32, 128, 4096)
    twist_row = np.stack([np.cos(t1), np.sin(t1)])
    t2 = np.tile(turn(256, 16, 4096), (1, 8))
    twist_col = np.stack([np.cos(t2), np.sin(t2)])
    half = ml_dtypes.bfloat16
    return (
        place.astype(half),
        pick.astype(half),
        halves(row_fwd),
        halves(row_inv),
        halves(col_fwd),
        halves(col_inv),
        halves(small_fwd),
        halves(small_inv),
        twist_row.astype(np.float32),
        twist_col.astype(np.float32),
    )


def dot(a, b, dims=((1,), (0,))):
    return lax.dot_general(a, b, (dims, ((), ())), preferred_element_type=F32)


def split(x):
    high = x.astype(BF16)
    return high, (x - high.astype(F32)).astype(BF16)


def cadd(a, b):
    return (a[0] + b[0], a[1] + b[1])


def csub(a, b):
    return (a[0] - b[0], a[1] - b[1])


def cmulc(a, angle):
    turns = angle / (2 * math.pi)
    quarter = round(turns * 4)
    if abs(turns * 4 - quarter) < 1e-9:
        quarter %= 4
        if quarter == 0:
            return a
        if quarter == 1:
            return (-a[1], a[0])
        if quarter == 2:
            return (-a[0], -a[1])
        return (a[1], -a[0])
    c, s = math.cos(angle), math.sin(angle)
    return (a[0] * c - a[1] * s, a[0] * s + a[1] * c)


def fft(items, sign):
    n = len(items)
    if n == 1:
        return items
    even = fft(items[0::2], sign)
    odd = fft(items[1::2], sign)
    out = [None] * n
    for k in range(n // 2):
        t = cmulc(odd[k], sign * 2 * math.pi * k / n)
        out[k] = cadd(even[k], t)
        out[k + n // 2] = csub(even[k], t)
    return out


def iota(shape, dim):
    return lax.broadcasted_iota(jnp.int32, shape, dim)


def row_sums(tiles):
    sub = iota((8, 128), 0)
    top = sub < 4
    tiles = [
        jnp.where(top, tiles[i], tiles[i + 4])
        + pltpu.roll(jnp.where(top, tiles[i + 4], tiles[i]), 4, 0)
        for i in range(4)
    ]
    for step in (2, 1):
        upper = lax.rem(sub, 2 * step) < step
        tiles = [
            jnp.where(
                upper,
                tiles[i] + pltpu.roll(tiles[i], 8 - step, 0),
                tiles[i + step] + pltpu.roll(tiles[i + step], step, 0),
            )
            for i in range(step)
        ]
    return tiles[0]


def fold(x):
    total = x[0:8]
    for b in range(1, x.shape[0] // 8):
        total = total + x[8 * b : 8 * b + 8]
    return total


def stencil_stage(proj, curf, shifts, rows_ref, ready):
    sub = iota((8, 128), 0)
    for g in range(4):
        lanes = slice(g * 128, (g + 1) * 128)
        dr = jnp.broadcast_to(shifts[0:1, lanes], (8, 128))
        home = (sub - dr >= 0) & (sub - dr < 8)
        cur = [curf[q, :, lanes] for q in range(RHS)]

        ready(g)

        def body(j, carry):
            parts = [[] for _ in range(RHS)]
            for i in range(8):
                weight = proj[i * 8 + j, :, lanes].astype(F32)
                for q in range(RHS):
                    parts[q].append(fold(weight * cur[q]))
            tiles = [row_sums(part) for part in parts]
            for q in range(RHS):
                moved = tiles[q]
                for o in OFFSETS:
                    moved = jnp.where(dr == o, pltpu.roll(tiles[q], o % 8, 0), moved)
                rows_ref[q, 0, j, :, lanes] = jnp.where(home, moved, 0.0)
                rows_ref[q, 1, j, :, lanes] = jnp.where(home, 0.0, moved)
            return carry

        lax.fori_loop(0, 8, body, 0, unroll=2)


def spread_stage(rows_ref, shifts, place, left_ref, grid_ref, send_ref):
    sub = iota((64, 128), 0)
    lane = iota((64, 128), 1)
    own = jnp.where((sub // 8) == (lane // 16), 1.0, 0.0).astype(BF16)
    for g in range(4):
        lanes = slice(g * 128, (g + 1) * 128)
        dc = jnp.broadcast_to(shifts[1:2, lanes], (8, 128))
        is_offset = {o: dc == o for o in OFFSETS}

        def body(idx, carry):
            q, kind = idx // 2, lax.rem(idx, 2)
            tiles = [rows_ref[q, kind, j, :, lanes] for j in range(8)]
            for j in range(8):
                moved = tiles[j]
                for o in OFFSETS:
                    moved = jnp.where(is_offset[o], tiles[(j - o) % 8], moved)
                home = (j - dc >= 0) & (j - dc < 8)
                pieces = [(j, jnp.where(home, moved, 0.0))]
                if j in EDGE_SLOT:
                    pieces.append((EDGE_SLOT[j], jnp.where(home, 0.0, moved)))
                for slot, piece in pieces:
                    pair = jnp.concatenate([piece] * 2, axis=0).astype(BF16)
                    left_ref[pl.ds(pl.multiple_of(idx * 64, 64), 64), slot * 128 : (slot + 1) * 128] = (
                        jnp.concatenate([pair] * 4, axis=0) * own
                    )
            return carry

        lax.fori_loop(0, 4, body, 0, unroll=4)
        product = dot(left_ref[...], place[...])
        for q in range(RHS):
            for kind in range(2):
                base = (q * 2 + kind) * 64
                grid_ref[q, kind, 8 + g * 64 : 8 + (g + 1) * 64, :] = product[base : base + 64]
    zero8 = jnp.zeros((8, 256), F32)
    for q in range(RHS):
        grid_ref[q, 1, 0:8, :] = zero8
        grid_ref[q, 1, 264:272, :] = zero8
    sub = lax.rem(iota((16, 256), 0), 8)
    lane1 = iota((16, 128), 1)
    real_rim = (lane1 < 2) | (lane1 >= 126)
    imag_rim = ((lane1 >= 2) & (lane1 < 4)) | ((lane1 >= 124) & (lane1 < 126))

    def message(parts):
        rim = jnp.where(real_rim, parts[0][:, 128:], jnp.where(imag_rim, parts[1][:, 128:], 0.0))
        return jnp.concatenate([parts[0][:, :128], parts[1][:, :128], rim], axis=0).astype(BF16)

    def slab(k, carry):
        parts = []
        for q in range(RHS):
            at = lambda shift: pl.ds(pl.multiple_of(k * 16 + shift, 8), 16)
            total = grid_ref[q, 0, at(8), :]
            total = total + jnp.where(sub >= 6, grid_ref[q, 1, at(16), :], 0.0)
            total = total + jnp.where(sub < 2, grid_ref[q, 1, at(0), :], 0.0)
            parts.append(total)
        send_ref[k] = message(parts)
        return carry

    lax.fori_loop(0, 16, slab, 0, unroll=4)
    full = iota((16, 256), 0)
    send_ref[16] = message(
        [jnp.where(full >= 14, grid_ref[q, 1, 0:16, :], 0.0) for q in range(RHS)]
    )
    send_ref[17] = message(
        [jnp.where(full < 2, grid_ref[q, 1, 256:272, :], 0.0) for q in range(RHS)]
    )


def row_forward_stage(recv, halo, has_halo, slab_ref, twist, table, mix_ref, flat_ref, out_ref):
    def widen(c, carry):
        slab_ref[c] = recv[c].astype(F32)
        return carry

    lax.fori_loop(0, 16, widen, 0, unroll=4)

    @pl.when(has_halo)
    def _():
        def add(c, carry):
            slab_ref[c] = slab_ref[c] + halo[c].astype(F32)
            return carry

        lax.fori_loop(0, 16, add, 0)

    lane = iota((8, 128), 1)

    def rows(h, carry):
        at = lambda start: pl.ds(pl.multiple_of(start + h * 8, 8), 8)
        rims = [slab_ref[c, at(32), :] for c in range(16)]
        items = []
        for c in range(16):
            real = slab_ref[c, at(0), :]
            imag = slab_ref[c, at(16), :]
            if c > 0:
                real = real + jnp.where(lane < 2, rims[c - 1], 0.0)
                imag = imag + jnp.where(lane < 2, pltpu.roll(rims[c - 1], 126, 1), 0.0)
            if c < 15:
                real = real + jnp.where(lane >= 126, rims[c + 1], 0.0)
                imag = imag + jnp.where(lane >= 126, pltpu.roll(rims[c + 1], 2, 1), 0.0)
            items.append((real, imag))
        even = fft(items, -1)
        odd = fft([cmulc(v, -2 * math.pi * c / 32) for c, v in enumerate(items)], -1)
        for m in range(16):
            for p, (real, imag) in enumerate((even[m], odd[m])):
                k0 = 2 * m + p
                cos, sin = twist[0, k0 : k0 + 1, :], twist[1, k0 : k0 + 1, :]
                mix_ref[at(k0 * 16), 0:128] = real * cos + imag * sin
                mix_ref[at(k0 * 16), 128:256] = imag * cos - real * sin
        return carry

    lax.fori_loop(0, 2, rows, 0, unroll=2)
    high, low = split(mix_ref[...])
    nt = ((1,), (1,))
    out = dot(table[0], high, nt) + dot(table[1], high, nt) + dot(table[0], low, nt)
    to_messages(out, flat_ref, out_ref)


def to_messages(out, flat_ref, out_ref):
    for ri in range(2):
        for g in range(4):
            flat_ref[pl.ds(ri * 4 + g, 128, stride=8), :] = out[
                ri * 128 : (ri + 1) * 128, g * 128 : (g + 1) * 128
            ]
    out_ref[...] = flat_ref[...].reshape(128, 8, 128).astype(BF16)


def from_messages(recv, flat_ref, half_ref):
    flat_ref[...] = recv[...].astype(F32).reshape(1024, 128)
    for ri in range(2):
        for g in range(4):
            half_ref[ri * 128 : (ri + 1) * 128, g * 128 : (g + 1) * 128] = flat_ref[
                pl.ds(ri * 4 + g, 128, stride=8), :
            ].astype(BF16)


def column_stage(recv, flat_ref, half_ref, fwd, inv, small, small_inv, twist, green, wide_ref, out_ref):
    from_messages(recv, flat_ref, half_ref)
    block = half_ref[...]
    wide_ref[...] = dot(fwd[0], block) + dot(fwd[1], block)
    cos, sin = twist[0], twist[1]
    for g in range(4):
        lanes = slice(g * 128, (g + 1) * 128)
        real, imag = wide_ref[0:256, lanes], wide_ref[256:512, lanes]
        turned = jnp.concatenate([real * cos + imag * sin, imag * cos - real * sin], axis=1)
        high, low = split(turned)
        spec = dot(high, small[0]) + dot(low, small[0])
        scale = green[:, lanes]
        spec = spec * jnp.concatenate([scale, scale], axis=1)
        high, low = split(spec)
        back = dot(high, small_inv[0]) + dot(low, small_inv[0])
        real, imag = back[:, 0:128], back[:, 128:256]
        wide_ref[0:256, lanes] = real * cos - imag * sin
        wide_ref[256:512, lanes] = imag * cos + real * sin
    high, low = split(wide_ref[...])
    out = dot(inv[0], high) + dot(inv[0], low)
    to_messages(out, flat_ref, out_ref)


def row_inverse_stage(recv, flat_ref, half_ref, table, twist, mix_ref, slab_ref, send_ref):
    from_messages(recv, flat_ref, half_ref)
    turned = half_ref[...].T
    mix_ref[...] = dot(turned, table[0]) + dot(turned, table[1])

    def rows(h, carry):
        at = lambda start: pl.ds(pl.multiple_of(start + h * 8, 8), 8)
        items = []
        for k0 in range(32):
            cos, sin = twist[0, k0 : k0 + 1, :], twist[1, k0 : k0 + 1, :]
            real, imag = mix_ref[at(k0 * 16), 0:128], mix_ref[at(k0 * 16), 128:256]
            items.append((real * cos - imag * sin, imag * cos + real * sin))
        even = fft(items[0::2], 1)
        odd = fft(items[1::2], 1)
        for c in range(16):
            real, imag = cadd(even[c], cmulc(odd[c], 2 * math.pi * c / 32))
            slab_ref[c, at(0), :] = real
            slab_ref[c, at(16), :] = imag
        return carry

    lax.fori_loop(0, 2, rows, 0, unroll=2)
    lane = iota((16, 128), 1)
    for c in range(16):
        rim = jnp.zeros((16, 128), F32)
        if c < 15:
            rim = jnp.where(lane < 2, slab_ref[c + 1, 0:16, :], rim)
            rim = jnp.where((lane >= 2) & (lane < 4), pltpu.roll(slab_ref[c + 1, 16:32, :], 2, 1), rim)
        if c > 0:
            rim = jnp.where(lane >= 126, slab_ref[c - 1, 0:16, :], rim)
            rim = jnp.where(
                (lane >= 124) & (lane < 126), pltpu.roll(slab_ref[c - 1, 16:32, :], 126, 1), rim
            )
        send_ref[c] = jnp.concatenate([slab_ref[c, 0:32, :], rim], axis=0).astype(BF16)


def sample_stage(recv, pick, shifts, tall_ref, rows_ref, sample_ref):
    sub = iota((8, 128), 0)
    lane = iota((8, 128), 1)
    owns = [(lane // 16) == e for e in range(8)]
    for q in range(RHS):
        main = recv[:, q * 16 : (q + 1) * 16, :].reshape(288, 128)
        rim = recv[:, 32:48, :].reshape(288, 128)
        tall_ref[...] = dot(jnp.concatenate([main, rim], axis=1), pick[q])
        for g in range(4):
            lanes = slice(g * 128, (g + 1) * 128)
            dr = jnp.broadcast_to(shifts[0:1, lanes], (8, 128))
            dc = jnp.broadcast_to(shifts[1:2, lanes], (8, 128))

            def body(slot, carry):
                column = pl.ds(pl.multiple_of(slot * 128, 128), 128)
                tiles = [
                    tall_ref[8 + 64 * g + 8 * t : 16 + 64 * g + 8 * t, column] for t in range(10)
                ]
                home = tiles[1]
                edge = jnp.where(sub < 4, tiles[2], tiles[0])
                for e in range(1, 8):
                    home = jnp.where(owns[e], tiles[e + 1], home)
                    edge = jnp.where(owns[e], jnp.where(sub < 4, tiles[e + 2], tiles[e]), edge)
                moved = home
                for o in OFFSETS:
                    kept = (sub >= o) if o > 0 else (sub < 8 + o)
                    shifted = pltpu.roll(jnp.where(kept, home, edge), (-o) % 8, 0)
                    moved = jnp.where(dr == o, shifted, moved)
                rows_ref[slot] = moved
                return carry

            lax.fori_loop(0, 12, body, 0, unroll=12)
            line = lambda j: rows_ref[j] if 0 <= j < 8 else rows_ref[EDGE_SLOT[j % 8]]
            for j in range(8):
                moved = line(j)
                for o in OFFSETS:
                    moved = jnp.where(dc == o, line(j + o), moved)
                sample_ref[q, j, :, lanes] = moved


def far_stage(proj, sample_ref, near_ref, out_ref):
    for g in range(4):
        lanes = slice(g * 128, (g + 1) * 128)

        def body(j, sums):
            sums = list(sums)
            for i in range(8):
                weight = proj[i * 8 + j, :, lanes].astype(F32)
                for q in range(RHS):
                    line = sample_ref[q, j, i : i + 1, lanes]
                    sums[q] = sums[q] + weight * line
            return tuple(sums)

        sums = lax.fori_loop(0, 8, body, tuple(near_ref[q, :, lanes] for q in range(RHS)), unroll=2)
        for q in range(RHS):
            out_ref[q, :, lanes] = sums[q]


def turn_green(green, rows_ref, out_ref):
    for j1 in range(16):
        for h in range(2):
            rows_ref[h, pl.ds(j1, 32, stride=16), :] = green[
                :, j1 * 256 + h * 128 : j1 * 256 + (h + 1) * 128
            ]
    for h in range(2):
        for g in range(4):
            out_ref[h * 128 : (h + 1) * 128, g * 128 : (g + 1) * 128] = rows_ref[
                h, g * 128 : (g + 1) * 128, :
            ].T * (1.0 / 16777216)


def edge_stage(curf, edge_row, edge_col):
    lane = iota((16, 128), 1)
    place = lax.rem(lane, 16)

    def body(m, carry):
        q, at = m // 4, pl.ds(pl.multiple_of(lax.rem(m, 4) * 16, 16), 16)
        here = pl.ds(pl.multiple_of(m * 16, 16), 16)
        tiles = [curf[q, at, t * 128 : (t + 1) * 128] for t in range(4)]
        edge_row[here, :] = jnp.where(lane < 64, tiles[0], tiles[3]).astype(BF16)
        packed = jnp.zeros((16, 128), F32)
        for t in range(4):
            packed = jnp.where(place == t, pltpu.roll(tiles[t], (t - 15) % 128, 1), packed)
            packed = jnp.where(place == 4 + t, pltpu.roll(tiles[t], 4 + t, 1), packed)
        edge_col[here, :] = packed.astype(BF16)
        return carry

    lax.fori_loop(0, 8, body, 0)


def partner_stage(curf, partners, edges, picked):
    lane = iota((16, 128), 1)
    place = lax.rem(lane, 16)

    def body(m, carry):
        q, at = m // 4, pl.ds(pl.multiple_of(lax.rem(m, 4) * 16, 16), 16)
        here = pl.ds(pl.multiple_of(m * 16, 16), 16)
        near = lambda dr, dc: edges[edge_slot(dr, dc), here, :].astype(F32)
        middle = [near(-1, 0)]
        middle += [curf[q, at, t * 128 : (t + 1) * 128] for t in range(4)]
        middle += [near(1, 0)]
        left, right = near(0, -1), near(0, 1)
        from_right = [near(-1, 1), right, right, right, right, near(1, 1)]
        from_left = [near(-1, -1), left, left, left, left, near(1, -1)]
        columns = {0: middle, 1: [], -1: []}
        for e in range(6):
            inner = e in (1, 2, 3, 4)
            t = e - 1
            outside = pltpu.roll(from_right[e], (11 - t) % 128 if inner else 15, 1)
            columns[1].append(jnp.where(place == 15, outside, pltpu.roll(middle[e], 127, 1)))
            outside = pltpu.roll(from_left[e], (-t) % 128 if inner else 113, 1)
            columns[-1].append(jnp.where(place == 0, outside, pltpu.roll(middle[e], 1, 1)))
        for t in range(4):
            lanes = slice(t * 128, (t + 1) * 128)
            views = {}
            for dc in (-1, 0, 1):
                x = columns[dc]
                views[0, dc] = x[t + 1]
                views[1, dc] = pltpu.roll(jnp.where(lane < 16, x[t + 2], x[t + 1]), 112, 1)
                views[-1, dc] = pltpu.roll(jnp.where(lane >= 112, x[t], x[t + 1]), 16, 1)
            for k in range(1, NEIGH):
                code = jnp.broadcast_to(partners[k : k + 1, lanes], (16, 128))
                chosen = views[0, 0]
                for dr in (-1, 0, 1):
                    for dc in (-1, 0, 1):
                        if dr or dc:
                            chosen = jnp.where(code == 3 * (dr + 1) + dc + 1, views[dr, dc], chosen)
                picked[k - 1, q, at, lanes] = chosen
        return carry

    lax.fori_loop(0, 8, body, 0)


def near_stage(blocks, k, values, near_ref):
    def body(m, carry):
        a0 = pl.multiple_of((m // 4) * 8, 8)
        lanes = pl.ds(pl.multiple_of(lax.rem(m, 4) * 128, 128), 128)
        sums = [None] * 16
        for b in range(4):
            at = slice(16 * b, 16 * b + 16)
            current = [values[q, at, lanes] for q in range(RHS)]
            for a in range(8):
                weight = blocks[k, a0 + a, at, lanes].astype(F32)
                for q in range(RHS):
                    part = fold(weight * current[q])
                    old = sums[q * 8 + a]
                    sums[q * 8 + a] = part if old is None else old + part
        for q in range(RHS):
            tile = row_sums(sums[q * 8 : q * 8 + 8])
            if k > 0:
                tile = tile + near_ref[q, pl.ds(a0, 8), lanes]
            near_ref[q, pl.ds(a0, 8), lanes] = tile
        return carry

    lax.fori_loop(0, 32, body, 0)


AROUND = [(dr, dc) for dr in (-1, 0, 1) for dc in (-1, 0, 1) if dr or dc]


def edge_slot(dr, dc):
    return AROUND.index((dr, dc))


def hop_order():
    hop = lambda d: min(d, 4 - d)
    offsets = [
        (x, y, z, core) for x in range(4) for y in range(4) for z in range(4) for core in range(2)
    ][1:]
    return sorted(offsets, key=lambda o: -(hop(o[0]) + hop(o[1]) + hop(o[2])))


def slots_wait(ref, count, sem):
    part = ref.at[pl.ds(0, count)]
    pltpu.make_async_copy(part, part, sem).wait()


TABLES = 10


def main_kernel(*refs):
    cur_hbm, shifts_hbm, partners_hbm, proj_hbm, blocks_hbm, green_hbm = refs[:6]
    tables_hbm = refs[6 : 6 + TABLES]
    out_ref = refs[6 + TABLES]
    scratch = refs[7 + TABLES :]
    tables = scratch[:TABLES]
    place, pick, row_fwd, row_inv, col_fwd, col_inv, small, small_inv, twist_row, twist_col = tables
    (
        proj, blocks, green, rows_ref, left_ref, grid_ref, send1, recv1, halo1, slab_ref, mix_ref,
        flat_ref, send2, recv2, half_ref, wide_ref, green_rows, green_turned, send3, recv3, send4,
        recv4, tall_ref, pick_rows, sample_ref, curf, edge_row, edge_col, edges, picked, near_ref,
        cur, shifts, partners, ssem, rsem, hsem, lsem, esem_out, esem_in, psem, nsem, tsem, csem, entered,
    ) = scratch[TABLES:]
    r, c = lax.axis_index("row"), lax.axis_index("col")
    me = r * 16 + c
    core, y_low, z = c & 1, lax.shift_right_logical(c, 1) & 1, lax.shift_right_logical(c, 2)
    x, y = lax.shift_right_logical(r, 1), (r & 1) * 2 + y_low

    proj_copies = [
        pltpu.make_async_copy(
            proj_hbm.at[:, :, pl.ds(g * 128, 128)], proj.at[:, :, pl.ds(g * 128, 128)], psem.at[g]
        )
        for g in range(4)
    ]
    table_copies = [pltpu.make_async_copy(a, b, tsem.at[i]) for i, (a, b) in enumerate(zip(tables_hbm, tables))]
    green_copy = pltpu.make_async_copy(green_hbm, green, tsem.at[TABLES])
    block_copies = [pltpu.make_async_copy(blocks_hbm.at[k], blocks.at[k], nsem.at[k]) for k in range(NEIGH)]
    small_copies = [
        pltpu.make_async_copy(a, b, csem.at[i])
        for i, (a, b) in enumerate(((cur_hbm, cur), (shifts_hbm, shifts), (partners_hbm, partners)))
    ]
    for copy in small_copies + proj_copies:
        copy.start()
    table_copies[0].start()

    barrier = pltpu.get_barrier_semaphore()

    def greet_column(k, carry):
        pl.semaphore_signal(barrier, inc=1, device_id=(r, (c + k) & 15), device_id_type=MESH)
        return carry

    def greet_row(k, carry):
        pl.semaphore_signal(barrier, inc=1, device_id=((r + k) & 7, c), device_id_type=MESH)
        return carry

    def greet_next(k, carry):
        pl.semaphore_signal(barrier, inc=1, device_id=(r + 1, k), device_id_type=MESH)
        return carry

    def greet_last(k, carry):
        pl.semaphore_signal(barrier, inc=1, device_id=(r - 1, k), device_id_type=MESH)
        return carry

    @pl.when((c == 15) & (r < 7))
    def _():
        lax.fori_loop(0, 16, greet_next, 0)

    @pl.when((c == 0) & (r > 0))
    def _():
        lax.fori_loop(0, 16, greet_last, 0)

    lax.fori_loop(1, 8, greet_row, 0)
    lax.fori_loop(1, 16, greet_column, 0)
    zero = jnp.zeros((48, 128), BF16)
    recv4[0] = zero
    recv4[17] = zero
    for copy in small_copies:
        copy.wait()
    curf[...] = cur[...].astype(BF16).astype(F32)
    stencil_stage(proj, curf, shifts, rows_ref, lambda g: proj_copies[g].wait())
    for copy in table_copies[1:]:
        copy.start()
    green_copy.start()
    for copy in block_copies:
        copy.start()
    table_copies[0].wait()
    spread_stage(rows_ref, shifts, place, left_ref, grid_ref, send1)
    pl.semaphore_wait(barrier, 22 + jnp.where(r > 0, 1, 0) + jnp.where(r < 7, 1, 0))

    def tell_column(k, carry):
        pl.semaphore_signal(entered, inc=1, device_id=(r, (c + k) & 15), device_id_type=MESH)
        return carry


    def remote(source, target, send_sem, recv_sem, where):
        return pltpu.make_async_remote_copy(
            source, target, send_sem, recv_sem, device_id=where, device_id_type=MESH
        )

    def to_column(send, recv, slot, index):
        for dx, dy, dz, dcore in hop_order():
            if dx == 0 and dy < 2:
                d = ((z + dz) & 3) * 4 + (y_low ^ dy) * 2 + (core ^ dcore)
                remote(send.at[d], recv.at[slot], ssem.at[index], rsem.at[index], (r, d)).start()

    @pl.when(r > 0)
    def _():
        remote(send1.at[16], halo1.at[c], ssem.at[4], hsem.at[0], (r - 1, 15)).start()

    @pl.when(r < 7)
    def _():
        remote(send1.at[17], halo1.at[c], ssem.at[5], hsem.at[0], (r + 1, 0)).start()

    to_column(send1, recv1, c, 0)
    own = pltpu.make_async_copy(send1.at[c], recv1.at[c], lsem.at[0])
    own.start()
    lax.fori_loop(1, 16, tell_column, 0)
    edge_stage(curf, edge_row, edge_col)

    def exists(dr, dc):
        there = None
        for move, at, last in ((dr, r, 7), (dc, c, 15)):
            test = at < last if move > 0 else at > 0
            if move:
                there = test if there is None else there & test
        return there

    def edge_copy(dr, dc):
        target = edge_slot(-dr, -dc)
        return remote(
            edge_row if dr else edge_col, edges.at[target], esem_out.at[edge_slot(dr, dc)],
            esem_in.at[target], (r + dr, c + dc),
        )

    pl.semaphore_wait(entered, 15)
    for dr, dc in AROUND:
        @pl.when(exists(dr, dc))
        def _():
            edge_copy(dr, dc).start()

    block_copies[0].wait()
    near_stage(blocks, 0, curf, near_ref)
    for copy in table_copies[1:]:
        copy.wait()
    own.wait()
    has_halo = ((c == 0) & (r > 0)) | ((c == 15) & (r < 7))
    slots_wait(recv1, 15, rsem.at[0])

    @pl.when(has_halo)
    def _():
        slots_wait(halo1, 16, hsem.at[0])

    row_forward_stage(recv1, halo1, has_halo, slab_ref, twist_row, row_fwd, mix_ref, flat_ref, send2)

    def to_all(send, recv, index):
        own = pltpu.make_async_copy(send.at[me], recv.at[me], lsem.at[index])
        own.start()
        for dx, dy, dz, dcore in hop_order():
            px, py, pz, pcore = (x + dx) & 3, (y + dy) & 3, (z + dz) & 3, core ^ dcore
            row = px * 2 + lax.shift_right_logical(py, 1)
            col = pz * 4 + (py & 1) * 2 + pcore
            remote(send.at[row * 16 + col], recv.at[me], ssem.at[index], rsem.at[index], (row, col)).start()
        return own

    own = to_all(send2, recv2, 1)
    green_copy.wait()
    turn_green(green, green_rows, green_turned)
    for dr, dc in AROUND:
        @pl.when(exists(dr, dc))
        def _():
            back = edges.at[edge_slot(dr, dc)]
            pltpu.make_async_copy(back, back, esem_in.at[edge_slot(dr, dc)]).wait()

    partner_stage(curf, partners, edges, picked)
    block_copies[1].wait()
    near_stage(blocks, 1, picked.at[0], near_ref)
    own.wait()
    slots_wait(recv2, 127, rsem.at[1])
    column_stage(
        recv2, flat_ref, half_ref, col_fwd, col_inv, small, small_inv, twist_col, green_turned, wide_ref, send3
    )
    own = to_all(send3, recv3, 2)
    block_copies[2].wait()
    near_stage(blocks, 2, picked.at[1], near_ref)
    own.wait()
    slots_wait(recv3, 127, rsem.at[2])
    row_inverse_stage(recv3, flat_ref, half_ref, row_inv, twist_row, mix_ref, slab_ref, send4)

    def to_neighbour_row(target, slot, index, sem):
        def go(d, carry):
            remote(send4.at[d], recv4.at[slot], ssem.at[index], hsem.at[sem], (target, d)).start()
            return carry

        lax.fori_loop(0, 16, go, 0)

    up = (c == 0) & (r > 0)
    down = (c == 15) & (r < 7)

    @pl.when(up)
    def _():
        to_neighbour_row(r - 1, 17, 6, 1)

    @pl.when(down)
    def _():
        to_neighbour_row(r + 1, 0, 7, 2)

    to_column(send4, recv4, c + 1, 3)
    own = pltpu.make_async_copy(send4.at[c], recv4.at[c + 1], lsem.at[3])
    own.start()
    block_copies[3].wait()
    near_stage(blocks, 3, picked.at[2], near_ref)
    own.wait()
    slots_wait(recv4, 15, rsem.at[3])

    @pl.when(r < 7)
    def _():
        slots_wait(recv4, 1, hsem.at[1])

    @pl.when(r > 0)
    def _():
        slots_wait(recv4, 1, hsem.at[2])

    sample_stage(recv4, pick, shifts, tall_ref, pick_rows, sample_ref)
    far_stage(proj, sample_ref, near_ref, out_ref)

    slots_wait(send1, 15, ssem.at[0])

    @pl.when(r > 0)
    def _():
        slots_wait(send1, 1, ssem.at[4])

    @pl.when(r < 7)
    def _():
        slots_wait(send1, 1, ssem.at[5])

    for dr, dc in AROUND:
        @pl.when(exists(dr, dc))
        def _():
            pltpu.make_async_copy(edge_row, edge_row, esem_out.at[edge_slot(dr, dc)]).wait()

    slots_wait(send2, 127, ssem.at[1])
    slots_wait(send3, 127, ssem.at[2])
    slots_wait(send4, 15, ssem.at[3])

    @pl.when(up)
    def _():
        slots_wait(send4, 16, ssem.at[6])

    @pl.when(down)
    def _():
        slots_wait(send4, 16, ssem.at[7])


def shards(currents, projection, near_blocks, partners, shifts, green):
    tables = [jnp.asarray(t) for t in make_tables()]
    vmem = pl.BlockSpec(memory_space=pltpu.VMEM)
    hbm = pl.BlockSpec(memory_space=pltpu.HBM)
    dma = pltpu.SemaphoreType.DMA
    return pl.pallas_call(
        main_kernel,
        out_shape=pltpu.VMEM((RHS, BASIS, ER * EC), F32),
        in_specs=[hbm] * (6 + len(tables)),
        out_specs=vmem,
        scratch_shapes=[pltpu.VMEM(t.shape, t.dtype) for t in tables]
        + [
            pltpu.VMEM((64, BASIS, 512), BF16),
            pltpu.VMEM((NEIGH, BASIS, BASIS, 512), BF16),
            pltpu.VMEM((32, 4096), F32),
            pltpu.VMEM((RHS, 2, 8, 8, 512), F32),
            pltpu.VMEM((256, 1536), BF16),
            pltpu.VMEM((RHS, 2, 272, 256), F32),
            pltpu.VMEM((18, 48, 128), BF16),
            pltpu.VMEM((16, 48, 128), BF16),
            pltpu.VMEM((16, 48, 128), BF16),
            pltpu.VMEM((16, 48, 128), F32),
            pltpu.VMEM((512, 256), F32),
            pltpu.VMEM((1024, 128), F32),
            pltpu.VMEM((128, 8, 128), BF16),
            pltpu.VMEM((128, 8, 128), BF16),
            pltpu.VMEM((256, 512), BF16),
            pltpu.VMEM((512, 512), F32),
            pltpu.VMEM((2, 512, 128), F32),
            pltpu.VMEM((256, 512), F32),
            pltpu.VMEM((128, 8, 128), BF16),
            pltpu.VMEM((128, 8, 128), BF16),
            pltpu.VMEM((16, 48, 128), BF16),
            pltpu.VMEM((18, 48, 128), BF16),
            pltpu.VMEM((288, 1536), F32),
            pltpu.VMEM((12, 8, 128), F32),
            pltpu.VMEM((RHS, 8, 8, 512), F32),
            pltpu.VMEM((RHS, BASIS, 512), F32),
            pltpu.VMEM((128, 128), BF16),
            pltpu.VMEM((128, 128), BF16),
            pltpu.VMEM((8, 128, 128), BF16),
            pltpu.VMEM((NEIGH - 1, RHS, BASIS, 512), F32),
            pltpu.VMEM((RHS, BASIS, 512), F32),
            pltpu.VMEM((RHS, BASIS, 512), F32),
            pltpu.VMEM((2, 512), jnp.int32),
            pltpu.VMEM((NEIGH, 512), jnp.int32),
            dma((8,)),
            dma((4,)),
            dma((3,)),
            dma((4,)),
            dma((8,)),
            dma((8,)),
            dma((4,)),
            dma((NEIGH,)),
            dma((len(tables) + 1,)),
            dma((3,)),
            pltpu.SemaphoreType.REGULAR,
        ],
        compiler_params=pltpu.CompilerParams(
            collective_id=0, has_side_effects=True, vmem_limit_bytes=int(60 * 2**20)
        ),
    )(currents, shifts, partners, projection, near_blocks, green, *tables)


def solution(mesh):
    in_specs = (
        P(None, None, ("row", "col")),
        P(None, None, ("row", "col")),
        P(None, None, None, ("row", "col")),
        P(None, ("row", "col")),
        P(None, ("row", "col")),
        P(("row", "col"), None),
    )
    out_specs = P(None, None, ("row", "col"))
    return jax.shard_map(shards, mesh=mesh, in_specs=in_specs, out_specs=out_specs, check_vma=False)
```

```python
import functools
import math

import jax
import jax.numpy as jnp
import ml_dtypes
import numpy as np
from jax import lax
from jax.experimental import pallas as pl
from jax.experimental.pallas import tpu as pltpu
from jax.sharding import PartitionSpec as P

MESH = pl.DeviceIdType.MESH
F32 = jnp.float32
BF16 = jnp.bfloat16
BASIS = 64
ER = 32
EC = 16
NEIGH = 4
RHS = 2
OFFSETS = (-2, -1, 1, 2)
EDGE_SLOT = {0: 8, 1: 9, 6: 10, 7: 11}


def halves(table):
    high = np.asarray(table, np.float64).astype(ml_dtypes.bfloat16)
    low = (table - high.astype(np.float64)).astype(ml_dtypes.bfloat16)
    return np.stack([high, low])


def make_tables():
    turn = lambda rows, cols, modulus: (
        2.0 * np.pi * ((np.arange(rows)[:, None] * np.arange(cols)[None, :]) % modulus) / modulus
    )
    place = np.zeros((12, 8, 16, 256))
    for ec in range(16):
        for j in range(8):
            place[j, :, ec, 8 * ec + j] = 1
        for j in (0, 1):
            if ec < 15:
                place[EDGE_SLOT[j], :, ec, 8 * (ec + 1) + j] = 1
            else:
                place[EDGE_SLOT[j], :, ec, 128 + j] = 1
                place[EDGE_SLOT[j], :, ec, 128 + 2 + j] = 1
        for j in (6, 7):
            if ec > 0:
                place[EDGE_SLOT[j], :, ec, 8 * (ec - 1) + j] = 1
            else:
                place[EDGE_SLOT[j], :, ec, 128 + 120 + j] = 1
                place[EDGE_SLOT[j], :, ec, 128 + 118 + j] = 1
    place = place.reshape(1536, 256)
    pick = np.stack([place.T, place.T])
    real_lanes = [128 + 0, 128 + 1, 128 + 126, 128 + 127]
    imag_lanes = [128 + 2, 128 + 3, 128 + 124, 128 + 125]
    pick[0, imag_lanes] = 0
    pick[1, real_lanes] = 0
    a = turn(128, 128, 128)
    row_fwd = np.block([[np.cos(a), np.sin(a)], [-np.sin(a), np.cos(a)]])
    row_inv = np.block([[np.cos(a), np.sin(a)], [-np.sin(a), np.cos(a)]])
    b = turn(256, 128, 256)
    col_fwd = np.block([[np.cos(b), np.sin(b)], [-np.sin(b), np.cos(b)]])
    col_inv = col_fwd.T
    c = turn(16, 16, 16)
    eye = np.eye(8)
    kc, ks = np.kron(eye, np.cos(c)), np.kron(eye, np.sin(c))
    small_fwd = np.block([[kc, -ks], [ks, kc]])
    small_inv = small_fwd.T
    t1 = turn(32, 128, 4096)
    twist_row = np.stack([np.cos(t1), np.sin(t1)])
    t2 = np.tile(turn(256, 16, 4096), (1, 8))
    twist_col = np.stack([np.cos(t2), np.sin(t2)])
    half = ml_dtypes.bfloat16
    return (
        place.astype(half),
        pick.astype(half),
        halves(row_fwd),
        halves(row_inv),
        halves(col_fwd),
        halves(col_inv),
        halves(small_fwd),
        halves(small_inv),
        twist_row.astype(np.float32),
        twist_col.astype(np.float32),
    )


def dot(a, b, dims=((1,), (0,))):
    return lax.dot_general(a, b, (dims, ((), ())), preferred_element_type=F32)


def split(x):
    high = x.astype(BF16)
    return high, (x - high.astype(F32)).astype(BF16)


def cadd(a, b):
    return (a[0] + b[0], a[1] + b[1])


def csub(a, b):
    return (a[0] - b[0], a[1] - b[1])


def cmulc(a, angle):
    turns = angle / (2 * math.pi)
    quarter = round(turns * 4)
    if abs(turns * 4 - quarter) < 1e-9:
        quarter %= 4
        if quarter == 0:
            return a
        if quarter == 1:
            return (-a[1], a[0])
        if quarter == 2:
            return (-a[0], -a[1])
        return (a[1], -a[0])
    c, s = math.cos(angle), math.sin(angle)
    return (a[0] * c - a[1] * s, a[0] * s + a[1] * c)


def fft(items, sign):
    n = len(items)
    if n == 1:
        return items
    even = fft(items[0::2], sign)
    odd = fft(items[1::2], sign)
    out = [None] * n
    for k in range(n // 2):
        t = cmulc(odd[k], sign * 2 * math.pi * k / n)
        out[k] = cadd(even[k], t)
        out[k + n // 2] = csub(even[k], t)
    return out


def iota(shape, dim):
    return lax.broadcasted_iota(jnp.int32, shape, dim)


def row_sums(tiles):
    sub = iota((8, 128), 0)
    top = sub < 4
    tiles = [
        jnp.where(top, tiles[i], tiles[i + 4])
        + pltpu.roll(jnp.where(top, tiles[i + 4], tiles[i]), 4, 0)
        for i in range(4)
    ]
    for step in (2, 1):
        upper = lax.rem(sub, 2 * step) < step
        tiles = [
            jnp.where(
                upper,
                tiles[i] + pltpu.roll(tiles[i], 8 - step, 0),
                tiles[i + step] + pltpu.roll(tiles[i + step], step, 0),
            )
            for i in range(step)
        ]
    return tiles[0]


def fold(x):
    total = x[0:8]
    for b in range(1, x.shape[0] // 8):
        total = total + x[8 * b : 8 * b + 8]
    return total


def stencil_stage(proj, curf, shifts, rows_ref, ready):
    sub = iota((8, 128), 0)
    for g in range(4):
        lanes = slice(g * 128, (g + 1) * 128)
        dr = jnp.broadcast_to(shifts[0:1, lanes], (8, 128))
        home = (sub - dr >= 0) & (sub - dr < 8)
        cur = [curf[q, :, lanes] for q in range(RHS)]

        ready(g)

        def body(j, carry):
            parts = [[] for _ in range(RHS)]
            for i in range(8):
                weight = proj[i * 8 + j, :, lanes].astype(F32)
                for q in range(RHS):
                    parts[q].append(fold(weight * cur[q]))
            tiles = [row_sums(part) for part in parts]
            for q in range(RHS):
                moved = tiles[q]
                for o in OFFSETS:
                    moved = jnp.where(dr == o, pltpu.roll(tiles[q], o % 8, 0), moved)
                rows_ref[q, 0, j, :, lanes] = jnp.where(home, moved, 0.0)
                rows_ref[q, 1, j, :, lanes] = jnp.where(home, 0.0, moved)
            return carry

        lax.fori_loop(0, 8, body, 0, unroll=4)


def spread_stage(rows_ref, shifts, place, left_ref, grid_ref, send_ref):
    sub = iota((64, 128), 0)
    lane = iota((64, 128), 1)
    own = jnp.where((sub // 8) == (lane // 16), 1.0, 0.0).astype(BF16)
    for g in range(4):
        lanes = slice(g * 128, (g + 1) * 128)
        dc = jnp.broadcast_to(shifts[1:2, lanes], (8, 128))
        is_offset = {o: dc == o for o in OFFSETS}

        def body(idx, carry):
            q, kind = idx // 2, lax.rem(idx, 2)
            tiles = [rows_ref[q, kind, j, :, lanes] for j in range(8)]
            for j in range(8):
                moved = tiles[j]
                for o in OFFSETS:
                    moved = jnp.where(is_offset[o], tiles[(j - o) % 8], moved)
                home = (j - dc >= 0) & (j - dc < 8)
                pieces = [(j, jnp.where(home, moved, 0.0))]
                if j in EDGE_SLOT:
                    pieces.append((EDGE_SLOT[j], jnp.where(home, 0.0, moved)))
                for slot, piece in pieces:
                    pair = jnp.concatenate([piece] * 2, axis=0).astype(BF16)
                    left_ref[pl.ds(pl.multiple_of(idx * 64, 64), 64), slot * 128 : (slot + 1) * 128] = (
                        jnp.concatenate([pair] * 4, axis=0) * own
                    )
            return carry

        lax.fori_loop(0, 4, body, 0, unroll=4)
        product = dot(left_ref[...], place[...])
        for q in range(RHS):
            for kind in range(2):
                base = (q * 2 + kind) * 64
                grid_ref[q, kind, 8 + g * 64 : 8 + (g + 1) * 64, :] = product[base : base + 64]
    zero8 = jnp.zeros((8, 256), F32)
    for q in range(RHS):
        grid_ref[q, 1, 0:8, :] = zero8
        grid_ref[q, 1, 264:272, :] = zero8
    sub = lax.rem(iota((16, 256), 0), 8)
    lane1 = iota((16, 128), 1)
    real_rim = (lane1 < 2) | (lane1 >= 126)
    imag_rim = ((lane1 >= 2) & (lane1 < 4)) | ((lane1 >= 124) & (lane1 < 126))

    def message(parts):
        rim = jnp.where(real_rim, parts[0][:, 128:], jnp.where(imag_rim, parts[1][:, 128:], 0.0))
        return jnp.concatenate([parts[0][:, :128], parts[1][:, :128], rim], axis=0).astype(BF16)

    def slab(k, carry):
        parts = []
        for q in range(RHS):
            at = lambda shift: pl.ds(pl.multiple_of(k * 16 + shift, 8), 16)
            total = grid_ref[q, 0, at(8), :]
            total = total + jnp.where(sub >= 6, grid_ref[q, 1, at(16), :], 0.0)
            total = total + jnp.where(sub < 2, grid_ref[q, 1, at(0), :], 0.0)
            parts.append(total)
        send_ref[k] = message(parts)
        return carry

    lax.fori_loop(0, 16, slab, 0, unroll=4)
    full = iota((16, 256), 0)
    send_ref[16] = message(
        [jnp.where(full >= 14, grid_ref[q, 1, 0:16, :], 0.0) for q in range(RHS)]
    )
    send_ref[17] = message(
        [jnp.where(full < 2, grid_ref[q, 1, 256:272, :], 0.0) for q in range(RHS)]
    )


def row_forward_stage(recv, halo, has_halo, slab_ref, twist, table, mix_ref, flat_ref, out_ref):
    def widen(c, carry):
        slab_ref[c] = recv[c].astype(F32)
        return carry

    lax.fori_loop(0, 16, widen, 0, unroll=4)

    @pl.when(has_halo)
    def _():
        def add(c, carry):
            slab_ref[c] = slab_ref[c] + halo[c].astype(F32)
            return carry

        lax.fori_loop(0, 16, add, 0)

    lane = iota((8, 128), 1)

    def rows(h, carry):
        at = lambda start: pl.ds(pl.multiple_of(start + h * 8, 8), 8)
        rims = [slab_ref[c, at(32), :] for c in range(16)]
        items = []
        for c in range(16):
            real = slab_ref[c, at(0), :]
            imag = slab_ref[c, at(16), :]
            if c > 0:
                real = real + jnp.where(lane < 2, rims[c - 1], 0.0)
                imag = imag + jnp.where(lane < 2, pltpu.roll(rims[c - 1], 126, 1), 0.0)
            if c < 15:
                real = real + jnp.where(lane >= 126, rims[c + 1], 0.0)
                imag = imag + jnp.where(lane >= 126, pltpu.roll(rims[c + 1], 2, 1), 0.0)
            items.append((real, imag))
        even = fft(items, -1)
        odd = fft([cmulc(v, -2 * math.pi * c / 32) for c, v in enumerate(items)], -1)
        for m in range(16):
            for p, (real, imag) in enumerate((even[m], odd[m])):
                k0 = 2 * m + p
                cos, sin = twist[0, k0 : k0 + 1, :], twist[1, k0 : k0 + 1, :]
                mix_ref[at(k0 * 16), 0:128] = real * cos + imag * sin
                mix_ref[at(k0 * 16), 128:256] = imag * cos - real * sin
        return carry

    lax.fori_loop(0, 2, rows, 0, unroll=2)
    high, low = split(mix_ref[...])
    nt = ((1,), (1,))
    out = dot(table[0], high, nt) + dot(table[1], high, nt) + dot(table[0], low, nt)
    to_messages(out, flat_ref, out_ref)


def to_messages(out, flat_ref, out_ref):
    for ri in range(2):
        for g in range(4):
            flat_ref[pl.ds(ri * 4 + g, 128, stride=8), :] = out[
                ri * 128 : (ri + 1) * 128, g * 128 : (g + 1) * 128
            ]
    out_ref[...] = flat_ref[...].reshape(128, 8, 128).astype(BF16)


def from_messages(recv, flat_ref, half_ref):
    flat_ref[...] = recv[...].astype(F32).reshape(1024, 128)
    for ri in range(2):
        for g in range(4):
            half_ref[ri * 128 : (ri + 1) * 128, g * 128 : (g + 1) * 128] = flat_ref[
                pl.ds(ri * 4 + g, 128, stride=8), :
            ].astype(BF16)


def column_stage(recv, flat_ref, half_ref, fwd, inv, small, small_inv, twist, green, wide_ref, out_ref):
    from_messages(recv, flat_ref, half_ref)
    block = half_ref[...]
    wide_ref[...] = dot(fwd[0], block) + dot(fwd[1], block)
    cos, sin = twist[0], twist[1]
    for g in range(4):
        lanes = slice(g * 128, (g + 1) * 128)
        real, imag = wide_ref[0:256, lanes], wide_ref[256:512, lanes]
        turned = jnp.concatenate([real * cos + imag * sin, imag * cos - real * sin], axis=1)
        high, low = split(turned)
        spec = dot(high, small[0]) + dot(low, small[0])
        scale = green[:, lanes]
        spec = spec * jnp.concatenate([scale, scale], axis=1)
        high, low = split(spec)
        back = dot(high, small_inv[0]) + dot(low, small_inv[0])
        real, imag = back[:, 0:128], back[:, 128:256]
        wide_ref[0:256, lanes] = real * cos - imag * sin
        wide_ref[256:512, lanes] = imag * cos + real * sin
    high, low = split(wide_ref[...])
    out = dot(inv[0], high) + dot(inv[0], low)
    to_messages(out, flat_ref, out_ref)


def row_inverse_stage(recv, flat_ref, half_ref, table, twist, mix_ref, slab_ref, send_ref):
    from_messages(recv, flat_ref, half_ref)
    turned = half_ref[...].T
    mix_ref[...] = dot(turned, table[0]) + dot(turned, table[1])

    def rows(h, carry):
        at = lambda start: pl.ds(pl.multiple_of(start + h * 8, 8), 8)
        items = []
        for k0 in range(32):
            cos, sin = twist[0, k0 : k0 + 1, :], twist[1, k0 : k0 + 1, :]
            real, imag = mix_ref[at(k0 * 16), 0:128], mix_ref[at(k0 * 16), 128:256]
            items.append((real * cos - imag * sin, imag * cos + real * sin))
        even = fft(items[0::2], 1)
        odd = fft(items[1::2], 1)
        for c in range(16):
            real, imag = cadd(even[c], cmulc(odd[c], 2 * math.pi * c / 32))
            slab_ref[c, at(0), :] = real
            slab_ref[c, at(16), :] = imag
        return carry

    lax.fori_loop(0, 2, rows, 0, unroll=2)
    lane = iota((16, 128), 1)
    for c in range(16):
        rim = jnp.zeros((16, 128), F32)
        if c < 15:
            rim = jnp.where(lane < 2, slab_ref[c + 1, 0:16, :], rim)
            rim = jnp.where((lane >= 2) & (lane < 4), pltpu.roll(slab_ref[c + 1, 16:32, :], 2, 1), rim)
        if c > 0:
            rim = jnp.where(lane >= 126, slab_ref[c - 1, 0:16, :], rim)
            rim = jnp.where(
                (lane >= 124) & (lane < 126), pltpu.roll(slab_ref[c - 1, 16:32, :], 126, 1), rim
            )
        send_ref[c] = jnp.concatenate([slab_ref[c, 0:32, :], rim], axis=0).astype(BF16)


def sample_stage(recv, pick, shifts, tall_ref, rows_ref, sample_ref):
    sub = iota((8, 128), 0)
    lane = iota((8, 128), 1)
    owns = [(lane // 16) == e for e in range(8)]
    for q in range(RHS):
        main = recv[:, q * 16 : (q + 1) * 16, :].reshape(288, 128)
        rim = recv[:, 32:48, :].reshape(288, 128)
        tall_ref[...] = dot(jnp.concatenate([main, rim], axis=1), pick[q])
        for g in range(4):
            lanes = slice(g * 128, (g + 1) * 128)
            dr = jnp.broadcast_to(shifts[0:1, lanes], (8, 128))
            dc = jnp.broadcast_to(shifts[1:2, lanes], (8, 128))

            def body(slot, carry):
                column = pl.ds(pl.multiple_of(slot * 128, 128), 128)
                tiles = [
                    tall_ref[8 + 64 * g + 8 * t : 16 + 64 * g + 8 * t, column] for t in range(10)
                ]
                home = tiles[1]
                edge = jnp.where(sub < 4, tiles[2], tiles[0])
                for e in range(1, 8):
                    home = jnp.where(owns[e], tiles[e + 1], home)
                    edge = jnp.where(owns[e], jnp.where(sub < 4, tiles[e + 2], tiles[e]), edge)
                moved = home
                for o in OFFSETS:
                    kept = (sub >= o) if o > 0 else (sub < 8 + o)
                    shifted = pltpu.roll(jnp.where(kept, home, edge), (-o) % 8, 0)
                    moved = jnp.where(dr == o, shifted, moved)
                rows_ref[slot] = moved
                return carry

            lax.fori_loop(0, 12, body, 0, unroll=12)
            line = lambda j: rows_ref[j] if 0 <= j < 8 else rows_ref[EDGE_SLOT[j % 8]]
            for j in range(8):
                moved = line(j)
                for o in OFFSETS:
                    moved = jnp.where(dc == o, line(j + o), moved)
                sample_ref[q, j, :, lanes] = moved


def far_stage(proj, sample_ref, near_ref, out_ref):
    for g in range(4):
        lanes = slice(g * 128, (g + 1) * 128)

        def body(j, sums):
            sums = list(sums)
            for i in range(8):
                weight = proj[i * 8 + j, :, lanes].astype(F32)
                for q in range(RHS):
                    line = sample_ref[q, j, i : i + 1, lanes]
                    sums[q] = sums[q] + weight * line
            return tuple(sums)

        sums = lax.fori_loop(0, 8, body, tuple(near_ref[q, :, lanes] for q in range(RHS)), unroll=4)
        for q in range(RHS):
            out_ref[q, :, lanes] = sums[q]


def turn_green(green, rows_ref, out_ref):
    for j1 in range(16):
        for h in range(2):
            rows_ref[h, pl.ds(j1, 32, stride=16), :] = green[
                :, j1 * 256 + h * 128 : j1 * 256 + (h + 1) * 128
            ]
    for h in range(2):
        for g in range(4):
            out_ref[h * 128 : (h + 1) * 128, g * 128 : (g + 1) * 128] = rows_ref[
                h, g * 128 : (g + 1) * 128, :
            ].T * (1.0 / 16777216)


def edge_stage(curf, edge_row, edge_col):
    lane = iota((16, 128), 1)
    place = lax.rem(lane, 16)

    def body(m, carry):
        q, at = m // 4, pl.ds(pl.multiple_of(lax.rem(m, 4) * 16, 16), 16)
        here = pl.ds(pl.multiple_of(m * 16, 16), 16)
        tiles = [curf[q, at, t * 128 : (t + 1) * 128] for t in range(4)]
        edge_row[here, :] = jnp.where(lane < 64, tiles[0], tiles[3]).astype(BF16)
        packed = jnp.zeros((16, 128), F32)
        for t in range(4):
            packed = jnp.where(place == t, pltpu.roll(tiles[t], (t - 15) % 128, 1), packed)
            packed = jnp.where(place == 4 + t, pltpu.roll(tiles[t], 4 + t, 1), packed)
        edge_col[here, :] = packed.astype(BF16)
        return carry

    lax.fori_loop(0, 8, body, 0)


def partner_stage(curf, partners, edges, picked):
    lane = iota((16, 128), 1)
    place = lax.rem(lane, 16)

    def body(m, carry):
        q, at = m // 4, pl.ds(pl.multiple_of(lax.rem(m, 4) * 16, 16), 16)
        here = pl.ds(pl.multiple_of(m * 16, 16), 16)
        near = lambda dr, dc: edges[edge_slot(dr, dc), here, :].astype(F32)
        middle = [near(-1, 0)]
        middle += [curf[q, at, t * 128 : (t + 1) * 128] for t in range(4)]
        middle += [near(1, 0)]
        left, right = near(0, -1), near(0, 1)
        from_right = [near(-1, 1), right, right, right, right, near(1, 1)]
        from_left = [near(-1, -1), left, left, left, left, near(1, -1)]
        columns = {0: middle, 1: [], -1: []}
        for e in range(6):
            inner = e in (1, 2, 3, 4)
            t = e - 1
            outside = pltpu.roll(from_right[e], (11 - t) % 128 if inner else 15, 1)
            columns[1].append(jnp.where(place == 15, outside, pltpu.roll(middle[e], 127, 1)))
            outside = pltpu.roll(from_left[e], (-t) % 128 if inner else 113, 1)
            columns[-1].append(jnp.where(place == 0, outside, pltpu.roll(middle[e], 1, 1)))
        for t in range(4):
            lanes = slice(t * 128, (t + 1) * 128)
            views = {}
            for dc in (-1, 0, 1):
                x = columns[dc]
                views[0, dc] = x[t + 1]
                views[1, dc] = pltpu.roll(jnp.where(lane < 16, x[t + 2], x[t + 1]), 112, 1)
                views[-1, dc] = pltpu.roll(jnp.where(lane >= 112, x[t], x[t + 1]), 16, 1)
            for k in range(1, NEIGH):
                code = jnp.broadcast_to(partners[k : k + 1, lanes], (16, 128))
                chosen = views[0, 0]
                for dr in (-1, 0, 1):
                    for dc in (-1, 0, 1):
                        if dr or dc:
                            chosen = jnp.where(code == 3 * (dr + 1) + dc + 1, views[dr, dc], chosen)
                picked[k - 1, q, at, lanes] = chosen
        return carry

    lax.fori_loop(0, 8, body, 0)


def near_stage(blocks, k, values, near_ref):
    def body(m, carry):
        a0 = pl.multiple_of((m // 4) * 8, 8)
        lanes = pl.ds(pl.multiple_of(lax.rem(m, 4) * 128, 128), 128)
        sums = [None] * 16
        for b in range(4):
            at = slice(16 * b, 16 * b + 16)
            current = [values[q, at, lanes] for q in range(RHS)]
            for a in range(8):
                weight = blocks[k, a0 + a, at, lanes].astype(F32)
                for q in range(RHS):
                    part = fold(weight * current[q])
                    old = sums[q * 8 + a]
                    sums[q * 8 + a] = part if old is None else old + part
        for q in range(RHS):
            tile = row_sums(sums[q * 8 : q * 8 + 8])
            if k > 0:
                tile = tile + near_ref[q, pl.ds(a0, 8), lanes]
            near_ref[q, pl.ds(a0, 8), lanes] = tile
        return carry

    lax.fori_loop(0, 32, body, 0)


AROUND = [(dr, dc) for dr in (-1, 0, 1) for dc in (-1, 0, 1) if dr or dc]


def edge_slot(dr, dc):
    return AROUND.index((dr, dc))


def hop_order():
    hop = lambda d: min(d, 4 - d)
    offsets = [
        (x, y, z, core) for x in range(4) for y in range(4) for z in range(4) for core in range(2)
    ][1:]
    return sorted(offsets, key=lambda o: -(hop(o[0]) + hop(o[1]) + hop(o[2])))


def slots_wait(ref, count, sem):
    part = ref.at[pl.ds(0, count)]
    pltpu.make_async_copy(part, part, sem).wait()


TABLES = 10


def main_kernel(*refs):
    cur_hbm, shifts_hbm, partners_hbm, proj_hbm, blocks_hbm, green_hbm = refs[:6]
    tables_hbm = refs[6 : 6 + TABLES]
    out_ref = refs[6 + TABLES]
    scratch = refs[7 + TABLES :]
    tables = scratch[:TABLES]
    place, pick, row_fwd, row_inv, col_fwd, col_inv, small, small_inv, twist_row, twist_col = tables
    (
        proj, blocks, green, rows_ref, left_ref, grid_ref, send1, recv1, halo1, slab_ref, mix_ref,
        flat_ref, send2, recv2, half_ref, wide_ref, green_rows, green_turned, send3, recv3, send4,
        recv4, tall_ref, pick_rows, sample_ref, curf, edge_row, edge_col, edges, picked, near_ref,
        cur, shifts, partners, ssem, rsem, hsem, lsem, esem_out, esem_in, psem, nsem, tsem, csem, entered,
    ) = scratch[TABLES:]
    r, c = lax.axis_index("row"), lax.axis_index("col")
    me = r * 16 + c
    core, y_low, z = c & 1, lax.shift_right_logical(c, 1) & 1, lax.shift_right_logical(c, 2)
    x, y = lax.shift_right_logical(r, 1), (r & 1) * 2 + y_low

    proj_copies = [
        pltpu.make_async_copy(
            proj_hbm.at[:, :, pl.ds(g * 128, 128)], proj.at[:, :, pl.ds(g * 128, 128)], psem.at[g]
        )
        for g in range(4)
    ]
    table_copies = [pltpu.make_async_copy(a, b, tsem.at[i]) for i, (a, b) in enumerate(zip(tables_hbm, tables))]
    green_copy = pltpu.make_async_copy(green_hbm, green, tsem.at[TABLES])
    block_copies = [pltpu.make_async_copy(blocks_hbm.at[k], blocks.at[k], nsem.at[k]) for k in range(NEIGH)]
    small_copies = [
        pltpu.make_async_copy(a, b, csem.at[i])
        for i, (a, b) in enumerate(((cur_hbm, cur), (shifts_hbm, shifts), (partners_hbm, partners)))
    ]
    for copy in small_copies + proj_copies:
        copy.start()
    table_copies[0].start()

    barrier = pltpu.get_barrier_semaphore()

    def greet_column(k, carry):
        pl.semaphore_signal(barrier, inc=1, device_id=(r, (c + k) & 15), device_id_type=MESH)
        return carry

    def greet_row(k, carry):
        pl.semaphore_signal(barrier, inc=1, device_id=((r + k) & 7, c), device_id_type=MESH)
        return carry

    def greet_next(k, carry):
        pl.semaphore_signal(barrier, inc=1, device_id=(r + 1, k), device_id_type=MESH)
        return carry

    def greet_last(k, carry):
        pl.semaphore_signal(barrier, inc=1, device_id=(r - 1, k), device_id_type=MESH)
        return carry

    @pl.when((c == 15) & (r < 7))
    def _():
        lax.fori_loop(0, 16, greet_next, 0)

    @pl.when((c == 0) & (r > 0))
    def _():
        lax.fori_loop(0, 16, greet_last, 0)

    lax.fori_loop(1, 8, greet_row, 0)
    lax.fori_loop(1, 16, greet_column, 0)
    zero = jnp.zeros((48, 128), BF16)
    recv4[0] = zero
    recv4[17] = zero
    for copy in small_copies:
        copy.wait()
    curf[...] = cur[...].astype(BF16).astype(F32)
    stencil_stage(proj, curf, shifts, rows_ref, lambda g: proj_copies[g].wait())
    for copy in table_copies[1:]:
        copy.start()
    green_copy.start()
    for copy in block_copies:
        copy.start()
    table_copies[0].wait()
    spread_stage(rows_ref, shifts, place, left_ref, grid_ref, send1)
    pl.semaphore_wait(barrier, 22 + jnp.where(r > 0, 1, 0) + jnp.where(r < 7, 1, 0))

    def tell_column(k, carry):
        pl.semaphore_signal(entered, inc=1, device_id=(r, (c + k) & 15), device_id_type=MESH)
        return carry


    def remote(source, target, send_sem, recv_sem, where):
        return pltpu.make_async_remote_copy(
            source, target, send_sem, recv_sem, device_id=where, device_id_type=MESH
        )

    def to_column(send, recv, slot, index):
        for dx, dy, dz, dcore in hop_order():
            if dx == 0 and dy < 2:
                d = ((z + dz) & 3) * 4 + (y_low ^ dy) * 2 + (core ^ dcore)
                remote(send.at[d], recv.at[slot], ssem.at[index], rsem.at[index], (r, d)).start()

    @pl.when(r > 0)
    def _():
        remote(send1.at[16], halo1.at[c], ssem.at[4], hsem.at[0], (r - 1, 15)).start()

    @pl.when(r < 7)
    def _():
        remote(send1.at[17], halo1.at[c], ssem.at[5], hsem.at[0], (r + 1, 0)).start()

    to_column(send1, recv1, c, 0)
    own = pltpu.make_async_copy(send1.at[c], recv1.at[c], lsem.at[0])
    own.start()
    lax.fori_loop(1, 16, tell_column, 0)
    edge_stage(curf, edge_row, edge_col)

    def exists(dr, dc):
        there = None
        for move, at, last in ((dr, r, 7), (dc, c, 15)):
            test = at < last if move > 0 else at > 0
            if move:
                there = test if there is None else there & test
        return there

    def edge_copy(dr, dc):
        target = edge_slot(-dr, -dc)
        return remote(
            edge_row if dr else edge_col, edges.at[target], esem_out.at[edge_slot(dr, dc)],
            esem_in.at[target], (r + dr, c + dc),
        )

    pl.semaphore_wait(entered, 15)
    for dr, dc in AROUND:
        @pl.when(exists(dr, dc))
        def _():
            edge_copy(dr, dc).start()

    block_copies[0].wait()
    near_stage(blocks, 0, curf, near_ref)
    for copy in table_copies[1:]:
        copy.wait()
    own.wait()
    has_halo = ((c == 0) & (r > 0)) | ((c == 15) & (r < 7))
    slots_wait(recv1, 15, rsem.at[0])

    @pl.when(has_halo)
    def _():
        slots_wait(halo1, 16, hsem.at[0])

    row_forward_stage(recv1, halo1, has_halo, slab_ref, twist_row, row_fwd, mix_ref, flat_ref, send2)

    def to_all(send, recv, index):
        own = pltpu.make_async_copy(send.at[me], recv.at[me], lsem.at[index])
        own.start()
        for dx, dy, dz, dcore in hop_order():
            px, py, pz, pcore = (x + dx) & 3, (y + dy) & 3, (z + dz) & 3, core ^ dcore
            row = px * 2 + lax.shift_right_logical(py, 1)
            col = pz * 4 + (py & 1) * 2 + pcore
            remote(send.at[row * 16 + col], recv.at[me], ssem.at[index], rsem.at[index], (row, col)).start()
        return own

    own = to_all(send2, recv2, 1)
    green_copy.wait()
    turn_green(green, green_rows, green_turned)
    for dr, dc in AROUND:
        @pl.when(exists(dr, dc))
        def _():
            back = edges.at[edge_slot(dr, dc)]
            pltpu.make_async_copy(back, back, esem_in.at[edge_slot(dr, dc)]).wait()

    partner_stage(curf, partners, edges, picked)
    block_copies[1].wait()
    near_stage(blocks, 1, picked.at[0], near_ref)
    own.wait()
    slots_wait(recv2, 127, rsem.at[1])
    column_stage(
        recv2, flat_ref, half_ref, col_fwd, col_inv, small, small_inv, twist_col, green_turned, wide_ref, send3
    )
    own = to_all(send3, recv3, 2)
    block_copies[2].wait()
    near_stage(blocks, 2, picked.at[1], near_ref)
    own.wait()
    slots_wait(recv3, 127, rsem.at[2])
    row_inverse_stage(recv3, flat_ref, half_ref, row_inv, twist_row, mix_ref, slab_ref, send4)

    def to_neighbour_row(target, slot, index, sem):
        def go(d, carry):
            remote(send4.at[d], recv4.at[slot], ssem.at[index], hsem.at[sem], (target, d)).start()
            return carry

        lax.fori_loop(0, 16, go, 0)

    up = (c == 0) & (r > 0)
    down = (c == 15) & (r < 7)

    @pl.when(up)
    def _():
        to_neighbour_row(r - 1, 17, 6, 1)

    @pl.when(down)
    def _():
        to_neighbour_row(r + 1, 0, 7, 2)

    to_column(send4, recv4, c + 1, 3)
    own = pltpu.make_async_copy(send4.at[c], recv4.at[c + 1], lsem.at[3])
    own.start()
    block_copies[3].wait()
    near_stage(blocks, 3, picked.at[2], near_ref)
    own.wait()
    slots_wait(recv4, 15, rsem.at[3])

    @pl.when(r < 7)
    def _():
        slots_wait(recv4, 1, hsem.at[1])

    @pl.when(r > 0)
    def _():
        slots_wait(recv4, 1, hsem.at[2])

    sample_stage(recv4, pick, shifts, tall_ref, pick_rows, sample_ref)
    far_stage(proj, sample_ref, near_ref, out_ref)

    slots_wait(send1, 15, ssem.at[0])

    @pl.when(r > 0)
    def _():
        slots_wait(send1, 1, ssem.at[4])

    @pl.when(r < 7)
    def _():
        slots_wait(send1, 1, ssem.at[5])

    for dr, dc in AROUND:
        @pl.when(exists(dr, dc))
        def _():
            pltpu.make_async_copy(edge_row, edge_row, esem_out.at[edge_slot(dr, dc)]).wait()

    slots_wait(send2, 127, ssem.at[1])
    slots_wait(send3, 127, ssem.at[2])
    slots_wait(send4, 15, ssem.at[3])

    @pl.when(up)
    def _():
        slots_wait(send4, 16, ssem.at[6])

    @pl.when(down)
    def _():
        slots_wait(send4, 16, ssem.at[7])


def shards(currents, projection, near_blocks, partners, shifts, green):
    tables = [jnp.asarray(t) for t in make_tables()]
    vmem = pl.BlockSpec(memory_space=pltpu.VMEM)
    hbm = pl.BlockSpec(memory_space=pltpu.HBM)
    dma = pltpu.SemaphoreType.DMA
    return pl.pallas_call(
        main_kernel,
        out_shape=pltpu.VMEM((RHS, BASIS, ER * EC), F32),
        in_specs=[hbm] * (6 + len(tables)),
        out_specs=vmem,
        scratch_shapes=[pltpu.VMEM(t.shape, t.dtype) for t in tables]
        + [
            pltpu.VMEM((64, BASIS, 512), BF16),
            pltpu.VMEM((NEIGH, BASIS, BASIS, 512), BF16),
            pltpu.VMEM((32, 4096), F32),
            pltpu.VMEM((RHS, 2, 8, 8, 512), F32),
            pltpu.VMEM((256, 1536), BF16),
            pltpu.VMEM((RHS, 2, 272, 256), F32),
            pltpu.VMEM((18, 48, 128), BF16),
            pltpu.VMEM((16, 48, 128), BF16),
            pltpu.VMEM((16, 48, 128), BF16),
            pltpu.VMEM((16, 48, 128), F32),
            pltpu.VMEM((512, 256), F32),
            pltpu.VMEM((1024, 128), F32),
            pltpu.VMEM((128, 8, 128), BF16),
            pltpu.VMEM((128, 8, 128), BF16),
            pltpu.VMEM((256, 512), BF16),
            pltpu.VMEM((512, 512), F32),
            pltpu.VMEM((2, 512, 128), F32),
            pltpu.VMEM((256, 512), F32),
            pltpu.VMEM((128, 8, 128), BF16),
            pltpu.VMEM((128, 8, 128), BF16),
            pltpu.VMEM((16, 48, 128), BF16),
            pltpu.VMEM((18, 48, 128), BF16),
            pltpu.VMEM((288, 1536), F32),
            pltpu.VMEM((12, 8, 128), F32),
            pltpu.VMEM((RHS, 8, 8, 512), F32),
            pltpu.VMEM((RHS, BASIS, 512), F32),
            pltpu.VMEM((128, 128), BF16),
            pltpu.VMEM((128, 128), BF16),
            pltpu.VMEM((8, 128, 128), BF16),
            pltpu.VMEM((NEIGH - 1, RHS, BASIS, 512), F32),
            pltpu.VMEM((RHS, BASIS, 512), F32),
            pltpu.VMEM((RHS, BASIS, 512), F32),
            pltpu.VMEM((2, 512), jnp.int32),
            pltpu.VMEM((NEIGH, 512), jnp.int32),
            dma((8,)),
            dma((4,)),
            dma((3,)),
            dma((4,)),
            dma((8,)),
            dma((8,)),
            dma((4,)),
            dma((NEIGH,)),
            dma((len(tables) + 1,)),
            dma((3,)),
            pltpu.SemaphoreType.REGULAR,
        ],
        compiler_params=pltpu.CompilerParams(
            collective_id=0, has_side_effects=True, vmem_limit_bytes=int(60 * 2**20)
        ),
    )(currents, shifts, partners, projection, near_blocks, green, *tables)


def solution(mesh):
    in_specs = (
        P(None, None, ("row", "col")),
        P(None, None, ("row", "col")),
        P(None, None, None, ("row", "col")),
        P(None, ("row", "col")),
        P(None, ("row", "col")),
        P(("row", "col"), None),
    )
    out_specs = P(None, None, ("row", "col"))
    return jax.shard_map(shards, mesh=mesh, in_specs=in_specs, out_specs=out_specs, check_vma=False)
```
